128 devices in a mesh: seq: 16 (over z_lo, y, core), rep: 8 (over z_hi, x).
Axes of the slice: x: 4, y: 4, z: 4 (z_hi: 2, z_lo: 2; z = z_hi * 2 + z_lo), core: 2. Of those that a mesh axis runs over, the one named last changes fastest.
Arguments:
- query_states: bfloat16 [8, 2048, 1024], P('rep', 'seq'), may hold values from -5 to 5
- key_states: bfloat16 [8, 2048, 1024], P('rep', 'seq'), may hold values from -5 to 5
- value_states: bfloat16 [8, 2048, 1024], P('rep', 'seq'), may hold values from -6 to 6
- grad_out: bfloat16 [8, 2048, 2048], P('rep', 'seq'), may hold values from -6 to 6
- doc_ids: int32 [8, 2048], P('rep', 'seq'), may hold values from 0 to 7, never falling along the last dimension, each value on 1 to 512 neighbouring positions
- out_weight: bfloat16 [1024, 2048], replicated, may hold values from -0.1875 to 0.1875
- owners: int32 [8], replicated, may hold values from 0 to 7, each once
- statistics: float32 [8, 2, 512, 512], P('rep', None, 'seq'), as said below
Outputs:
- query_grad: bfloat16 [8, 2048, 1024], P('rep', 'seq')
- key_grad: bfloat16 [8, 2048, 1024], P('rep', 'seq')
- value_grad: bfloat16 [8, 2048, 1024], P('rep', 'seq')
- new_statistics: float32 [8, 2, 512, 512], P('rep', None, 'seq')
- update: bfloat16 [8, 512, 512], P(None, 'seq')
The draws below stay inside these ranges and needn't reach their ends.
Inputs may be any that keep to these rules, and one draw needn't show every extreme that they name: `doc_ids`: never falls along a sequence. `owners`: each slot holds exactly one block. `statistics`: each matrix is symmetric with a positive diagonal that dominates its row.
All inputs are finite; a program needn't handle non-finite values.
Results may differ from the reference program's by a relative error of at most 0.023.
Values may be sent and summed in bfloat16 or wider, within the bound.
No kernel may reach another device: no remote copies, remote signals or barrier semaphores. Data moves between devices by JAX's collectives and lax.ppermute only.
A program may use at most 128 MiB of HBM per device.

```python
import math
import jax
import jax.numpy as jnp
import numpy as np
from jax import lax

D = 2048
HEADS = 8
HD = 128
HW = 1024
TOK_DEV = 128
TOKENS = 2048
BATCH = 8
WIN = 256
DOCS = 8
BLK = 512
NBLK = 8
N_SEQ = 16


def draw_query_states(key, part):
    own_key = jax.random.fold_in(key, 11)
    return jnp.clip(jax.random.normal(own_key, (BATCH, TOKENS, HW), jnp.float32), -5.0, 5.0).astype(jnp.bfloat16)


def draw_key_states(key, part):
    own_key = jax.random.fold_in(key, 12)
    return jnp.clip(jax.random.normal(own_key, (BATCH, TOKENS, HW), jnp.float32), -5.0, 5.0).astype(jnp.bfloat16)


def draw_statistics(key, part):
    key = jax.random.fold_in(key, 3)
    noise_key, gain_key = jax.random.split(key)
    noise_draw = jax.random.uniform(noise_key, (NBLK, 2, BLK, BLK), jnp.float32, -1.0, 1.0)
    symmetric = 0.5 * (noise_draw + jnp.swapaxes(noise_draw, 2, 3))
    diag_gain = jax.random.uniform(gain_key, (NBLK, 2, BLK), jnp.float32, 1.0, 1.6)
    identity = jnp.eye(BLK, dtype=jnp.float32)
    spread = 1.0 / (TOKENS * BATCH * TOK_DEV)
    return spread * (symmetric * (1.0 - identity) + identity * (BLK * diag_gain)[..., None])


def steps_of(stream_key, extent, shards, least, top_value):
    def one(axis_at, shards_of):
        draws = jax.random.uniform(jax.random.fold_in(jax.random.fold_in(stream_key, 6), axis_at), (shards_of,), jnp.float32, least / len(shards), top_value / len(shards))
        return jnp.repeat(jnp.exp(draws), extent[axis_at] // shards_of).reshape((-1,) + (1,) * (len(extent) - axis_at - 1))

    level = one(*shards[0])
    for cut in shards[1:]:
        level = level * one(*cut)
    return level


def profile(amount, total, limit, slope):
    loads = [(1 << 20) // math.isqrt(rank ** slope) + 1 for rank in range(2, amount + 1)]
    rest, given = total - limit - (amount - 1), [1] * (amount - 1)
    while rest > 0:
        movable = [i for i in range(amount - 1) if given[i] < limit]
        mass, budget = sum([loads[i] for i in movable]), rest
        for i in movable:
            extra = min(limit - given[i], max(1, budget * loads[i] // mass), rest)
            given[i] = given[i] + extra
            rest = rest - extra
    return np.array([limit] + given)


def ragged(key, amount, total, most, lean):
    if amount == 2:
        one = jax.random.randint(key, (), max(1, total - most), min(most, total - 1) + 1)
        return jnp.stack([one, total - one])
    tallies = jnp.asarray(profile(amount, total, most, lean), jnp.int32)
    twos = (amount - 1) // 2
    source_of, sink = tallies[1:1 + 2 * twos:2], tallies[2:2 + 2 * twos:2]
    room = jnp.minimum(source_of - 1, most - sink)
    passed = jax.random.randint(jax.random.fold_in(key, 1), (twos,), 0, 1 << 20) % (room + 1)
    tallies = tallies.at[1:1 + 2 * twos:2].set(source_of - passed).at[2:2 + 2 * twos:2].set(sink + passed)
    return tallies[jax.random.permutation(jax.random.fold_in(key, 2), amount)]


def noise(key, shape, scale, limit, cuts=(), kind=jnp.bfloat16):
    level = steps_of(key, shape, cuts, -0.22, 0.18) if cuts else 1.0
    values = jax.random.normal(key, shape, jnp.float32) * scale * level
    return jnp.minimum(jnp.maximum(values, -limit), limit).astype(kind)


def setup_inputs(seed: int = 0) -> dict:
    seeds = jax.random.split(jax.random.key(seed), 9)
    return {
        "query_states": draw_query_states(jax.random.fold_in(seeds[8], 71), 0),
        "key_states": draw_key_states(jax.random.fold_in(seeds[8], 71), 0),
        "value_states": noise(seeds[2], (BATCH, TOKENS, HW), 1.0, 6.0, ((0, 8), (1, 16))),
        "grad_out": noise(seeds[3], (BATCH, TOKENS, D), 1.0, 6.0, ((0, 8), (1, 16))),
        "doc_ids": jax.vmap(lambda own: jnp.searchsorted(jnp.cumsum(ragged(own, DOCS, TOKENS, TOKENS // 4, 1)), jnp.arange(TOKENS), side="right"))(jax.random.split(seeds[4], BATCH)).reshape((BATCH, TOKENS)).astype(jnp.int32),
        "out_weight": noise(seeds[5], (HW, D), HW ** -0.5, 0.1875),
        "owners": jax.random.permutation(seeds[6], NBLK).astype(jnp.int32),
        "statistics": draw_statistics(jax.random.fold_in(seeds[8], 71), 0),
    }


masked_score = -1e+30
decay_rate = 0.9
step_scale = 16.0

def head_major(rows_by_width):
    row_total = rows_by_width.shape[0]
    return rows_by_width.reshape(row_total, HEADS, HD).transpose(1, 0, 2)

def token_major(heads_first):
    row_total = heads_first.shape[1]
    return heads_first.transpose(1, 0, 2).reshape(row_total, HEADS * HD)

def contract_last(left_mat, right_mat):
    return lax.dot_general(left_mat, right_mat, (((1,), (1,)), ((), ())), preferred_element_type=jnp.float32)

def contract_first(left_mat, right_mat):
    return lax.dot_general(left_mat, right_mat, (((0,), (0,)), ((), ())), preferred_element_type=jnp.float32)

def highest(left_mat, right_mat):
    return jnp.dot(left_mat, right_mat, precision=lax.Precision.HIGHEST, preferred_element_type=jnp.float32)

def window_mask(query_pos, key_pos, query_doc, key_doc):
    causal = key_pos[None, :] <= query_pos[:, None]
    inside = key_pos[None, :] > query_pos[:, None] - WIN
    present = key_pos[None, :] >= 0
    same_doc = query_doc[:, None] == key_doc[None, :]
    return causal & inside & present & same_doc

def head_scores(query_head, key_head, visible):
    scores = contract_last(query_head, key_head) * HD ** (-0.5)
    return jnp.where(visible, scores, masked_score)

def forward_head(query_head, key_head, value_head, visible):
    scores = head_scores(query_head, key_head, visible)
    row_max = lax.optimization_barrier(jnp.max(scores, axis=1, keepdims=True))
    log_norm = row_max + jnp.log(lax.optimization_barrier(jnp.sum(jnp.exp(scores - row_max), axis=1, keepdims=True)))
    weights = jnp.where(visible, jnp.exp(scores - log_norm), 0.0).astype(jnp.bfloat16)
    attended = jnp.dot(weights, value_head, preferred_element_type=jnp.float32)
    return (attended, log_norm[:, 0])

def grad_scores_head(query_head, grad_head, key_head, value_head, norm_head, dot_head, visible):
    scores = head_scores(query_head, key_head, visible)
    weights = jnp.where(visible, jnp.exp(scores - norm_head[:, None]), 0.0)
    grad_weights = contract_last(grad_head, value_head)
    grad_scores = (weights * (grad_weights - dot_head[:, None])).astype(jnp.bfloat16)
    return (grad_scores, weights.astype(jnp.bfloat16))

def inverse_root(matrix):
    identity = jnp.eye(matrix.shape[0], dtype=jnp.float32)
    frobenius = jnp.sqrt(jnp.sum(matrix * matrix))
    scaled = matrix / frobenius
    factor = (5.0 * identity - scaled) * 0.25
    square = highest(factor, factor)
    moved_mat = highest(highest(square, square), scaled)
    second = (5.0 * identity - moved_mat) * 0.25
    return highest(factor, second) * frobenius ** (-0.25)

def sequence_grads(query_seq, key_seq, value_seq, grad_seq, doc_seq, out_weight):
    pad_rows = 2 * TOK_DEV
    key_pad = jnp.concatenate([jnp.zeros((pad_rows, HW), key_seq.dtype), key_seq], axis=0)
    value_pad = jnp.concatenate([jnp.zeros((pad_rows, HW), value_seq.dtype), value_seq], axis=0)
    doc_pad = jnp.concatenate([jnp.full((pad_rows,), -1, jnp.int32), doc_seq.astype(jnp.int32)], axis=0)
    grad_attended = contract_last(grad_seq, out_weight).astype(jnp.bfloat16)
    firsts = jnp.arange(N_SEQ, dtype=jnp.int32) * TOK_DEV
    offsets = jnp.arange(TOK_DEV, dtype=jnp.int32)
    key_offsets = jnp.arange(3 * TOK_DEV, dtype=jnp.int32)

    def pieces_at(first_row):
        query_rows = lax.dynamic_slice_in_dim(query_seq, first_row, TOK_DEV, 0)
        key_rows = lax.dynamic_slice_in_dim(key_pad, first_row, 3 * TOK_DEV, 0)
        value_rows = lax.dynamic_slice_in_dim(value_pad, first_row, 3 * TOK_DEV, 0)
        query_doc = lax.dynamic_slice_in_dim(doc_seq.astype(jnp.int32), first_row, TOK_DEV, 0)
        key_doc = lax.dynamic_slice_in_dim(doc_pad, first_row, 3 * TOK_DEV, 0)
        visible = window_mask(first_row + offsets, first_row - pad_rows + key_offsets, query_doc, key_doc)
        return (query_rows, key_rows, value_rows, visible)

    def forward_block(first_row):
        query_rows, key_rows, value_rows, visible = pieces_at(first_row)
        attended, log_norm = lax.map(lambda pieces: forward_head(pieces[0], pieces[1], pieces[2], visible), (head_major(query_rows), head_major(key_rows), head_major(value_rows)))
        return (token_major(attended).astype(jnp.bfloat16), log_norm)
    attended, log_norm = lax.map(forward_block, firsts)
    attended = attended.reshape(TOKENS, HW)
    norm_heads = log_norm.transpose(1, 0, 2).reshape(HEADS, TOKENS)
    grad_dot = lax.optimization_barrier(jnp.sum((grad_attended.astype(jnp.float32) * attended.astype(jnp.float32)).reshape(TOKENS, HEADS, HD), axis=2))
    dot_heads = grad_dot.T

    def backward_block(running, first_row):
        key_acc, value_acc = running
        query_rows, key_rows, value_rows, visible = pieces_at(first_row)
        grad_rows = lax.dynamic_slice_in_dim(grad_attended, first_row, TOK_DEV, 0)
        norm_rows = lax.dynamic_slice_in_dim(norm_heads, first_row, TOK_DEV, 1)
        dot_rows = lax.dynamic_slice_in_dim(dot_heads, first_row, TOK_DEV, 1)

        def per_head(pieces):
            query_head, grad_head, key_head, value_head, norm_head, dot_head = pieces
            grad_scores, weights_low = grad_scores_head(query_head, grad_head, key_head, value_head, norm_head, dot_head, visible)
            head_query = jnp.dot(grad_scores, key_head, preferred_element_type=jnp.float32) * HD ** (-0.5)
            head_key = contract_first(grad_scores, query_head) * HD ** (-0.5)
            head_value = contract_first(weights_low, grad_head)
            return (head_query, head_key, head_value)
        head_query, head_key, head_value = lax.map(per_head, (head_major(query_rows), head_major(grad_rows), head_major(key_rows), head_major(value_rows), norm_rows, dot_rows))
        key_acc = lax.dynamic_update_slice_in_dim(key_acc, lax.dynamic_slice_in_dim(key_acc, first_row, 3 * TOK_DEV, 0) + token_major(head_key), first_row, 0)
        value_acc = lax.dynamic_update_slice_in_dim(value_acc, lax.dynamic_slice_in_dim(value_acc, first_row, 3 * TOK_DEV, 0) + token_major(head_value), first_row, 0)
        return ((key_acc, value_acc), token_major(head_query))
    empty_acc = jnp.zeros((pad_rows + TOKENS, HW), jnp.float32)
    (key_acc, value_acc), query_grad = lax.scan(backward_block, (empty_acc, empty_acc), firsts)
    weight_term = contract_first(attended, grad_seq)
    return (query_grad.reshape(TOKENS, HW).astype(jnp.bfloat16), key_acc[pad_rows:].astype(jnp.bfloat16), value_acc[pad_rows:].astype(jnp.bfloat16), weight_term)

def precondition(pieces):
    grad_block, old_pair = pieces
    left_stat = decay_rate * old_pair[0] + highest(grad_block, grad_block.T)
    right_stat = decay_rate * old_pair[1] + highest(grad_block.T, grad_block)
    result = highest(highest(inverse_root(left_stat), grad_block), inverse_root(right_stat))
    return (jnp.stack([left_stat, right_stat]), result)

def reference(query_states, key_states, value_states, grad_out, doc_ids, out_weight, owners, statistics):

    def one_sequence(pieces):
        return sequence_grads(pieces[0], pieces[1], pieces[2], pieces[3], pieces[4], out_weight)
    query_grad, key_grad, value_grad, weight_terms = lax.map(one_sequence, (query_states, key_states, value_states, grad_out, doc_ids))
    weight_grad = lax.optimization_barrier(jnp.sum(weight_terms, axis=0)) / (TOKENS * BATCH)
    grad_blocks = weight_grad.reshape(HW // BLK, BLK, D // BLK, BLK).transpose(0, 2, 1, 3).reshape(NBLK, BLK, BLK)
    slot_grad = jnp.zeros_like(grad_blocks).at[owners].set(grad_blocks)
    new_statistics, slot_updates = lax.map(precondition, (slot_grad, statistics))
    update = (step_scale * slot_updates[owners]).astype(jnp.bfloat16)
    return (query_grad, key_grad, value_grad, new_statistics, update)
```

```python
import functools

import jax
import jax.numpy as jnp
from jax import lax
from jax.experimental import pallas as pl
from jax.experimental.pallas import tpu as pltpu
from jax.sharding import Mesh, PartitionSpec as P

D = 2048
HD = 128
HW = 1024
TOK = 128
BLK = 512
NBLK = 8
HALF = HW // 2
PAIR = 2 * TOK
QTR = 256
KVW = 2 * HALF + TOK

SEQ = ("zl", "y", "c")
REP = ("zh", "x")
OUTER = ("zl", "zh", "x")
N_SEQ = 16
N_OUTER = 16
ROWS = BLK // N_SEQ
PART = 128

masked_score = -1e30
decay_rate = 0.9
step_scale = 16.0
head_scale = HD ** (-0.5)
weight_scale = 1.0 / 16384.0

f32 = jnp.float32
bf16 = jnp.bfloat16
VMEM_LIMIT = 48 * 1024 * 1024
WHOLE = pl.BlockSpec(memory_space=pltpu.VMEM)
SCALARS = pl.BlockSpec(memory_space=pltpu.SMEM)


def nt(left, right):
    return lax.dot_general(left, right, (((1,), (1,)), ((), ())), preferred_element_type=f32)


def tn(left, right):
    return lax.dot_general(left, right, (((0,), (0,)), ((), ())), preferred_element_type=f32)


def nn(left, right):
    return lax.dot_general(left, right, (((1,), (0,)), ((), ())), preferred_element_type=f32)


def call(body, outs, args, scratch=(), flops=0, nbytes=0, name=None):
    specs = [SCALARS if a.dtype == jnp.int32 and a.ndim == 1 else WHOLE for a in args]
    return pl.pallas_call(
        body,
        out_shape=outs,
        in_specs=specs,
        out_specs=jax.tree.map(lambda _: WHOLE, outs),
        scratch_shapes=list(scratch),
        compiler_params=pltpu.CompilerParams(vmem_limit_bytes=VMEM_LIMIT),
        cost_estimate=pl.CostEstimate(flops=flops, bytes_accessed=nbytes, transcendentals=0),
        name=name,
    )(*args)


def shaped(shape, dtype):
    return jax.ShapeDtypeStruct(shape, dtype)


def pick(core, ref, half):
    first = ref[:, half * HALF : half * HALF + QTR]
    second = ref[:, half * HALF + QTR : (half + 1) * HALF]
    return jnp.where(core == 0, first, second)


def pack_kernel(at_ref, key_ref, value_ref, doc_ref, own_ref, other_ref):
    core = at_ref[0]
    docs = jnp.broadcast_to(doc_ref[...].astype(f32), (TOK, TOK)).T.astype(bf16)
    for out_ref, which in ((own_ref, core), (other_ref, 1 - core)):
        for half in range(2):
            out_ref[:, half * QTR : (half + 1) * QTR] = pick(which, key_ref, half)
            out_ref[:, HALF + half * QTR : HALF + (half + 1) * QTR] = pick(which, value_ref, half)
        out_ref[:, 2 * HALF :] = docs


def own_rows(core):
    return pl.ds(pl.multiple_of(core * TOK, TOK), TOK)


def grad_attended_kernel(
    at_ref, query_ref, query_other_ref, grad_ref, grad_other_ref, weight_ref,
    attended_grad_ref, query_all_ref, grad_all_ref,
):
    core = at_ref[0]
    mine, other = own_rows(core), own_rows(1 - core)
    for half in range(2):
        cols = slice(half * QTR, (half + 1) * QTR)
        query_all_ref[mine, cols] = pick(core, query_ref, half)
        query_all_ref[other, cols] = pick(core, query_other_ref, half)
    grad_all_ref[mine, :] = grad_ref[...]
    grad_all_ref[other, :] = grad_other_ref[...]
    grad_rows = grad_all_ref[...]
    for half in range(2):
        start = pl.multiple_of(half * HALF + core * QTR, QTR)
        weight_rows = weight_ref[pl.ds(start, QTR), :]
        attended_grad_ref[:, half * QTR : (half + 1) * QTR] = nt(grad_rows, weight_rows).astype(bf16)


def place_blocks(core, own_ref, other_ref, before_ref, crossed_ref, all_ref):
    for ref, place in (
        (before_ref, core), (crossed_ref, 1 - core), (own_ref, 2 + core), (other_ref, 3 - core)
    ):
        all_ref[pl.ds(pl.multiple_of(place * TOK, TOK), TOK), :] = ref[...]


def forward_kernel(
    at_ref, owner_ref, query_ref, grad_ref, own_ref, other_ref, before_ref, crossed_ref,
    terms_ref, weights_ref, all_ref, attended_ref,
):
    core, chip = at_ref[0], at_ref[1]
    place_blocks(core, own_ref, other_ref, before_ref, crossed_ref, all_ref)
    doc_cols = [all_ref[b * TOK : (b + 1) * TOK, 2 * HALF :].astype(f32) for b in range(4)]
    doc_row = jnp.concatenate([block.T for block in doc_cols], axis=1)
    query_at = lax.broadcasted_iota(jnp.int32, (TOK, 3 * TOK), 0)
    key_at = lax.broadcasted_iota(jnp.int32, (TOK, 3 * TOK), 1)
    window = (key_at <= query_at + PAIR) & (key_at > query_at)
    for part in range(2):
        same = jnp.concatenate([doc_cols[2 + part]] * 3, axis=1) == doc_row[:, part * TOK : (part + 3) * TOK]
        present = key_at + part * TOK >= jnp.where(chip > 0, 0, PAIR)
        visible = window & same & present
        rows = slice(part * TOK, (part + 1) * TOK)
        keys = slice(part * TOK, (part + 3) * TOK)
        for head in range(4):
            cols = slice(head * HD, (head + 1) * HD)
            value_cols = slice(HALF + head * HD, HALF + (head + 1) * HD)
            scores = nt(query_ref[rows, cols], all_ref[keys, cols]) * head_scale
            scores = jnp.where(visible, scores, masked_score)
            row_max = jnp.max(scores, axis=1, keepdims=True)
            grown = jnp.exp(scores - row_max)
            total = jnp.sum(grown, axis=1, keepdims=True)
            weights = (grown * (1.0 / total)).astype(bf16)
            weights_ref[head, part] = weights
            attended_ref[rows, cols] = nn(weights, all_ref[keys, value_cols]).astype(bf16)
    for i in range(2):
        turned = attended_ref[:, i * QTR : (i + 1) * QTR].astype(f32).T.astype(bf16)
        for j in range(4):
            slot = owner_ref[4 * i + j]
            term = (nn(turned, grad_ref[:, j * BLK : (j + 1) * BLK]) * weight_scale).astype(bf16)
            terms_ref[0, slot] = term[:PART]
            terms_ref[1, slot] = term[PART:]


def backward_kernel(
    at_ref, weights_ref, query_ref, grad_ref, own_ref, other_ref, before_ref, crossed_ref,
    query_out_ref, sent_ref, kept_ref, all_ref, sum_ref,
):
    core = at_ref[0]
    place_blocks(core, own_ref, other_ref, before_ref, crossed_ref, all_ref)
    sum_ref[...] = jnp.zeros_like(sum_ref)
    for part in range(2):
        rows = slice(part * TOK, (part + 1) * TOK)
        keys = slice(part * TOK, (part + 3) * TOK)
        for head in range(4):
            cols = slice(head * HD, (head + 1) * HD)
            value_cols = slice(HALF + head * HD, HALF + (head + 1) * HD)
            low = weights_ref[head, part]
            weights = low.astype(f32)
            grad_head = grad_ref[rows, cols]
            query_head = query_ref[rows, cols]
            grad_weights = nt(grad_head, all_ref[keys, value_cols])
            grad_dot = jnp.sum(weights * grad_weights, axis=1, keepdims=True)
            grad_scores = (weights * (grad_weights - grad_dot)).astype(bf16)
            query_out_ref[rows, cols] = (nn(grad_scores, all_ref[keys, cols]) * head_scale).astype(bf16)
            sum_ref[keys, cols] += tn(grad_scores, query_head) * head_scale
            sum_ref[keys, value_cols] += tn(low, grad_head)
    sent_ref[...] = sum_ref[:PAIR].astype(bf16)
    kept_ref[...] = sum_ref[PAIR:]


def gather_grads_kernel(at_ref, query_ref, kept_ref, back_ref, mine_ref, other_ref):
    core = at_ref[0]
    for out_ref, rows in ((mine_ref, own_rows(core)), (other_ref, own_rows(1 - core))):
        out_ref[:, :HALF] = query_ref[rows, :]
        out_ref[:, HALF:] = (kept_ref[rows, :] + back_ref[rows, :].astype(f32)).astype(bf16)


def whole_width_kernel(at_ref, mine_ref, other_ref, query_ref, key_ref, value_ref):
    core = at_ref[0]
    for n, out_ref in enumerate((query_ref, key_ref, value_ref)):
        for half in range(2):
            cols = slice(n * HALF + half * QTR, n * HALF + (half + 1) * QTR)
            mine, other = mine_ref[:, cols], other_ref[:, cols]
            out_ref[0, :, half * HALF : half * HALF + QTR] = jnp.where(core == 0, mine, other)
            out_ref[0, :, half * HALF + QTR : (half + 1) * HALF] = jnp.where(core == 0, other, mine)


def sum_parts_kernel(parts_ref, total_ref):
    total = parts_ref[0].astype(f32)
    for n in range(1, N_OUTER):
        total = total + parts_ref[n].astype(f32)
    total_ref[...] = total.astype(bf16)


def newton_kernel(
    at_ref, grad_ref, grad_zl_ref, grad_c_ref, grad_zl_c_ref, stats_ref, stat_rows_ref,
    new_rows_ref, update_ref, slot_ref, left_ref, right_ref,
):
    core, low, row_first = at_ref[0], at_ref[2], at_ref[3]
    for ref, c, zl in (
        (grad_ref, core, low), (grad_zl_ref, core, 1 - low),
        (grad_c_ref, 1 - core, low), (grad_zl_c_ref, 1 - core, 1 - low),
    ):
        slot_ref[pl.ds(pl.multiple_of((2 * c + zl) * PART, PART), PART), :] = ref[...]
    slot = slot_ref[...]
    own = pl.ds(pl.multiple_of(row_first, ROWS), ROWS)
    left_ref[...] = nt(slot, slot)
    right_ref[...] = tn(slot, slot)
    new_rows_ref[0, 0] = decay_rate * stat_rows_ref[0, 0] + left_ref[own, :]
    new_rows_ref[0, 1] = decay_rate * stat_rows_ref[0, 1] + right_ref[own, :]
    left = decay_rate * stats_ref[:, 0].reshape(BLK, BLK).astype(f32) + left_ref[...]
    right = decay_rate * stats_ref[:, 1].reshape(BLK, BLK).astype(f32) + right_ref[...]

    def scaled(stat):
        norm_square = jnp.sum(jnp.sum(stat * stat, axis=0, keepdims=True), axis=1, keepdims=True)
        matrix = stat * lax.rsqrt(norm_square)
        low_matrix = matrix.astype(bf16)
        step = (nn(low_matrix, low_matrix) - 10.0 * matrix).astype(bf16)
        return matrix, low_matrix, step, jnp.exp(-0.125 * jnp.log(norm_square))

    left_matrix, left_low, left_step, left_scale = scaled(left)
    right_matrix, right_low, right_step, right_scale = scaled(right)
    left_ref[...] = left_matrix
    identity_rows = jnp.where(
        lax.broadcasted_iota(jnp.int32, (ROWS, BLK), 0) + row_first
        == lax.broadcasted_iota(jnp.int32, (ROWS, BLK), 1),
        1.0,
        0.0,
    )

    def rooted(factor, low_matrix, step):
        square = (25.0 * factor + nn(factor.astype(bf16), step)) * 0.0625
        fourth = (25.0 * square + nn(square.astype(bf16), step)) * 0.0625
        return (5.0 * factor - nn(fourth.astype(bf16), low_matrix)) * 0.25

    left_factor = (5.0 * identity_rows - left_ref[own, :]) * 0.25
    left_rows = rooted(left_factor, left_low, left_step)
    moved = nn(left_rows.astype(bf16), slot)
    right_factor = (5.0 * moved - nn(moved.astype(bf16), right_low)) * 0.25
    update = rooted(right_factor, right_low, right_step) * (step_scale * left_scale * right_scale)
    update_low = update.astype(bf16)
    for n in range(NBLK):
        update_ref[n] = update_low


def order_kernel(owner_ref, slots_ref, blocks_ref):
    for block in range(NBLK):
        blocks_ref[block] = slots_ref[owner_ref[block]]


def swapped(block, axis, mask=1):
    n = lax.axis_size(axis)
    return lax.ppermute(block, axis, [(i, i ^ mask) for i in range(n)])


def local(query_states, key_states, value_states, grad_out, doc_ids, out_weight, owners, statistics):
    core, low, along = lax.axis_index("c"), lax.axis_index("zl"), lax.axis_index("y")
    chip = low * 4 + along
    at = jnp.stack([core, chip, low, (chip * 2 + core) * ROWS]).astype(jnp.int32)
    query, key, value, grad = query_states[0], key_states[0], value_states[0], grad_out[0]

    stats_all = lax.all_gather(statistics[0].astype(bf16), SEQ, axis=0, tiled=False)

    own, other = call(
        pack_kernel,
        (shaped((TOK, KVW), bf16), shaped((TOK, KVW), bf16)),
        (at, key, value, doc_ids),
        name="pack",
    )
    before = lax.ppermute(own, SEQ, [(i, i + 2) for i in range(N_SEQ - 2)])
    crossed = lax.ppermute(other, SEQ, [(i, (i ^ 1) + 2) for i in range(N_SEQ - 2)])
    partner = swapped(other, "c")
    query_partner = swapped(query, "c")
    grad_partner = swapped(grad, "c")

    attended_grad, query_all, grad_all = call(
        grad_attended_kernel,
        (shaped((PAIR, HALF), bf16), shaped((PAIR, HALF), bf16), shaped((PAIR, D), bf16)),
        (at, query, query_partner, grad, grad_partner, out_weight),
        flops=2 * PAIR * HALF * D,
        nbytes=8 * 2**20,
        name="grad_attended",
    )
    terms, weights = call(
        forward_kernel,
        (shaped((2, NBLK, PART, BLK), bf16), shaped((4, 2, TOK, 3 * TOK), bf16)),
        (at, owners, query_all, grad_all, own, partner, before, crossed),
        scratch=(pltpu.VMEM((2 * PAIR, KVW), bf16), pltpu.VMEM((PAIR, HALF), bf16)),
        flops=2 * PAIR * HALF * (D + 6 * TOK),
        nbytes=6 * 2**20,
        name="forward",
    )
    parts = lax.all_to_all(terms.reshape(N_OUTER, PART, BLK), OUTER, 0, 0, tiled=True)
    over_outer = call(
        sum_parts_kernel, shaped((PART, BLK), bf16), (parts,), nbytes=2 * 2**20, name="sum_outer"
    )
    weights, over_outer = lax.optimization_barrier((weights, over_outer))
    others = [swapped(over_outer, "y", n) for n in (1, 2, 3)]

    query_grad, sent, kept = call(
        backward_kernel,
        (shaped((PAIR, HALF), bf16), shaped((PAIR, HW), bf16), shaped((PAIR, HW), f32)),
        (at, weights, query_all, attended_grad, own, partner, before, crossed),
        scratch=(pltpu.VMEM((2 * PAIR, KVW), bf16), pltpu.VMEM((2 * PAIR, HW), f32)),
        flops=2 * PAIR * HALF * 4 * 3 * TOK,
        nbytes=6 * 2**20,
        name="backward",
    )

    slot_part = sum((p.astype(f32) for p in others), over_outer.astype(f32)).astype(bf16)
    slot_zl = swapped(slot_part, "zl")
    slot_c = swapped(slot_part, "c")
    slot_zl_c = swapped(slot_zl, "c")
    back = lax.ppermute(sent, SEQ, [(i + 2, i) for i in range(N_SEQ - 2)])

    new_statistics, update_rows = call(
        newton_kernel,
        (shaped((1, 2, ROWS, BLK), f32), shaped((NBLK, ROWS, BLK), bf16)),
        (at, slot_part, slot_zl, slot_c, slot_zl_c, stats_all, statistics),
        scratch=(
            pltpu.VMEM((BLK, BLK), bf16), pltpu.VMEM((BLK, BLK), f32), pltpu.VMEM((BLK, BLK), f32)
        ),
        flops=2 * BLK**3 * 5,
        nbytes=4 * 2**20,
        name="newton",
    )
    slots = lax.all_to_all(update_rows, REP, 0, 0, tiled=True)
    update = call(order_kernel, shaped((NBLK, ROWS, BLK), bf16), (owners, slots), name="order")

    mine, theirs = call(
        gather_grads_kernel,
        (shaped((TOK, 3 * HALF), bf16), shaped((TOK, 3 * HALF), bf16)),
        (at, query_grad, kept, back),
        name="gather_grads",
    )
    received = swapped(theirs, "c")
    query_out, key_out, value_out = call(
        whole_width_kernel,
        tuple(shaped((1, TOK, HW), bf16) for _ in range(3)),
        (at, mine, received),
        name="whole_width",
    )
    return query_out, key_out, value_out, new_statistics, update


def solution(mesh):
    split = Mesh(mesh.devices.reshape(2, 4, 2, 2, 4), ("zl", "y", "c", "zh", "x"))
    tokens = P(REP, SEQ, None)
    return jax.shard_map(
        local,
        mesh=split,
        in_specs=(
            tokens, tokens, tokens, tokens, P(REP, SEQ), P(), P(), P(REP, None, SEQ, None),
        ),
        out_specs=(tokens, tokens, tokens, P(REP, None, SEQ, None), P(None, SEQ, None)),
        check_vma=False,
    )
```

```python
import functools

import jax
import jax.numpy as jnp
from jax import lax
from jax.experimental import pallas as pl
from jax.experimental.pallas import tpu as pltpu
from jax.sharding import Mesh, PartitionSpec as P

D = 2048
HD = 128
HW = 1024
TOK = 128
BLK = 512
NBLK = 8
HALF = HW // 2
PAIR = 2 * TOK
QTR = 256
KVW = 2 * HALF + TOK

SEQ = ("zl", "y", "c")
REP = ("zh", "x")
OUTER = ("zl", "zh", "x")
N_SEQ = 16
N_OUTER = 16
ROWS = BLK // N_SEQ
PART = 128

masked_score = -1e30
decay_rate = 0.9
step_scale = 16.0
head_scale = HD ** (-0.5)
weight_scale = 1.0 / 16384.0

f32 = jnp.float32
bf16 = jnp.bfloat16
VMEM_LIMIT = 48 * 1024 * 1024
ANYWHERE = pl.BlockSpec(memory_space=pl.ANY)
SCALARS = pl.BlockSpec(memory_space=pltpu.SMEM)


def nt(left, right):
    return lax.dot_general(left, right, (((1,), (1,)), ((), ())), preferred_element_type=f32)


def tn(left, right):
    return lax.dot_general(left, right, (((0,), (0,)), ((), ())), preferred_element_type=f32)


def nn(left, right):
    return lax.dot_general(left, right, (((1,), (0,)), ((), ())), preferred_element_type=f32)


def whole(array):
    zeros = (0,) * len(array.shape)
    return pl.BlockSpec(tuple(array.shape), lambda i: zeros)


def call(body, outs, args, scratch=(), flops=0, nbytes=0, name=None):
    specs = [SCALARS if a.dtype == jnp.int32 and a.ndim == 1 else whole(a) for a in args]
    return pl.pallas_call(
        body,
        grid=(1,),
        out_shape=outs,
        in_specs=specs,
        out_specs=jax.tree.map(whole, outs),
        scratch_shapes=list(scratch),
        compiler_params=pltpu.CompilerParams(vmem_limit_bytes=VMEM_LIMIT),
        cost_estimate=pl.CostEstimate(flops=flops, bytes_accessed=nbytes, transcendentals=0),
        name=name,
    )(*args)


def shaped(shape, dtype):
    return jax.ShapeDtypeStruct(shape, dtype)


def pick(core, ref, half):
    first = ref[:, half * HALF : half * HALF + QTR]
    second = ref[:, half * HALF + QTR : (half + 1) * HALF]
    return jnp.where(core == 0, first, second)


def pack_kernel(at_ref, key_ref, value_ref, doc_ref, own_ref, other_ref):
    core = at_ref[0]
    docs = jnp.broadcast_to(doc_ref[...].astype(f32), (TOK, TOK)).T.astype(bf16)
    for out_ref, which in ((own_ref, core), (other_ref, 1 - core)):
        for half in range(2):
            out_ref[:, half * QTR : (half + 1) * QTR] = pick(which, key_ref, half)
            out_ref[:, HALF + half * QTR : HALF + (half + 1) * QTR] = pick(which, value_ref, half)
        out_ref[:, 2 * HALF :] = docs


def own_rows(core):
    return pl.ds(pl.multiple_of(core * TOK, TOK), TOK)


def grad_attended_kernel(
    at_ref, query_ref, query_other_ref, grad_ref, grad_other_ref, weight_ref,
    attended_grad_ref, query_all_ref, grad_all_ref,
):
    core = at_ref[0]
    mine, other = own_rows(core), own_rows(1 - core)
    for half in range(2):
        cols = slice(half * QTR, (half + 1) * QTR)
        query_all_ref[mine, cols] = pick(core, query_ref, half)
        query_all_ref[other, cols] = pick(core, query_other_ref, half)
    grad_all_ref[mine, :] = grad_ref[...]
    grad_all_ref[other, :] = grad_other_ref[...]
    grad_rows = grad_all_ref[...]
    for half in range(2):
        start = pl.multiple_of(half * HALF + core * QTR, QTR)
        weight_rows = weight_ref[pl.ds(start, QTR), :]
        attended_grad_ref[:, half * QTR : (half + 1) * QTR] = nt(grad_rows, weight_rows).astype(bf16)


def place_blocks(core, own_ref, other_ref, before_ref, crossed_ref, all_ref):
    for ref, place in (
        (before_ref, core), (crossed_ref, 1 - core), (own_ref, 2 + core), (other_ref, 3 - core)
    ):
        all_ref[pl.ds(pl.multiple_of(place * TOK, TOK), TOK), :] = ref[...]


def forward_kernel(
    at_ref, owner_ref, query_ref, grad_ref, own_ref, other_ref, before_ref, crossed_ref,
    terms_ref, weights_ref, all_ref, attended_ref,
):
    core, chip = at_ref[0], at_ref[1]
    place_blocks(core, own_ref, other_ref, before_ref, crossed_ref, all_ref)
    doc_cols = [all_ref[b * TOK : (b + 1) * TOK, 2 * HALF :].astype(f32) for b in range(4)]
    doc_row = jnp.concatenate([block.T for block in doc_cols], axis=1)
    query_at = lax.broadcasted_iota(jnp.int32, (TOK, 3 * TOK), 0)
    key_at = lax.broadcasted_iota(jnp.int32, (TOK, 3 * TOK), 1)
    window = (key_at <= query_at + PAIR) & (key_at > query_at)
    for part in range(2):
        same = jnp.concatenate([doc_cols[2 + part]] * 3, axis=1) == doc_row[:, part * TOK : (part + 3) * TOK]
        present = key_at + part * TOK >= jnp.where(chip > 0, 0, PAIR)
        visible = window & same & present
        rows = slice(part * TOK, (part + 1) * TOK)
        keys = slice(part * TOK, (part + 3) * TOK)
        for head in range(4):
            cols = slice(head * HD, (head + 1) * HD)
            value_cols = slice(HALF + head * HD, HALF + (head + 1) * HD)
            scores = nt(query_ref[rows, cols], all_ref[keys, cols]) * head_scale
            scores = jnp.where(visible, scores, masked_score)
            row_max = jnp.max(scores, axis=1, keepdims=True)
            grown = jnp.exp(scores - row_max)
            total = jnp.sum(grown, axis=1, keepdims=True)
            weights = (grown * (1.0 / total)).astype(bf16)
            weights_ref[head, part] = weights
            attended_ref[rows, cols] = nn(weights, all_ref[keys, value_cols]).astype(bf16)
    for i in range(2):
        turned = attended_ref[:, i * QTR : (i + 1) * QTR].astype(f32).T.astype(bf16)
        for j in range(4):
            slot = owner_ref[4 * i + j]
            term = (nn(turned, grad_ref[:, j * BLK : (j + 1) * BLK]) * weight_scale).astype(bf16)
            terms_ref[0, slot] = term[:PART]
            terms_ref[1, slot] = term[PART:]


def backward_kernel(
    at_ref, weights_ref, query_ref, grad_ref, own_ref, other_ref, before_ref, crossed_ref,
    query_out_ref, sent_ref, kept_ref, all_ref, sum_ref,
):
    core = at_ref[0]
    place_blocks(core, own_ref, other_ref, before_ref, crossed_ref, all_ref)
    sum_ref[...] = jnp.zeros_like(sum_ref)
    for part in range(2):
        rows = slice(part * TOK, (part + 1) * TOK)
        keys = slice(part * TOK, (part + 3) * TOK)
        for head in range(4):
            cols = slice(head * HD, (head + 1) * HD)
            value_cols = slice(HALF + head * HD, HALF + (head + 1) * HD)
            low = weights_ref[head, part]
            weights = low.astype(f32)
            grad_head = grad_ref[rows, cols]
            query_head = query_ref[rows, cols]
            grad_weights = nt(grad_head, all_ref[keys, value_cols])
            grad_dot = jnp.sum(weights * grad_weights, axis=1, keepdims=True)
            grad_scores = (weights * (grad_weights - grad_dot)).astype(bf16)
            query_out_ref[rows, cols] = (nn(grad_scores, all_ref[keys, cols]) * head_scale).astype(bf16)
            sum_ref[keys, cols] += tn(grad_scores, query_head) * head_scale
            sum_ref[keys, value_cols] += tn(low, grad_head)
    sent_ref[...] = sum_ref[:PAIR].astype(bf16)
    kept_ref[...] = sum_ref[PAIR:]


def gather_grads_kernel(at_ref, query_ref, kept_ref, back_ref, mine_ref, other_ref):
    core = at_ref[0]
    for out_ref, rows in ((mine_ref, own_rows(core)), (other_ref, own_rows(1 - core))):
        out_ref[:, :HALF] = query_ref[rows, :]
        out_ref[:, HALF:] = (kept_ref[rows, :] + back_ref[rows, :].astype(f32)).astype(bf16)


def whole_width_kernel(at_ref, mine_ref, other_ref, query_ref, key_ref, value_ref):
    core = at_ref[0]
    for n, out_ref in enumerate((query_ref, key_ref, value_ref)):
        for half in range(2):
            cols = slice(n * HALF + half * QTR, n * HALF + (half + 1) * QTR)
            mine, other = mine_ref[:, cols], other_ref[:, cols]
            out_ref[0, :, half * HALF : half * HALF + QTR] = jnp.where(core == 0, mine, other)
            out_ref[0, :, half * HALF + QTR : (half + 1) * HALF] = jnp.where(core == 0, other, mine)


def sum_parts_kernel(parts_ref, total_ref):
    total = parts_ref[0].astype(f32)
    for n in range(1, N_OUTER):
        total = total + parts_ref[n].astype(f32)
    total_ref[...] = total.astype(bf16)


def newton_kernel(
    at_ref, grad_ref, grad_zl_ref, grad_c_ref, grad_zl_c_ref, stats_ref, stat_rows_ref,
    new_rows_ref, update_ref, slot_ref, left_ref, right_ref,
):
    core, low, row_first = at_ref[0], at_ref[2], at_ref[3]
    for ref, c, zl in (
        (grad_ref, core, low), (grad_zl_ref, core, 1 - low),
        (grad_c_ref, 1 - core, low), (grad_zl_c_ref, 1 - core, 1 - low),
    ):
        slot_ref[pl.ds(pl.multiple_of((2 * c + zl) * PART, PART), PART), :] = ref[...]
    slot = slot_ref[...]
    own = pl.ds(pl.multiple_of(row_first, ROWS), ROWS)
    left_ref[...] = nt(slot, slot)
    right_ref[...] = tn(slot, slot)
    new_rows_ref[0, 0] = decay_rate * stat_rows_ref[0, 0] + left_ref[own, :]
    new_rows_ref[0, 1] = decay_rate * stat_rows_ref[0, 1] + right_ref[own, :]
    left = decay_rate * stats_ref[0].astype(f32) + left_ref[...]
    right = decay_rate * stats_ref[1].astype(f32) + right_ref[...]

    def scaled(stat):
        norm_square = jnp.sum(jnp.sum(stat * stat, axis=0, keepdims=True), axis=1, keepdims=True)
        matrix = stat * lax.rsqrt(norm_square)
        low_matrix = matrix.astype(bf16)
        step = (nn(low_matrix, low_matrix) - 10.0 * matrix).astype(bf16)
        return matrix, low_matrix, step, jnp.exp(-0.125 * jnp.log(norm_square))

    left_matrix, left_low, left_step, left_scale = scaled(left)
    right_matrix, right_low, right_step, right_scale = scaled(right)
    left_ref[...] = left_matrix
    identity_rows = jnp.where(
        lax.broadcasted_iota(jnp.int32, (ROWS, BLK), 0) + row_first
        == lax.broadcasted_iota(jnp.int32, (ROWS, BLK), 1),
        1.0,
        0.0,
    )

    def rooted(factor, low_matrix, step):
        square = (25.0 * factor + nn(factor.astype(bf16), step)) * 0.0625
        fourth = (25.0 * square + nn(square.astype(bf16), step)) * 0.0625
        return (5.0 * factor - nn(fourth.astype(bf16), low_matrix)) * 0.25

    left_factor = (5.0 * identity_rows - left_ref[own, :]) * 0.25
    left_rows = rooted(left_factor, left_low, left_step)
    moved = nn(left_rows.astype(bf16), slot)
    right_factor = (5.0 * moved - nn(moved.astype(bf16), right_low)) * 0.25
    update = rooted(right_factor, right_low, right_step) * (step_scale * left_scale * right_scale)
    update_low = update.astype(bf16)
    for n in range(NBLK):
        update_ref[n] = update_low


def order_kernel(owner_ref, slots_ref, blocks_ref, sems):
    copies = [
        pltpu.make_async_copy(slots_ref.at[owner_ref[block]], blocks_ref.at[block], sems.at[block])
        for block in range(NBLK)
    ]
    for copy in copies:
        copy.start()
    for copy in copies:
        copy.wait()


def in_block_order(owners, slots):
    return pl.pallas_call(
        order_kernel,
        out_shape=shaped((NBLK, ROWS, BLK), bf16),
        in_specs=[SCALARS, ANYWHERE],
        out_specs=ANYWHERE,
        scratch_shapes=[pltpu.SemaphoreType.DMA((NBLK,))],
        name="order",
    )(owners, slots)


def gather_stats_kernel(at_ref, mine_ref, other_ref, stats_ref):
    core, along, low = at_ref[0], at_ref[4], at_ref[2]
    for ref, c in ((mine_ref, core), (other_ref, 1 - core)):
        for dy in range(4):
            for dz in range(2):
                place = (low ^ dz) * 8 + (along ^ dy) * 2 + c
                rows = pl.ds(pl.multiple_of(place * ROWS, ROWS), ROWS)
                for side in range(2):
                    stats_ref[side, rows, :] = ref[dy, dz, side]


def swapped(block, axis, mask=1):
    n = lax.axis_size(axis)
    return lax.ppermute(block, axis, [(i, i ^ mask) for i in range(n)])


def local(query_states, key_states, value_states, grad_out, doc_ids, out_weight, owners, statistics):
    core, low, along = lax.axis_index("c"), lax.axis_index("zl"), lax.axis_index("y")
    chip = low * 4 + along
    at = jnp.stack([core, chip, low, (chip * 2 + core) * ROWS, along]).astype(jnp.int32)
    query, key, value, grad = query_states[0], key_states[0], value_states[0], grad_out[0]

    own, other = call(
        pack_kernel,
        (shaped((TOK, KVW), bf16), shaped((TOK, KVW), bf16)),
        (at, key, value, doc_ids),
        name="pack",
    )
    before = lax.ppermute(own, SEQ, [(i, i + 2) for i in range(N_SEQ - 2)])
    crossed = lax.ppermute(other, SEQ, [(i, (i ^ 1) + 2) for i in range(N_SEQ - 2)])
    partner = swapped(other, "c")
    query_partner = swapped(query, "c")
    grad_partner = swapped(grad, "c")

    stats_own = statistics[0].astype(bf16)
    stats_pair = jnp.stack([stats_own, swapped(stats_own, "zl")])

    attended_grad, query_all, grad_all = call(
        grad_attended_kernel,
        (shaped((PAIR, HALF), bf16), shaped((PAIR, HALF), bf16), shaped((PAIR, D), bf16)),
        (at, query, query_partner, grad, grad_partner, out_weight),
        flops=2 * PAIR * HALF * D,
        nbytes=8 * 2**20,
        name="grad_attended",
    )
    terms, weights = call(
        forward_kernel,
        (shaped((2, NBLK, PART, BLK), bf16), shaped((4, 2, TOK, 3 * TOK), bf16)),
        (at, owners, query_all, grad_all, own, partner, before, crossed),
        scratch=(pltpu.VMEM((2 * PAIR, KVW), bf16), pltpu.VMEM((PAIR, HALF), bf16)),
        flops=2 * PAIR * HALF * (D + 6 * TOK),
        nbytes=6 * 2**20,
        name="forward",
    )
    stats_pair, terms = lax.optimization_barrier((stats_pair, terms))
    parts = lax.all_to_all(terms.reshape(N_OUTER, PART, BLK), OUTER, 0, 0, tiled=True)
    stats_mine = jnp.stack([stats_pair] + [swapped(stats_pair, "y", n) for n in (1, 2, 3)])
    stats_other = swapped(stats_mine, "c")
    stats_all = call(
        gather_stats_kernel,
        shaped((2, BLK, BLK), bf16),
        (at, stats_mine, stats_other),
        nbytes=2 * 2**20,
        name="gather_stats",
    )
    over_outer = call(
        sum_parts_kernel, shaped((PART, BLK), bf16), (parts,), nbytes=2 * 2**20, name="sum_outer"
    )
    weights, over_outer = lax.optimization_barrier((weights, over_outer))
    others = [swapped(over_outer, "y", n) for n in (1, 2, 3)]

    query_grad, sent, kept = call(
        backward_kernel,
        (shaped((PAIR, HALF), bf16), shaped((PAIR, HW), bf16), shaped((PAIR, HW), f32)),
        (at, weights, query_all, attended_grad, own, partner, before, crossed),
        scratch=(pltpu.VMEM((2 * PAIR, KVW), bf16), pltpu.VMEM((2 * PAIR, HW), f32)),
        flops=2 * PAIR * HALF * 4 * 3 * TOK,
        nbytes=6 * 2**20,
        name="backward",
    )

    slot_part = sum((p.astype(f32) for p in others), over_outer.astype(f32)).astype(bf16)
    slot_zl = swapped(slot_part, "zl")
    slot_c = swapped(slot_part, "c")
    slot_zl_c = swapped(slot_zl, "c")
    back = lax.ppermute(sent, SEQ, [(i + 2, i) for i in range(N_SEQ - 2)])

    new_statistics, update_rows = call(
        newton_kernel,
        (shaped((1, 2, ROWS, BLK), f32), shaped((NBLK, ROWS, BLK), bf16)),
        (at, slot_part, slot_zl, slot_c, slot_zl_c, stats_all, statistics),
        scratch=(
            pltpu.VMEM((BLK, BLK), bf16), pltpu.VMEM((BLK, BLK), f32), pltpu.VMEM((BLK, BLK), f32)
        ),
        flops=2 * BLK**3 * 5,
        nbytes=4 * 2**20,
        name="newton",
    )
    slots = lax.all_to_all(update_rows, REP, 0, 0, tiled=True)
    update = in_block_order(owners, slots)

    back, kept, _ = lax.optimization_barrier((back, kept, update_rows))
    mine, theirs = call(
        gather_grads_kernel,
        (shaped((TOK, 3 * HALF), bf16), shaped((TOK, 3 * HALF), bf16)),
        (at, query_grad, kept, back),
        name="gather_grads",
    )
    received = swapped(theirs, "c")
    query_out, key_out, value_out = call(
        whole_width_kernel,
        tuple(shaped((1, TOK, HW), bf16) for _ in range(3)),
        (at, mine, received),
        name="whole_width",
    )
    return query_out, key_out, value_out, new_statistics, update


def solution(mesh):
    split = Mesh(mesh.devices.reshape(2, 4, 2, 2, 4), ("zl", "y", "c", "zh", "x"))
    tokens = P(REP, SEQ, None)
    return jax.shard_map(
        local,
        mesh=split,
        in_specs=(
            tokens, tokens, tokens, tokens, P(REP, SEQ), P(), P(), P(REP, None, SEQ, None),
        ),
        out_specs=(tokens, tokens, tokens, P(REP, None, SEQ, None), P(None, SEQ, None)),
        check_vma=False,
    )
```

```python
import functools

import jax
import jax.numpy as jnp
from jax import lax
from jax.experimental import pallas as pl
from jax.experimental.pallas import tpu as pltpu
from jax.sharding import Mesh, PartitionSpec as P

D = 2048
HD = 128
HW = 1024
TOK = 128
BLK = 512
NBLK = 8
HALF = HW // 2
PAIR = 2 * TOK
QTR = 256
KVW = 2 * HALF + TOK

SEQ = ("zl", "y", "c")
REP = ("zh", "x")
OUTER = ("zl", "y", "zh", "x")
PLANE = ("zl", "y")
N_SEQ = 16
N_PLANE = 8
N_OUTER = N_PLANE * NBLK
ROWS = BLK // N_SEQ

masked_score = -1e30
decay_rate = 0.9
step_scale = 16.0
head_scale = HD ** (-0.5)
weight_scale = 1.0 / 16384.0

f32 = jnp.float32
bf16 = jnp.bfloat16
VMEM_LIMIT = 60 * 1024 * 1024
ANYWHERE = pl.BlockSpec(memory_space=pl.ANY)
SCALARS = pl.BlockSpec(memory_space=pltpu.SMEM)


def nt(left, right):
    return lax.dot_general(left, right, (((1,), (1,)), ((), ())), preferred_element_type=f32)


def tn(left, right):
    return lax.dot_general(left, right, (((0,), (0,)), ((), ())), preferred_element_type=f32)


def nn(left, right):
    return lax.dot_general(left, right, (((1,), (0,)), ((), ())), preferred_element_type=f32)


def whole(array):
    zeros = (0,) * len(array.shape)
    return pl.BlockSpec(tuple(array.shape), lambda i: zeros)


def call(body, outs, args, scratch=(), flops=0, nbytes=0, name=None, manual=False):
    place = (lambda array: ANYWHERE) if manual else whole
    specs = [SCALARS if a.dtype == jnp.int32 and a.ndim == 1 else place(a) for a in args]
    return pl.pallas_call(
        body,
        grid=(1,),
        out_shape=outs,
        in_specs=specs,
        out_specs=jax.tree.map(place, outs),
        scratch_shapes=list(scratch),
        compiler_params=pltpu.CompilerParams(vmem_limit_bytes=VMEM_LIMIT),
        cost_estimate=pl.CostEstimate(flops=flops, bytes_accessed=nbytes, transcendentals=0),
        name=name,
    )(*args)


def shaped(shape, dtype):
    return jax.ShapeDtypeStruct(shape, dtype)


def pick(core, ref, half):
    first = ref[:, half * HALF : half * HALF + QTR]
    second = ref[:, half * HALF + QTR : (half + 1) * HALF]
    return jnp.where(core == 0, first, second)


def pack_kernel(at_ref, key_ref, value_ref, doc_ref, own_ref, other_ref):
    core = at_ref[0]
    docs = jnp.broadcast_to(doc_ref[...].astype(f32), (TOK, TOK)).T.astype(bf16)
    for out_ref, which in ((own_ref, core), (other_ref, 1 - core)):
        for half in range(2):
            out_ref[:, half * QTR : (half + 1) * QTR] = pick(which, key_ref, half)
            out_ref[:, HALF + half * QTR : HALF + (half + 1) * QTR] = pick(which, value_ref, half)
        out_ref[:, 2 * HALF :] = docs


def own_rows(core):
    return pl.ds(pl.multiple_of(core * TOK, TOK), TOK)


def grad_attended_kernel(
    at_ref, query_ref, query_other_ref, grad_ref, grad_other_ref, weight_ref,
    attended_grad_ref, query_all_ref, grad_all_ref,
):
    core = at_ref[0]
    mine, other = own_rows(core), own_rows(1 - core)
    for half in range(2):
        cols = slice(half * QTR, (half + 1) * QTR)
        query_all_ref[mine, cols] = pick(core, query_ref, half)
        query_all_ref[other, cols] = pick(core, query_other_ref, half)
    grad_all_ref[mine, :] = grad_ref[...]
    grad_all_ref[other, :] = grad_other_ref[...]
    grad_rows = grad_all_ref[...]
    for half in range(2):
        start = pl.multiple_of(half * HALF + core * QTR, QTR)
        weight_rows = weight_ref[pl.ds(start, QTR), :]
        attended_grad_ref[:, half * QTR : (half + 1) * QTR] = nt(grad_rows, weight_rows).astype(bf16)


def place_blocks(core, own_ref, other_ref, before_ref, crossed_ref, all_ref):
    for ref, place in (
        (before_ref, core), (crossed_ref, 1 - core), (own_ref, 2 + core), (other_ref, 3 - core)
    ):
        all_ref[pl.ds(pl.multiple_of(place * TOK, TOK), TOK), :] = ref[...]


def forward_kernel(
    at_ref, owner_ref, query_hbm, grad_hbm, own_hbm, other_hbm, before_hbm, crossed_hbm,
    terms_hbm, weights_hbm,
    query_ref, grad_ref, all_ref, attended_ref, weights_ref, terms_ref, in_sems, out_sems,
):
    core, chip = at_ref[0], at_ref[1]
    arrivals = [pltpu.make_async_copy(query_hbm, query_ref, in_sems.at[0])]
    for n, (ref, place) in enumerate((
        (own_hbm, 2 + core), (other_hbm, 3 - core), (before_hbm, core), (crossed_hbm, 1 - core)
    )):
        rows = pl.ds(pl.multiple_of(place * TOK, TOK), TOK)
        arrivals.append(pltpu.make_async_copy(ref, all_ref.at[rows], in_sems.at[1 + n]))
    grad_arrival = pltpu.make_async_copy(grad_hbm, grad_ref, in_sems.at[5])
    for copy in arrivals:
        copy.start()
    grad_arrival.start()
    for copy in arrivals:
        copy.wait()
    doc_cols = [all_ref[b * TOK : (b + 1) * TOK, 2 * HALF :].astype(f32) for b in range(4)]
    doc_row = jnp.concatenate([block.T for block in doc_cols], axis=1)
    query_at = lax.broadcasted_iota(jnp.int32, (TOK, 3 * TOK), 0)
    key_at = lax.broadcasted_iota(jnp.int32, (TOK, 3 * TOK), 1)
    window = (key_at <= query_at + PAIR) & (key_at > query_at)
    for part in range(2):
        same = jnp.concatenate([doc_cols[2 + part]] * 3, axis=1) == doc_row[:, part * TOK : (part + 3) * TOK]
        present = key_at + part * TOK >= jnp.where(chip > 0, 0, PAIR)
        visible = window & same & present
        rows = slice(part * TOK, (part + 1) * TOK)
        keys = slice(part * TOK, (part + 3) * TOK)
        for head in range(4):
            cols = slice(head * HD, (head + 1) * HD)
            value_cols = slice(HALF + head * HD, HALF + (head + 1) * HD)
            scores = nt(query_ref[rows, cols], all_ref[keys, cols]) * head_scale
            scores = jnp.where(visible, scores, masked_score)
            row_max = jnp.max(scores, axis=1, keepdims=True)
            grown = jnp.exp(scores - row_max)
            total = jnp.sum(grown, axis=1, keepdims=True)
            weights = (grown * (1.0 / total)).astype(bf16)
            weights_ref[head, part] = weights
            attended_ref[rows, cols] = nn(weights, all_ref[keys, value_cols]).astype(bf16)
    departures = [pltpu.make_async_copy(weights_ref, weights_hbm, out_sems.at[NBLK])]
    departures[0].start()
    grad_arrival.wait()
    for i in range(2):
        turned = attended_ref[:, i * QTR : (i + 1) * QTR].astype(f32).T.astype(bf16)
        for j in range(4):
            block = 4 * i + j
            term = (nn(turned, grad_ref[:, j * BLK : (j + 1) * BLK]) * weight_scale).astype(bf16)
            terms_ref[block] = term.reshape(N_PLANE, ROWS, BLK)
            copy = pltpu.make_async_copy(
                terms_ref.at[block], terms_hbm.at[:, owner_ref[block]], out_sems.at[block]
            )
            copy.start()
            departures.append(copy)
    for copy in departures:
        copy.wait()


def backward_kernel(
    at_ref, weights_ref, query_ref, grad_ref, own_ref, other_ref, before_ref, crossed_ref,
    query_out_ref, sent_ref, kept_ref, all_ref, sum_ref,
):
    core = at_ref[0]
    place_blocks(core, own_ref, other_ref, before_ref, crossed_ref, all_ref)
    sum_ref[...] = jnp.zeros_like(sum_ref)
    for part in range(2):
        rows = slice(part * TOK, (part + 1) * TOK)
        keys = slice(part * TOK, (part + 3) * TOK)
        for head in range(4):
            cols = slice(head * HD, (head + 1) * HD)
            value_cols = slice(HALF + head * HD, HALF + (head + 1) * HD)
            low = weights_ref[head, part]
            weights = low.astype(f32)
            grad_head = grad_ref[rows, cols]
            query_head = query_ref[rows, cols]
            grad_weights = nt(grad_head, all_ref[keys, value_cols])
            grad_dot = jnp.sum(weights * grad_weights, axis=1, keepdims=True)
            grad_scores = (weights * (grad_weights - grad_dot)).astype(bf16)
            query_out_ref[rows, cols] = (nn(grad_scores, all_ref[keys, cols]) * head_scale).astype(bf16)
            sum_ref[keys, cols] += tn(grad_scores, query_head) * head_scale
            sum_ref[keys, value_cols] += tn(low, grad_head)
    sent_ref[...] = sum_ref[:PAIR].astype(bf16)
    kept_ref[...] = sum_ref[PAIR:]


def gather_grads_kernel(at_ref, query_ref, kept_ref, back_ref, mine_ref, other_ref):
    core = at_ref[0]
    for out_ref, rows in ((mine_ref, own_rows(core)), (other_ref, own_rows(1 - core))):
        out_ref[:, :HALF] = query_ref[rows, :]
        out_ref[:, HALF:] = (kept_ref[rows, :] + back_ref[rows, :].astype(f32)).astype(bf16)


def whole_width_kernel(at_ref, mine_ref, other_ref, query_ref, key_ref, value_ref):
    core = at_ref[0]
    for n, out_ref in enumerate((query_ref, key_ref, value_ref)):
        for half in range(2):
            cols = slice(n * HALF + half * QTR, n * HALF + (half + 1) * QTR)
            mine, other = mine_ref[:, cols], other_ref[:, cols]
            out_ref[0, :, half * HALF : half * HALF + QTR] = jnp.where(core == 0, mine, other)
            out_ref[0, :, half * HALF + QTR : (half + 1) * HALF] = jnp.where(core == 0, other, mine)


def sum_parts_kernel(parts_ref, total_ref):
    total = parts_ref[0].astype(f32)
    for n in range(1, N_OUTER):
        total = total + parts_ref[n].astype(f32)
    total_low = total.astype(bf16)
    for n in range(N_PLANE):
        total_ref[n] = total_low


def newton_kernel(
    at_ref, grad_ref, grad_c_ref, stats_ref, stat_rows_ref,
    new_rows_ref, update_ref, slot_ref, left_ref, right_ref,
):
    core, row_first = at_ref[0], at_ref[3]
    for ref, c in ((grad_ref, core), (grad_c_ref, 1 - core)):
        slot_ref[pl.ds(pl.multiple_of(c * QTR, QTR), QTR), :] = ref[...].reshape(QTR, BLK)
    slot = slot_ref[...]
    own = pl.ds(pl.multiple_of(row_first, ROWS), ROWS)
    left_ref[...] = nt(slot, slot)
    right_ref[...] = tn(slot, slot)
    new_rows_ref[0, 0] = decay_rate * stat_rows_ref[0, 0] + left_ref[own, :]
    new_rows_ref[0, 1] = decay_rate * stat_rows_ref[0, 1] + right_ref[own, :]
    left = decay_rate * stats_ref[0].astype(f32) + left_ref[...]
    right = decay_rate * stats_ref[1].astype(f32) + right_ref[...]

    def scaled(stat):
        norm_square = jnp.sum(jnp.sum(stat * stat, axis=0, keepdims=True), axis=1, keepdims=True)
        matrix = stat * lax.rsqrt(norm_square)
        low_matrix = matrix.astype(bf16)
        step = (nn(low_matrix, low_matrix) - 10.0 * matrix).astype(bf16)
        return matrix, low_matrix, step, jnp.exp(-0.125 * jnp.log(norm_square))

    left_matrix, left_low, left_step, left_scale = scaled(left)
    right_matrix, right_low, right_step, right_scale = scaled(right)
    left_ref[...] = left_matrix
    identity_rows = jnp.where(
        lax.broadcasted_iota(jnp.int32, (ROWS, BLK), 0) + row_first
        == lax.broadcasted_iota(jnp.int32, (ROWS, BLK), 1),
        1.0,
        0.0,
    )

    def rooted(factor, low_matrix, step):
        square = (25.0 * factor + nn(factor.astype(bf16), step)) * 0.0625
        fourth = (25.0 * square + nn(square.astype(bf16), step)) * 0.0625
        return (5.0 * factor - nn(fourth.astype(bf16), low_matrix)) * 0.25

    left_factor = (5.0 * identity_rows - left_ref[own, :]) * 0.25
    left_rows = rooted(left_factor, left_low, left_step)
    moved = nn(left_rows.astype(bf16), slot)
    right_factor = (5.0 * moved - nn(moved.astype(bf16), right_low)) * 0.25
    update = rooted(right_factor, right_low, right_step) * (step_scale * left_scale * right_scale)
    update_low = update.astype(bf16)
    for n in range(NBLK):
        update_ref[n] = update_low


def order_kernel(owner_ref, slots_hbm, blocks_hbm, blocks_ref, in_sems, out_sems):
    arrivals, departures = [], []
    for block in range(NBLK):
        arrivals.append(pltpu.make_async_copy(
            slots_hbm.at[owner_ref[block]], blocks_ref.at[block], in_sems.at[block]
        ))
        departures.append(pltpu.make_async_copy(
            blocks_ref.at[block], blocks_hbm.at[block], out_sems.at[block]
        ))
        arrivals[block].start()
    for block in range(NBLK):
        arrivals[block].wait()
        departures[block].start()
    for copy in departures:
        copy.wait()


def gather_stats_kernel(at_ref, mine_ref, other_ref, stats_ref):
    core, along, low = at_ref[0], at_ref[4], at_ref[2]
    for ref, c in ((mine_ref, core), (other_ref, 1 - core)):
        for dy in range(4):
            for dz in range(2):
                place = (low ^ dz) * 8 + (along ^ dy) * 2 + c
                rows = pl.ds(pl.multiple_of(place * ROWS, ROWS), ROWS)
                for side in range(2):
                    stats_ref[side, rows, :] = ref[dy, dz, side]


def swapped(block, axis, mask=1):
    n = lax.axis_size(axis)
    return lax.ppermute(block, axis, [(i, i ^ mask) for i in range(n)])


def local(query_states, key_states, value_states, grad_out, doc_ids, out_weight, owners, statistics):
    core, low, along = lax.axis_index("c"), lax.axis_index("zl"), lax.axis_index("y")
    chip = low * 4 + along
    at = jnp.stack([core, chip, low, (chip * 2 + core) * ROWS, along]).astype(jnp.int32)
    query, key, value, grad = query_states[0], key_states[0], value_states[0], grad_out[0]

    own, other = call(
        pack_kernel,
        (shaped((TOK, KVW), bf16), shaped((TOK, KVW), bf16)),
        (at, key, value, doc_ids),
        name="pack",
    )
    before = lax.ppermute(own, SEQ, [(i, i + 2) for i in range(N_SEQ - 2)])
    crossed = lax.ppermute(other, SEQ, [(i, (i ^ 1) + 2) for i in range(N_SEQ - 2)])
    partner = swapped(other, "c")
    query_partner = swapped(query, "c")
    grad_partner = swapped(grad, "c")
    statistics, own, other = lax.optimization_barrier((statistics, own, other))
    stats_own = statistics[0].astype(bf16)
    stats_pair = jnp.stack([stats_own, swapped(stats_own, "zl")])
    stats_mine = jnp.stack([stats_pair] + [swapped(stats_pair, "y", n) for n in (1, 2, 3)])
    stats_other = swapped(stats_mine, "c")

    attended_grad, query_all, grad_all = call(
        grad_attended_kernel,
        (shaped((PAIR, HALF), bf16), shaped((PAIR, HALF), bf16), shaped((PAIR, D), bf16)),
        (at, query, query_partner, grad, grad_partner, out_weight),
        flops=2 * PAIR * HALF * D,
        nbytes=8 * 2**20,
        name="grad_attended",
    )
    terms, weights = call(
        forward_kernel,
        (shaped((N_PLANE, NBLK, ROWS, BLK), bf16), shaped((4, 2, TOK, 3 * TOK), bf16)),
        (at, owners, query_all, grad_all, own, partner, before, crossed),
        scratch=(
            pltpu.VMEM((PAIR, HALF), bf16),
            pltpu.VMEM((PAIR, D), bf16),
            pltpu.VMEM((2 * PAIR, KVW), bf16),
            pltpu.VMEM((PAIR, HALF), bf16),
            pltpu.VMEM((4, 2, TOK, 3 * TOK), bf16),
            pltpu.VMEM((NBLK, N_PLANE, ROWS, BLK), bf16),
            pltpu.SemaphoreType.DMA((6,)),
            pltpu.SemaphoreType.DMA((NBLK + 1,)),
        ),
        flops=2 * PAIR * HALF * (D + 6 * TOK),
        nbytes=6 * 2**20,
        name="forward",
        manual=True,
    )
    parts = lax.all_to_all(terms.reshape(N_OUTER, ROWS, BLK), OUTER, 0, 0, tiled=True)
    query_grad, sent, kept = call(
        backward_kernel,
        (shaped((PAIR, HALF), bf16), shaped((PAIR, HW), bf16), shaped((PAIR, HW), f32)),
        (at, weights, query_all, attended_grad, own, partner, before, crossed),
        scratch=(pltpu.VMEM((2 * PAIR, KVW), bf16), pltpu.VMEM((2 * PAIR, HW), f32)),
        flops=2 * PAIR * HALF * 4 * 3 * TOK,
        nbytes=6 * 2**20,
        name="backward",
    )
    stats_all = call(
        gather_stats_kernel,
        shaped((2, BLK, BLK), bf16),
        (at, stats_mine, stats_other),
        nbytes=2 * 2**20,
        name="gather_stats",
    )
    copies = call(
        sum_parts_kernel,
        shaped((N_PLANE, ROWS, BLK), bf16),
        (parts,),
        nbytes=2 * 2**20,
        name="sum_outer",
    )
    copies, sent = lax.optimization_barrier((copies, sent))
    half_slot = lax.all_to_all(copies, PLANE, 0, 0, tiled=True)
    half_slot_c = swapped(half_slot, "c")
    back = lax.ppermute(sent, SEQ, [(i + 2, i) for i in range(N_SEQ - 2)])

    new_statistics, update_rows = call(
        newton_kernel,
        (shaped((1, 2, ROWS, BLK), f32), shaped((NBLK, ROWS, BLK), bf16)),
        (at, half_slot, half_slot_c, stats_all, statistics),
        scratch=(
            pltpu.VMEM((BLK, BLK), bf16), pltpu.VMEM((BLK, BLK), f32), pltpu.VMEM((BLK, BLK), f32)
        ),
        flops=2 * BLK**3 * 5,
        nbytes=4 * 2**20,
        name="newton",
    )
    back, kept, _ = lax.optimization_barrier((back, kept, update_rows))
    slots = lax.all_to_all(update_rows, REP, 0, 0, tiled=True)
    mine, theirs = call(
        gather_grads_kernel,
        (shaped((TOK, 3 * HALF), bf16), shaped((TOK, 3 * HALF), bf16)),
        (at, query_grad, kept, back),
        name="gather_grads",
    )
    received = swapped(theirs, "c")
    query_out, key_out, value_out = call(
        whole_width_kernel,
        tuple(shaped((1, TOK, HW), bf16) for _ in range(3)),
        (at, mine, received),
        name="whole_width",
    )
    update = call(
        order_kernel,
        shaped((NBLK, ROWS, BLK), bf16),
        (owners, slots),
        scratch=(
            pltpu.VMEM((NBLK, ROWS, BLK), bf16),
            pltpu.SemaphoreType.DMA((NBLK,)),
            pltpu.SemaphoreType.DMA((NBLK,)),
        ),
        name="order",
        manual=True,
    )
    return query_out, key_out, value_out, new_statistics, update


def solution(mesh):
    split = Mesh(mesh.devices.reshape(2, 4, 2, 2, 4), ("zl", "y", "c", "zh", "x"))
    tokens = P(REP, SEQ, None)
    return jax.shard_map(
        local,
        mesh=split,
        in_specs=(
            tokens, tokens, tokens, tokens, P(REP, SEQ), P(), P(), P(REP, None, SEQ, None),
        ),
        out_specs=(tokens, tokens, tokens, P(REP, None, SEQ, None), P(None, SEQ, None)),
        check_vma=False,
    )
```

```python
import functools

import jax
import jax.numpy as jnp
from jax import lax
from jax.experimental import pallas as pl
from jax.experimental.pallas import tpu as pltpu
from jax.sharding import Mesh, PartitionSpec as P

D = 2048
HD = 128
HW = 1024
TOK = 128
BLK = 512
NBLK = 8
HALF = HW // 2
PAIR = 2 * TOK
QTR = 256
KVW = 2 * HALF + TOK

SEQ = ("zl", "y", "c")
REP = ("zh", "x")
OUTER = ("zl", "y", "zh", "x")
PLANE = ("zl", "y")
N_SEQ = 16
N_PLANE = 8
N_OUTER = N_PLANE * NBLK
ROWS = BLK // N_SEQ

masked_score = -1e30
decay_rate = 0.9
step_scale = 16.0
head_scale = HD ** (-0.5)
weight_scale = 1.0 / 16384.0

f32 = jnp.float32
bf16 = jnp.bfloat16
MIB = 1024 * 1024
ANYWHERE = pl.BlockSpec(memory_space=pl.ANY)
SCALARS = pl.BlockSpec(memory_space=pltpu.SMEM)


def nt(left, right):
    return lax.dot_general(left, right, (((1,), (1,)), ((), ())), preferred_element_type=f32)


def tn(left, right):
    return lax.dot_general(left, right, (((0,), (0,)), ((), ())), preferred_element_type=f32)


def nn(left, right):
    return lax.dot_general(left, right, (((1,), (0,)), ((), ())), preferred_element_type=f32)


def whole(array):
    zeros = (0,) * len(array.shape)
    return pl.BlockSpec(tuple(array.shape), lambda i: zeros)


def call(body, outs, args, scratch=(), flops=0, nbytes=0, name=None, manual=False, limit=24):
    place = (lambda array: ANYWHERE) if manual else whole
    specs = [SCALARS if a.dtype == jnp.int32 and a.ndim == 1 else place(a) for a in args]
    return pl.pallas_call(
        body,
        grid=(1,),
        out_shape=outs,
        in_specs=specs,
        out_specs=jax.tree.map(place, outs),
        scratch_shapes=list(scratch),
        compiler_params=pltpu.CompilerParams(vmem_limit_bytes=limit * MIB),
        cost_estimate=pl.CostEstimate(flops=flops, bytes_accessed=nbytes, transcendentals=0),
        name=name,
    )(*args)


def shaped(shape, dtype):
    return jax.ShapeDtypeStruct(shape, dtype)


def pick(core, ref, half):
    first = ref[:, half * HALF : half * HALF + QTR]
    second = ref[:, half * HALF + QTR : (half + 1) * HALF]
    return jnp.where(core == 0, first, second)


def pack_kernel(at_ref, key_ref, value_ref, doc_ref, own_ref, other_ref):
    core = at_ref[0]
    docs = jnp.broadcast_to(doc_ref[...].astype(f32), (TOK, TOK)).T.astype(bf16)
    for out_ref, which in ((own_ref, core), (other_ref, 1 - core)):
        for half in range(2):
            out_ref[:, half * QTR : (half + 1) * QTR] = pick(which, key_ref, half)
            out_ref[:, HALF + half * QTR : HALF + (half + 1) * QTR] = pick(which, value_ref, half)
        out_ref[:, 2 * HALF :] = docs


def own_rows(core):
    return pl.ds(pl.multiple_of(core * TOK, TOK), TOK)


def grad_attended_kernel(
    at_ref, query_ref, query_other_ref, grad_ref, grad_other_ref, weight_ref,
    attended_grad_ref, query_all_ref, grad_all_ref,
):
    core = at_ref[0]
    mine, other = own_rows(core), own_rows(1 - core)
    for half in range(2):
        cols = slice(half * QTR, (half + 1) * QTR)
        query_all_ref[mine, cols] = pick(core, query_ref, half)
        query_all_ref[other, cols] = pick(core, query_other_ref, half)
    grad_all_ref[mine, :] = grad_ref[...]
    grad_all_ref[other, :] = grad_other_ref[...]
    grad_rows = grad_all_ref[...]
    for half in range(2):
        start = pl.multiple_of(half * HALF + core * QTR, QTR)
        weight_rows = weight_ref[pl.ds(start, QTR), :]
        attended_grad_ref[:, half * QTR : (half + 1) * QTR] = nt(grad_rows, weight_rows).astype(bf16)


def place_blocks(core, own_ref, other_ref, before_ref, crossed_ref, all_ref):
    for ref, place in (
        (before_ref, core), (crossed_ref, 1 - core), (own_ref, 2 + core), (other_ref, 3 - core)
    ):
        all_ref[pl.ds(pl.multiple_of(place * TOK, TOK), TOK), :] = ref[...]


def forward_kernel(
    at_ref, owner_ref, query_hbm, grad_hbm, own_hbm, other_hbm, before_hbm, crossed_hbm,
    terms_hbm, weights_hbm,
    query_ref, grad_ref, all_ref, attended_ref, weights_ref, terms_ref, in_sems, out_sems,
):
    core, chip = at_ref[0], at_ref[1]
    arrivals = [pltpu.make_async_copy(query_hbm, query_ref, in_sems.at[0])]
    for n, (ref, place) in enumerate((
        (own_hbm, 2 + core), (other_hbm, 3 - core), (before_hbm, core), (crossed_hbm, 1 - core)
    )):
        rows = pl.ds(pl.multiple_of(place * TOK, TOK), TOK)
        arrivals.append(pltpu.make_async_copy(ref, all_ref.at[rows], in_sems.at[1 + n]))
    grad_arrival = pltpu.make_async_copy(grad_hbm, grad_ref, in_sems.at[5])
    for copy in arrivals:
        copy.start()
    grad_arrival.start()
    for copy in arrivals:
        copy.wait()
    doc_cols = [all_ref[b * TOK : (b + 1) * TOK, 2 * HALF :].astype(f32) for b in range(4)]
    doc_row = jnp.concatenate([block.T for block in doc_cols], axis=1)
    query_at = lax.broadcasted_iota(jnp.int32, (TOK, 3 * TOK), 0)
    key_at = lax.broadcasted_iota(jnp.int32, (TOK, 3 * TOK), 1)
    window = (key_at <= query_at + PAIR) & (key_at > query_at)
    for part in range(2):
        same = jnp.concatenate([doc_cols[2 + part]] * 3, axis=1) == doc_row[:, part * TOK : (part + 3) * TOK]
        present = key_at + part * TOK >= jnp.where(chip > 0, 0, PAIR)
        visible = window & same & present
        rows = slice(part * TOK, (part + 1) * TOK)
        keys = slice(part * TOK, (part + 3) * TOK)
        for head in range(4):
            cols = slice(head * HD, (head + 1) * HD)
            value_cols = slice(HALF + head * HD, HALF + (head + 1) * HD)
            scores = nt(query_ref[rows, cols], all_ref[keys, cols]) * head_scale
            scores = jnp.where(visible, scores, masked_score)
            row_max = jnp.max(scores, axis=1, keepdims=True)
            grown = jnp.exp(scores - row_max)
            total = jnp.sum(grown, axis=1, keepdims=True)
            weights = (grown * (1.0 / total)).astype(bf16)
            weights_ref[head, part] = weights
            attended_ref[rows, cols] = nn(weights, all_ref[keys, value_cols]).astype(bf16)
    departures = [pltpu.make_async_copy(weights_ref, weights_hbm, out_sems.at[NBLK])]
    departures[0].start()
    grad_arrival.wait()
    for i in range(2):
        turned = attended_ref[:, i * QTR : (i + 1) * QTR].astype(f32).T.astype(bf16)
        for j in range(4):
            block = 4 * i + j
            term = (nn(turned, grad_ref[:, j * BLK : (j + 1) * BLK]) * weight_scale).astype(bf16)
            terms_ref[block] = term.reshape(N_PLANE, ROWS, BLK)
            copy = pltpu.make_async_copy(
                terms_ref.at[block], terms_hbm.at[:, owner_ref[block]], out_sems.at[block]
            )
            copy.start()
            departures.append(copy)
    for copy in departures:
        copy.wait()


def backward_kernel(
    at_ref, weights_ref, query_ref, grad_ref, own_ref, other_ref, before_ref, crossed_ref,
    query_out_ref, sent_ref, kept_ref, all_ref, sum_ref,
):
    core = at_ref[0]
    place_blocks(core, own_ref, other_ref, before_ref, crossed_ref, all_ref)
    sum_ref[...] = jnp.zeros_like(sum_ref)
    for part in range(2):
        rows = slice(part * TOK, (part + 1) * TOK)
        keys = slice(part * TOK, (part + 3) * TOK)
        for head in range(4):
            cols = slice(head * HD, (head + 1) * HD)
            value_cols = slice(HALF + head * HD, HALF + (head + 1) * HD)
            low = weights_ref[head, part]
            weights = low.astype(f32)
            grad_head = grad_ref[rows, cols]
            query_head = query_ref[rows, cols]
            grad_weights = nt(grad_head, all_ref[keys, value_cols])
            grad_dot = jnp.sum(weights * grad_weights, axis=1, keepdims=True)
            grad_scores = (weights * (grad_weights - grad_dot)).astype(bf16)
            query_out_ref[rows, cols] = (nn(grad_scores, all_ref[keys, cols]) * head_scale).astype(bf16)
            sum_ref[keys, cols] += tn(grad_scores, query_head) * head_scale
            sum_ref[keys, value_cols] += tn(low, grad_head)
    sent_ref[...] = sum_ref[:PAIR].astype(bf16)
    kept_ref[...] = sum_ref[PAIR:]


def gather_grads_kernel(at_ref, query_ref, kept_ref, back_ref, mine_ref, other_ref):
    core = at_ref[0]
    for out_ref, rows in ((mine_ref, own_rows(core)), (other_ref, own_rows(1 - core))):
        out_ref[:, :HALF] = query_ref[rows, :]
        out_ref[:, HALF:] = (kept_ref[rows, :] + back_ref[rows, :].astype(f32)).astype(bf16)


def whole_width_kernel(at_ref, mine_ref, other_ref, query_ref, key_ref, value_ref):
    core = at_ref[0]
    for n, out_ref in enumerate((query_ref, key_ref, value_ref)):
        for half in range(2):
            cols = slice(n * HALF + half * QTR, n * HALF + (half + 1) * QTR)
            mine, other = mine_ref[:, cols], other_ref[:, cols]
            out_ref[0, :, half * HALF : half * HALF + QTR] = jnp.where(core == 0, mine, other)
            out_ref[0, :, half * HALF + QTR : (half + 1) * HALF] = jnp.where(core == 0, other, mine)


def sum_parts_kernel(parts_ref, stat_rows_ref, total_ref):
    total = parts_ref[0].astype(f32)
    for n in range(1, N_OUTER):
        total = total + parts_ref[n].astype(f32)
    total_low = total.astype(bf16)
    left_low, right_low = stat_rows_ref[0, 0].astype(bf16), stat_rows_ref[0, 1].astype(bf16)
    for n in range(N_PLANE):
        total_ref[n, :ROWS] = total_low
        total_ref[n, ROWS : 2 * ROWS] = left_low
        total_ref[n, 2 * ROWS :] = right_low


def newton_kernel(
    at_ref, half_ref, half_c_ref, stat_rows_ref,
    new_rows_ref, update_ref, slot_ref, stats_ref, left_ref, right_ref,
):
    core, row_first = at_ref[0], at_ref[3]
    for ref, c in ((half_ref, core), (half_c_ref, 1 - core)):
        for n in range(N_PLANE):
            rows = pl.ds(pl.multiple_of(c * QTR + n * ROWS, ROWS), ROWS)
            slot_ref[rows, :] = ref[n, :ROWS]
            rows = pl.ds(pl.multiple_of((2 * n + c) * ROWS, ROWS), ROWS)
            stats_ref[0, rows, :] = ref[n, ROWS : 2 * ROWS]
            stats_ref[1, rows, :] = ref[n, 2 * ROWS :]
    slot = slot_ref[...]
    own = pl.ds(pl.multiple_of(row_first, ROWS), ROWS)
    left_ref[...] = nt(slot, slot)
    right_ref[...] = tn(slot, slot)
    new_rows_ref[0, 0] = decay_rate * stat_rows_ref[0, 0] + left_ref[own, :]
    new_rows_ref[0, 1] = decay_rate * stat_rows_ref[0, 1] + right_ref[own, :]
    left = decay_rate * stats_ref[0].astype(f32) + left_ref[...]
    right = decay_rate * stats_ref[1].astype(f32) + right_ref[...]

    def scaled(stat):
        norm_square = jnp.sum(jnp.sum(stat * stat, axis=0, keepdims=True), axis=1, keepdims=True)
        matrix = stat * lax.rsqrt(norm_square)
        low_matrix = matrix.astype(bf16)
        step = (nn(low_matrix, low_matrix) - 10.0 * matrix).astype(bf16)
        return matrix, low_matrix, step, jnp.exp(-0.125 * jnp.log(norm_square))

    left_matrix, left_low, left_step, left_scale = scaled(left)
    right_matrix, right_low, right_step, right_scale = scaled(right)
    left_ref[...] = left_matrix
    identity_rows = jnp.where(
        lax.broadcasted_iota(jnp.int32, (ROWS, BLK), 0) + row_first
        == lax.broadcasted_iota(jnp.int32, (ROWS, BLK), 1),
        1.0,
        0.0,
    )

    def rooted(factor, low_matrix, step):
        square = (25.0 * factor + nn(factor.astype(bf16), step)) * 0.0625
        fourth = (25.0 * square + nn(square.astype(bf16), step)) * 0.0625
        return (5.0 * factor - nn(fourth.astype(bf16), low_matrix)) * 0.25

    left_factor = (5.0 * identity_rows - left_ref[own, :]) * 0.25
    left_rows = rooted(left_factor, left_low, left_step)
    moved = nn(left_rows.astype(bf16), slot)
    right_factor = (5.0 * moved - nn(moved.astype(bf16), right_low)) * 0.25
    update = rooted(right_factor, right_low, right_step) * (step_scale * left_scale * right_scale)
    update_low = update.astype(bf16)
    for n in range(NBLK):
        update_ref[n] = update_low


def order_kernel(owner_ref, slots_hbm, blocks_hbm, blocks_ref, in_sems, out_sems):
    arrivals, departures = [], []
    for block in range(NBLK):
        arrivals.append(pltpu.make_async_copy(
            slots_hbm.at[owner_ref[block]], blocks_ref.at[block], in_sems.at[block]
        ))
        departures.append(pltpu.make_async_copy(
            blocks_ref.at[block], blocks_hbm.at[block], out_sems.at[block]
        ))
        arrivals[block].start()
    for block in range(NBLK):
        arrivals[block].wait()
        departures[block].start()
    for copy in departures:
        copy.wait()


def swapped(block, axis, mask=1):
    n = lax.axis_size(axis)
    return lax.ppermute(block, axis, [(i, i ^ mask) for i in range(n)])


def local(query_states, key_states, value_states, grad_out, doc_ids, out_weight, owners, statistics):
    core, low, along = lax.axis_index("c"), lax.axis_index("zl"), lax.axis_index("y")
    chip = low * 4 + along
    at = jnp.stack([core, chip, low, (chip * 2 + core) * ROWS]).astype(jnp.int32)
    query, key, value, grad = query_states[0], key_states[0], value_states[0], grad_out[0]

    own, other = call(
        pack_kernel,
        (shaped((TOK, KVW), bf16), shaped((TOK, KVW), bf16)),
        (at, key, value, doc_ids),
        name="pack",
        limit=60,
    )
    before = lax.ppermute(own, SEQ, [(i, i + 2) for i in range(N_SEQ - 2)])
    crossed = lax.ppermute(other, SEQ, [(i, (i ^ 1) + 2) for i in range(N_SEQ - 2)])
    query, grad, own, other = lax.optimization_barrier((query, grad, own, other))
    partner = swapped(other, "c")
    query_partner = swapped(query, "c")
    grad_partner = swapped(grad, "c")
    attended_grad, query_all, grad_all = call(
        grad_attended_kernel,
        (shaped((PAIR, HALF), bf16), shaped((PAIR, HALF), bf16), shaped((PAIR, D), bf16)),
        (at, query, query_partner, grad, grad_partner, out_weight),
        flops=2 * PAIR * HALF * D,
        nbytes=8 * 2**20,
        name="grad_attended",
        limit=60,
    )
    terms, weights = call(
        forward_kernel,
        (shaped((N_PLANE, NBLK, ROWS, BLK), bf16), shaped((4, 2, TOK, 3 * TOK), bf16)),
        (at, owners, query_all, grad_all, own, partner, before, crossed),
        scratch=(
            pltpu.VMEM((PAIR, HALF), bf16),
            pltpu.VMEM((PAIR, D), bf16),
            pltpu.VMEM((2 * PAIR, KVW), bf16),
            pltpu.VMEM((PAIR, HALF), bf16),
            pltpu.VMEM((4, 2, TOK, 3 * TOK), bf16),
            pltpu.VMEM((NBLK, N_PLANE, ROWS, BLK), bf16),
            pltpu.SemaphoreType.DMA((6,)),
            pltpu.SemaphoreType.DMA((NBLK + 1,)),
        ),
        flops=2 * PAIR * HALF * (D + 6 * TOK),
        nbytes=6 * 2**20,
        name="forward",
        manual=True,
        limit=60,
    )
    parts = lax.all_to_all(terms.reshape(N_OUTER, ROWS, BLK), OUTER, 0, 0, tiled=True)
    query_grad, sent, kept = call(
        backward_kernel,
        (shaped((PAIR, HALF), bf16), shaped((PAIR, HW), bf16), shaped((PAIR, HW), f32)),
        (at, weights, query_all, attended_grad, own, partner, before, crossed),
        scratch=(pltpu.VMEM((2 * PAIR, KVW), bf16), pltpu.VMEM((2 * PAIR, HW), f32)),
        flops=2 * PAIR * HALF * 4 * 3 * TOK,
        nbytes=6 * 2**20,
        name="backward",
        limit=60,
    )
    back = lax.ppermute(sent, SEQ, [(i + 2, i) for i in range(N_SEQ - 2)])
    parts, kept = lax.optimization_barrier((parts, kept))
    copies = call(
        sum_parts_kernel,
        shaped((N_PLANE, 3 * ROWS, BLK), bf16),
        (parts, statistics),
        nbytes=2 * 2**20,
        name="sum_outer",
    )
    half_slot = lax.all_to_all(copies, PLANE, 0, 0, tiled=True)
    kept, _ = lax.optimization_barrier((kept, copies))
    mine, theirs = call(
        gather_grads_kernel,
        (shaped((TOK, 3 * HALF), bf16), shaped((TOK, 3 * HALF), bf16)),
        (at, query_grad, kept, back),
        name="gather_grads",
    )
    received = swapped(theirs, "c")
    query_out, key_out, value_out = call(
        whole_width_kernel,
        tuple(shaped((1, TOK, HW), bf16) for _ in range(3)),
        (at, mine, received),
        name="whole_width",
    )
    half_slot, query_out, key_out, value_out = lax.optimization_barrier(
        (half_slot, query_out, key_out, value_out)
    )
    half_slot_c = swapped(half_slot, "c")

    new_statistics, update_rows = call(
        newton_kernel,
        (shaped((1, 2, ROWS, BLK), f32), shaped((NBLK, ROWS, BLK), bf16)),
        (at, half_slot, half_slot_c, statistics),
        scratch=(
            pltpu.VMEM((BLK, BLK), bf16),
            pltpu.VMEM((2, BLK, BLK), bf16),
            pltpu.VMEM((BLK, BLK), f32),
            pltpu.VMEM((BLK, BLK), f32),
        ),
        flops=2 * BLK**3 * 5,
        nbytes=4 * 2**20,
        name="newton",
    )
    slots = lax.all_to_all(update_rows, REP, 0, 0, tiled=True)
    update = call(
        order_kernel,
        shaped((NBLK, ROWS, BLK), bf16),
        (owners, slots),
        scratch=(
            pltpu.VMEM((NBLK, ROWS, BLK), bf16),
            pltpu.SemaphoreType.DMA((NBLK,)),
            pltpu.SemaphoreType.DMA((NBLK,)),
        ),
        name="order",
        manual=True,
    )
    return query_out, key_out, value_out, new_statistics, update


def solution(mesh):
    split = Mesh(mesh.devices.reshape(2, 4, 2, 2, 4), ("zl", "y", "c", "zh", "x"))
    tokens = P(REP, SEQ, None)
    return jax.shard_map(
        local,
        mesh=split,
        in_specs=(
            tokens, tokens, tokens, tokens, P(REP, SEQ), P(), P(), P(REP, None, SEQ, None),
        ),
        out_specs=(tokens, tokens, tokens, P(REP, None, SEQ, None), P(None, SEQ, None)),
        check_vma=False,
    )
```

```python
import functools

import jax
import jax.numpy as jnp
from jax import lax
from jax.experimental import pallas as pl
from jax.experimental.pallas import tpu as pltpu
from jax.sharding import Mesh, PartitionSpec as P

D = 2048
HD = 128
HW = 1024
TOK = 128
BLK = 512
NBLK = 8
HALF = HW // 2
PAIR = 2 * TOK
QTR = 256
KVW = 2 * HALF + TOK

SEQ = ("zl", "y", "c")
REP = ("zh", "xh", "xl")
OUTER = ("zl", "y", "zh", "xh")
PLANE = ("zl", "y")
N_SEQ = 16
N_PLANE = 8
N_SIDE = NBLK // 2
N_OUTER = N_PLANE * N_SIDE
ROWS = BLK // N_SEQ

masked_score = -1e30
decay_rate = 0.9
step_scale = 16.0
head_scale = HD ** (-0.5)
weight_scale = 1.0 / 16384.0

f32 = jnp.float32
bf16 = jnp.bfloat16
MIB = 1024 * 1024
ANYWHERE = pl.BlockSpec(memory_space=pl.ANY)
SCALARS = pl.BlockSpec(memory_space=pltpu.SMEM)


def nt(left, right):
    return lax.dot_general(left, right, (((1,), (1,)), ((), ())), preferred_element_type=f32)


def tn(left, right):
    return lax.dot_general(left, right, (((0,), (0,)), ((), ())), preferred_element_type=f32)


def nn(left, right):
    return lax.dot_general(left, right, (((1,), (0,)), ((), ())), preferred_element_type=f32)


def whole(array):
    zeros = (0,) * len(array.shape)
    return pl.BlockSpec(tuple(array.shape), lambda i: zeros)


def call(body, outs, args, scratch=(), flops=0, nbytes=0, name=None, manual=False, limit=24, at_hbm=(), out_specs=None):
    place = (lambda array: ANYWHERE) if manual else whole
    specs = [
        SCALARS if a.dtype == jnp.int32 and a.ndim == 1 else ANYWHERE if n in at_hbm else place(a)
        for n, a in enumerate(args)
    ]
    return pl.pallas_call(
        body,
        grid=(1,),
        out_shape=outs,
        in_specs=specs,
        out_specs=out_specs or jax.tree.map(place, outs),
        scratch_shapes=list(scratch),
        compiler_params=pltpu.CompilerParams(vmem_limit_bytes=limit * MIB),
        cost_estimate=pl.CostEstimate(flops=flops, bytes_accessed=nbytes, transcendentals=0),
        name=name,
    )(*args)


def far(array):
    return pltpu.with_memory_space_constraint(array, pltpu.HBM)


def shaped(shape, dtype):
    return jax.ShapeDtypeStruct(shape, dtype)


def pick(core, ref, half):
    first = ref[:, half * HALF : half * HALF + QTR]
    second = ref[:, half * HALF + QTR : (half + 1) * HALF]
    return jnp.where(core == 0, first, second)


def pack_kernel(at_ref, key_ref, value_ref, doc_ref, own_ref, other_ref):
    core = at_ref[0]
    docs = jnp.broadcast_to(doc_ref[...].astype(f32), (TOK, TOK)).T.astype(bf16)
    for out_ref, which in ((own_ref, core), (other_ref, 1 - core)):
        for half in range(2):
            out_ref[:, half * QTR : (half + 1) * QTR] = pick(which, key_ref, half)
            out_ref[:, HALF + half * QTR : HALF + (half + 1) * QTR] = pick(which, value_ref, half)
        out_ref[:, 2 * HALF :] = docs


def own_rows(core):
    return pl.ds(pl.multiple_of(core * TOK, TOK), TOK)


def grad_attended_kernel(
    at_ref, query_ref, query_other_ref, grad_ref, grad_other_ref, weight_hbm,
    attended_grad_ref, query_all_ref, grad_all_ref, weight_ref, sems,
):
    core = at_ref[0]
    copies = []
    for half in range(2):
        start = pl.multiple_of(half * HALF + core * QTR, QTR)
        copies.append(pltpu.make_async_copy(
            weight_hbm.at[pl.ds(start, QTR)], weight_ref.at[half], sems.at[half]
        ))
        copies[half].start()
    mine, other = own_rows(core), own_rows(1 - core)
    for half in range(2):
        cols = slice(half * QTR, (half + 1) * QTR)
        query_all_ref[mine, cols] = pick(core, query_ref, half)
        query_all_ref[other, cols] = pick(core, query_other_ref, half)
    grad_all_ref[mine, :] = grad_ref[...]
    grad_all_ref[other, :] = grad_other_ref[...]
    grad_rows = grad_all_ref[...]
    for half in range(2):
        copies[half].wait()
        product = nt(grad_rows, weight_ref[half])
        attended_grad_ref[:, half * QTR : (half + 1) * QTR] = product.astype(bf16)


def place_blocks(core, own_ref, other_ref, before_ref, crossed_ref, all_ref):
    for ref, place in (
        (before_ref, core), (crossed_ref, 1 - core), (own_ref, 2 + core), (other_ref, 3 - core)
    ):
        all_ref[pl.ds(pl.multiple_of(place * TOK, TOK), TOK), :] = ref[...]


def forward_kernel(
    at_ref, query_ref, own_ref, other_ref, before_ref, crossed_ref,
    attended_ref, weights_ref, all_ref,
):
    core, chip = at_ref[0], at_ref[1]
    place_blocks(core, own_ref, other_ref, before_ref, crossed_ref, all_ref)
    doc_cols = [all_ref[b * TOK : (b + 1) * TOK, 2 * HALF :].astype(f32) for b in range(4)]
    doc_row = jnp.concatenate([block.T for block in doc_cols], axis=1)
    query_at = lax.broadcasted_iota(jnp.int32, (TOK, 3 * TOK), 0)
    key_at = lax.broadcasted_iota(jnp.int32, (TOK, 3 * TOK), 1)
    window = (key_at <= query_at + PAIR) & (key_at > query_at)
    for part in range(2):
        same = jnp.concatenate([doc_cols[2 + part]] * 3, axis=1) == doc_row[:, part * TOK : (part + 3) * TOK]
        present = key_at + part * TOK >= jnp.where(chip > 0, 0, PAIR)
        visible = window & same & present
        rows = slice(part * TOK, (part + 1) * TOK)
        keys = slice(part * TOK, (part + 3) * TOK)
        for head in range(4):
            cols = slice(head * HD, (head + 1) * HD)
            value_cols = slice(HALF + head * HD, HALF + (head + 1) * HD)
            scores = nt(query_ref[rows, cols], all_ref[keys, cols]) * head_scale
            scores = jnp.where(visible, scores, masked_score)
            row_max = jnp.max(scores, axis=1, keepdims=True)
            grown = jnp.exp(scores - row_max)
            total = jnp.sum(grown, axis=1, keepdims=True)
            weights = (grown * (1.0 / total)).astype(bf16)
            weights_ref[head, part] = weights
            attended_ref[rows, cols] = nn(weights, all_ref[keys, value_cols]).astype(bf16)


def weight_grad_kernel(
    at_ref, owner_ref, attended_ref, attended_pair_ref, grad_ref, grad_pair_ref, grad_pair_c_ref,
    terms_hbm, turned_ref, pair_ref, terms_ref, sems,
):
    core, side = at_ref[0], at_ref[2]
    for half in range(2):
        cols = slice(half * QTR, (half + 1) * QTR)
        turned_ref[cols, :PAIR] = attended_ref[:, cols].astype(f32).T.astype(bf16)
        turned_ref[cols, PAIR:] = attended_pair_ref[:, cols].astype(f32).T.astype(bf16)
    pair_ref[:PAIR] = grad_ref[...]
    for ref, c in ((grad_pair_ref, core), (grad_pair_c_ref, 1 - core)):
        pair_ref[pl.ds(pl.multiple_of(PAIR + c * TOK, TOK), TOK), :] = ref[...]
    for block in range(NBLK):
        i, j = divmod(block, 4)
        slot = owner_ref[block]

        @pl.when(slot % 2 == side)
        def _():
            rows = turned_ref[i * QTR : (i + 1) * QTR, :]
            term = (nn(rows, pair_ref[:, j * BLK : (j + 1) * BLK]) * weight_scale).astype(bf16)
            place = slot // 2
            terms_ref[place] = term.reshape(N_PLANE, ROWS, BLK)
            pltpu.make_async_copy(
                terms_ref.at[place], terms_hbm.at[:, place], sems.at[place]
            ).start()

    for place in range(N_SIDE):
        pltpu.make_async_copy(terms_ref.at[place], terms_hbm.at[:, place], sems.at[place]).wait()


def backward_kernel(
    at_ref, weights_ref, query_ref, grad_ref, own_ref, other_ref, before_ref, crossed_ref,
    query_out_ref, sent_ref, kept_ref, all_ref, sum_ref,
):
    core = at_ref[0]
    place_blocks(core, own_ref, other_ref, before_ref, crossed_ref, all_ref)
    sum_ref[...] = jnp.zeros_like(sum_ref)
    for part in range(2):
        rows = slice(part * TOK, (part + 1) * TOK)
        keys = slice(part * TOK, (part + 3) * TOK)
        for head in range(4):
            cols = slice(head * HD, (head + 1) * HD)
            value_cols = slice(HALF + head * HD, HALF + (head + 1) * HD)
            low = weights_ref[head, part]
            weights = low.astype(f32)
            grad_head = grad_ref[rows, cols]
            query_head = query_ref[rows, cols]
            grad_weights = nt(grad_head, all_ref[keys, value_cols])
            grad_dot = jnp.sum(weights * grad_weights, axis=1, keepdims=True)
            grad_scores = (weights * (grad_weights - grad_dot)).astype(bf16)
            query_out_ref[rows, cols] = (nn(grad_scores, all_ref[keys, cols]) * head_scale).astype(bf16)
            sum_ref[keys, cols] += tn(grad_scores, query_head) * head_scale
            sum_ref[keys, value_cols] += tn(low, grad_head)
    sent_ref[...] = sum_ref[:PAIR].astype(bf16)
    kept_ref[...] = sum_ref[PAIR:]


def gather_grads_kernel(at_ref, query_ref, kept_ref, back_ref, mine_ref, other_ref):
    core = at_ref[0]
    for out_ref, rows in ((mine_ref, own_rows(core)), (other_ref, own_rows(1 - core))):
        out_ref[:, :HALF] = query_ref[rows, :]
        out_ref[:, HALF:] = (kept_ref[rows, :] + back_ref[rows, :].astype(f32)).astype(bf16)


def whole_width_kernel(at_ref, mine_ref, other_ref, query_ref, key_ref, value_ref):
    core = at_ref[0]
    for n, out_ref in enumerate((query_ref, key_ref, value_ref)):
        for half in range(2):
            cols = slice(n * HALF + half * QTR, n * HALF + (half + 1) * QTR)
            mine, other = mine_ref[:, cols], other_ref[:, cols]
            out_ref[0, :, half * HALF : half * HALF + QTR] = jnp.where(core == 0, mine, other)
            out_ref[0, :, half * HALF + QTR : (half + 1) * HALF] = jnp.where(core == 0, other, mine)


def sum_parts_kernel(parts_ref, stats_ref, total_ref):
    total = parts_ref[0].astype(f32)
    for n in range(1, N_OUTER):
        total = total + parts_ref[n].astype(f32)
    total_low = total.astype(bf16)
    for n in range(N_PLANE):
        total_ref[n, :ROWS] = total_low
        total_ref[n, ROWS : 2 * ROWS] = stats_ref[0]
        total_ref[n, 2 * ROWS :] = stats_ref[1]


def newton_kernel(
    at_ref, half_ref, half_c_ref, stat_rows_hbm,
    new_rows_ref, update_ref, slot_ref, stats_ref, left_ref, right_ref, stat_rows_ref, sem,
):
    core, row_first = at_ref[0], at_ref[3]
    arrival = pltpu.make_async_copy(stat_rows_hbm, stat_rows_ref, sem)
    arrival.start()
    for ref, c in ((half_ref, core), (half_c_ref, 1 - core)):
        for n in range(N_PLANE):
            rows = pl.ds(pl.multiple_of(c * QTR + n * ROWS, ROWS), ROWS)
            slot_ref[rows, :] = ref[n, :ROWS]
            rows = pl.ds(pl.multiple_of((2 * n + c) * ROWS, ROWS), ROWS)
            stats_ref[0, rows, :] = ref[n, ROWS : 2 * ROWS]
            stats_ref[1, rows, :] = ref[n, 2 * ROWS :]
    slot = slot_ref[...]
    own = pl.ds(pl.multiple_of(row_first, ROWS), ROWS)
    left_ref[...] = nt(slot, slot)
    right_ref[...] = tn(slot, slot)
    new_rows_ref[0, 0] = left_ref[own, :]
    new_rows_ref[0, 1] = right_ref[own, :]
    left = decay_rate * stats_ref[0].astype(f32) + left_ref[...]
    right = decay_rate * stats_ref[1].astype(f32) + right_ref[...]

    def scaled(stat):
        norm_square = jnp.sum(jnp.sum(stat * stat, axis=0, keepdims=True), axis=1, keepdims=True)
        matrix = stat * lax.rsqrt(norm_square)
        low_matrix = matrix.astype(bf16)
        step = (nn(low_matrix, low_matrix) - 10.0 * matrix).astype(bf16)
        return matrix, low_matrix, step, jnp.exp(-0.125 * jnp.log(norm_square))

    left_matrix, left_low, left_step, left_scale = scaled(left)
    right_matrix, right_low, right_step, right_scale = scaled(right)
    left_ref[...] = left_matrix
    identity_rows = jnp.where(
        lax.broadcasted_iota(jnp.int32, (ROWS, BLK), 0) + row_first
        == lax.broadcasted_iota(jnp.int32, (ROWS, BLK), 1),
        1.0,
        0.0,
    )

    def rooted(factor, low_matrix, step):
        square = (25.0 * factor + nn(factor.astype(bf16), step)) * 0.0625
        fourth = (25.0 * square + nn(square.astype(bf16), step)) * 0.0625
        return (5.0 * factor - nn(fourth.astype(bf16), low_matrix)) * 0.25

    left_factor = (5.0 * identity_rows - left_ref[own, :]) * 0.25
    left_rows = rooted(left_factor, left_low, left_step)
    moved = nn(left_rows.astype(bf16), slot)
    right_factor = (5.0 * moved - nn(moved.astype(bf16), right_low)) * 0.25
    update = rooted(right_factor, right_low, right_step) * (step_scale * left_scale * right_scale)
    update_low = update.astype(bf16)
    for n in range(NBLK):
        update_ref[n] = update_low
    arrival.wait()
    new_rows_ref[...] += decay_rate * stat_rows_ref[...]


def order_kernel(owner_ref, slots_ref, blocks_ref):
    for block in range(NBLK):
        blocks_ref[block] = slots_ref[owner_ref[block]]


def swapped(block, axis, mask=1):
    n = lax.axis_size(axis)
    return lax.ppermute(block, axis, [(i, i ^ mask) for i in range(n)])


def local(query_states, key_states, value_states, grad_out, doc_ids, out_weight, owners, statistics):
    core, side = lax.axis_index("c"), lax.axis_index("xl")
    chip = lax.axis_index(PLANE)
    at = jnp.stack([core, chip, side, (chip * 2 + core) * ROWS]).astype(jnp.int32)
    query, key, value, grad = query_states[0], key_states[0], value_states[0], grad_out[0]

    own, other = call(
        pack_kernel,
        (shaped((TOK, KVW), bf16), shaped((TOK, KVW), bf16)),
        (at, key, value, doc_ids),
        name="pack",
        limit=60,
    )
    before = lax.ppermute(own, SEQ, [(i, i + 2) for i in range(N_SEQ - 2)])
    crossed = lax.ppermute(other, SEQ, [(i, (i ^ 1) + 2) for i in range(N_SEQ - 2)])
    query, grad, own, other = lax.optimization_barrier((query, grad, own, other))
    partner = swapped(other, "c")
    query_partner = swapped(query, "c")
    grad_partner = swapped(grad, "c")
    stats_low = statistics[0].astype(bf16)
    grad_pair = swapped(grad, "xl")
    attended_grad, query_all, grad_all = call(
        grad_attended_kernel,
        (shaped((PAIR, HALF), bf16), shaped((PAIR, HALF), bf16), shaped((PAIR, D), bf16)),
        (at, query, query_partner, grad, grad_partner, far(out_weight)),
        flops=2 * PAIR * HALF * D,
        nbytes=8 * MIB,
        scratch=(pltpu.VMEM((2, QTR, D), bf16), pltpu.SemaphoreType.DMA((2,))),
        name="grad_attended",
        at_hbm=(5,),
    )
    attended, weights = call(
        forward_kernel,
        (shaped((PAIR, HALF), bf16), shaped((4, 2, TOK, 3 * TOK), bf16)),
        (at, query_all, own, partner, before, crossed),
        scratch=(pltpu.VMEM((2 * PAIR, KVW), bf16),),
        flops=2 * PAIR * HALF * 6 * TOK,
        nbytes=3 * MIB,
        name="forward",
    )
    attended_pair = swapped(attended, "xl")
    grad_pair, stats_low, _ = lax.optimization_barrier((grad_pair, stats_low, attended))
    grad_pair_c = swapped(grad_pair, "c")
    query_grad, sent, kept = call(
        backward_kernel,
        (shaped((PAIR, HALF), bf16), shaped((PAIR, HW), bf16), shaped((PAIR, HW), f32)),
        (at, weights, query_all, attended_grad, own, partner, before, crossed),
        scratch=(pltpu.VMEM((2 * PAIR, KVW), bf16), pltpu.VMEM((2 * PAIR, HW), f32)),
        flops=2 * PAIR * HALF * 4 * 3 * TOK,
        nbytes=6 * MIB,
        name="backward",
    )
    attended_pair, kept, sent = lax.optimization_barrier((attended_pair, kept, sent))
    terms = call(
        weight_grad_kernel,
        shaped((N_PLANE, N_SIDE, ROWS, BLK), bf16),
        (at, owners, attended, attended_pair, grad_all, grad_pair, grad_pair_c),
        scratch=(
            pltpu.VMEM((HALF, 2 * PAIR), bf16),
            pltpu.VMEM((2 * PAIR, D), bf16),
            pltpu.VMEM((N_SIDE, N_PLANE, ROWS, BLK), bf16),
            pltpu.SemaphoreType.DMA((N_SIDE,)),
        ),
        flops=2 * PAIR * HALF * D,
        nbytes=4 * MIB,
        name="weight_grad",
        out_specs=ANYWHERE,
    )
    parts = lax.all_to_all(terms.reshape(N_OUTER, ROWS, BLK), OUTER, 0, 0, tiled=True)
    copies = call(
        sum_parts_kernel,
        shaped((N_PLANE, 3 * ROWS, BLK), bf16),
        (parts, stats_low),
        nbytes=2 * MIB,
        name="sum_outer",
    )
    half_slot = lax.all_to_all(copies, PLANE, 0, 0, tiled=True)
    half_slot_c = swapped(half_slot, "c")
    sent, _ = lax.optimization_barrier((sent, half_slot))
    back = lax.ppermute(sent, SEQ, [(i + 2, i) for i in range(N_SEQ - 2)])

    new_statistics, update_rows = call(
        newton_kernel,
        (shaped((1, 2, ROWS, BLK), f32), shaped((NBLK, ROWS, BLK), bf16)),
        (at, half_slot, half_slot_c, far(statistics)),
        scratch=(
            pltpu.VMEM((BLK, BLK), bf16),
            pltpu.VMEM((2, BLK, BLK), bf16),
            pltpu.VMEM((BLK, BLK), f32),
            pltpu.VMEM((BLK, BLK), f32),
            pltpu.VMEM((1, 2, ROWS, BLK), f32),
            pltpu.SemaphoreType.DMA,
        ),
        flops=2 * BLK**3 * 5,
        nbytes=4 * MIB,
        name="newton",
        at_hbm=(3,),
    )
    slots = lax.all_to_all(update_rows, REP, 0, 0, tiled=True)
    kept, _ = lax.optimization_barrier((kept, slots))
    mine, theirs = call(
        gather_grads_kernel,
        (shaped((TOK, 3 * HALF), bf16), shaped((TOK, 3 * HALF), bf16)),
        (at, query_grad, kept, back),
        name="gather_grads",
    )
    received = swapped(theirs, "c")
    query_out, key_out, value_out = call(
        whole_width_kernel,
        tuple(shaped((1, TOK, HW), bf16) for _ in range(3)),
        (at, mine, received),
        name="whole_width",
    )
    update = call(order_kernel, shaped((NBLK, ROWS, BLK), bf16), (owners, slots), name="order")
    return query_out, key_out, value_out, new_statistics, update


def solution(mesh):
    split = Mesh(mesh.devices.reshape(2, 4, 2, 2, 2, 2), ("zl", "y", "c", "zh", "xh", "xl"))
    tokens = P(REP, SEQ, None)
    return jax.shard_map(
        local,
        mesh=split,
        in_specs=(
            tokens, tokens, tokens, tokens, P(REP, SEQ), P(), P(), P(REP, None, SEQ, None),
        ),
        out_specs=(tokens, tokens, tokens, P(REP, None, SEQ, None), P(None, SEQ, None)),
        check_vma=False,
    )
```

```python
import functools

import jax
import jax.numpy as jnp
from jax import lax
from jax.experimental import pallas as pl
from jax.experimental.pallas import tpu as pltpu
from jax.sharding import Mesh, PartitionSpec as P

D = 2048
HD = 128
HW = 1024
TOK = 128
BLK = 512
NBLK = 8
HALF = HW // 2
PAIR = 2 * TOK
QTR = 256
KVW = 2 * HALF + TOK

SEQ = ("zl", "y", "c")
REP = ("zh", "xh", "xl")
OUTER = ("zl", "y", "zh", "xh")
PLANE = ("zl", "y")
N_SEQ = 16
N_PLANE = 8
N_SIDE = NBLK // 2
N_OUTER = N_PLANE * N_SIDE
ROWS = BLK // N_SEQ

masked_score = -1e30
decay_rate = 0.9
step_scale = 16.0
head_scale = HD ** (-0.5)
weight_scale = 1.0 / 16384.0

f32 = jnp.float32
bf16 = jnp.bfloat16
MIB = 1024 * 1024
ANYWHERE = pl.BlockSpec(memory_space=pl.ANY)
SCALARS = pl.BlockSpec(memory_space=pltpu.SMEM)


def nt(left, right):
    return lax.dot_general(left, right, (((1,), (1,)), ((), ())), preferred_element_type=f32)


def tn(left, right):
    return lax.dot_general(left, right, (((0,), (0,)), ((), ())), preferred_element_type=f32)


def nn(left, right):
    return lax.dot_general(left, right, (((1,), (0,)), ((), ())), preferred_element_type=f32)


def whole(array):
    zeros = (0,) * len(array.shape)
    return pl.BlockSpec(tuple(array.shape), lambda i: zeros)


def call(body, outs, args, scratch=(), flops=0, nbytes=0, name=None, manual=False, limit=24, at_hbm=(), out_specs=None):
    place = (lambda array: ANYWHERE) if manual else whole
    specs = [
        SCALARS if a.dtype == jnp.int32 and a.ndim == 1 else ANYWHERE if n in at_hbm else place(a)
        for n, a in enumerate(args)
    ]
    return pl.pallas_call(
        body,
        grid=(1,),
        out_shape=outs,
        in_specs=specs,
        out_specs=out_specs or jax.tree.map(place, outs),
        scratch_shapes=list(scratch),
        compiler_params=pltpu.CompilerParams(vmem_limit_bytes=limit * MIB),
        cost_estimate=pl.CostEstimate(flops=flops, bytes_accessed=nbytes, transcendentals=0),
        name=name,
    )(*args)


def far(array):
    return pltpu.with_memory_space_constraint(array, pltpu.HBM)


def shaped(shape, dtype):
    return jax.ShapeDtypeStruct(shape, dtype)


def pick(core, ref, half):
    first = ref[:, half * HALF : half * HALF + QTR]
    second = ref[:, half * HALF + QTR : (half + 1) * HALF]
    return jnp.where(core == 0, first, second)


def pack_kernel(key_hbm, value_hbm, doc_hbm, own_ref, other_ref, doc_ref, sems, doc_sem):
    core = lax.axis_index("c")
    doc_copy = pltpu.make_async_copy(doc_hbm, doc_ref, doc_sem)
    doc_copy.start()
    copies = []
    for out_ref, which in ((own_ref, core), (other_ref, 1 - core)):
        for n, hbm in enumerate((key_hbm, value_hbm)):
            for half in range(2):
                start = pl.multiple_of(half * HALF + which * QTR, QTR)
                place = n * HALF + half * QTR
                copies.append(pltpu.make_async_copy(
                    hbm.at[:, pl.ds(start, QTR)],
                    out_ref.at[:, pl.ds(place, QTR)],
                    sems.at[len(copies)],
                ))
                copies[-1].start()
    doc_copy.wait()
    docs = jnp.broadcast_to(doc_ref[...].astype(f32), (TOK, TOK)).T.astype(bf16)
    own_ref[:, 2 * HALF :] = docs
    other_ref[:, 2 * HALF :] = docs
    for copy in copies:
        copy.wait()


def own_rows(core):
    return pl.ds(pl.multiple_of(core * TOK, TOK), TOK)


def grad_attended_kernel(
    at_ref, query_ref, query_other_ref, grad_ref, grad_other_ref, weight_hbm,
    attended_grad_ref, query_all_ref, grad_all_ref, weight_ref, sems,
):
    core = at_ref[0]
    copies = []
    for half in range(2):
        start = pl.multiple_of(half * HALF + core * QTR, QTR)
        copies.append(pltpu.make_async_copy(
            weight_hbm.at[pl.ds(start, QTR)], weight_ref.at[half], sems.at[half]
        ))
        copies[half].start()
    mine, other = own_rows(core), own_rows(1 - core)
    for half in range(2):
        cols = slice(half * QTR, (half + 1) * QTR)
        query_all_ref[mine, cols] = pick(core, query_ref, half)
        query_all_ref[other, cols] = pick(core, query_other_ref, half)
    grad_all_ref[mine, :] = grad_ref[...]
    grad_all_ref[other, :] = grad_other_ref[...]
    grad_rows = grad_all_ref[...]
    for half in range(2):
        copies[half].wait()
        product = nt(grad_rows, weight_ref[half])
        attended_grad_ref[:, half * QTR : (half + 1) * QTR] = product.astype(bf16)


def place_blocks(core, own_ref, other_ref, before_ref, crossed_ref, all_ref):
    for ref, place in (
        (before_ref, core), (crossed_ref, 1 - core), (own_ref, 2 + core), (other_ref, 3 - core)
    ):
        all_ref[pl.ds(pl.multiple_of(place * TOK, TOK), TOK), :] = ref[...]


def forward_kernel(
    part, at_ref, query_ref, own_ref, other_ref, before_ref, crossed_ref,
    attended_ref, weights_ref, all_ref,
):
    core, chip = at_ref[0], at_ref[1]
    place_blocks(core, own_ref, other_ref, before_ref, crossed_ref, all_ref)
    doc_cols = [all_ref[b * TOK : (b + 1) * TOK, 2 * HALF :].astype(f32) for b in range(4)]
    doc_row = jnp.concatenate([block.T for block in doc_cols], axis=1)
    query_at = lax.broadcasted_iota(jnp.int32, (TOK, 3 * TOK), 0)
    key_at = lax.broadcasted_iota(jnp.int32, (TOK, 3 * TOK), 1)
    window = (key_at <= query_at + PAIR) & (key_at > query_at)
    same = jnp.concatenate([doc_cols[2 + part]] * 3, axis=1) == doc_row[:, part * TOK : (part + 3) * TOK]
    present = key_at + part * TOK >= jnp.where(chip > 0, 0, PAIR)
    visible = window & same & present
    rows = slice(part * TOK, (part + 1) * TOK)
    keys = slice(part * TOK, (part + 3) * TOK)
    for head in range(4):
        cols = slice(head * HD, (head + 1) * HD)
        value_cols = slice(HALF + head * HD, HALF + (head + 1) * HD)
        scores = nt(query_ref[rows, cols], all_ref[keys, cols]) * head_scale
        scores = jnp.where(visible, scores, masked_score)
        row_max = jnp.max(scores, axis=1, keepdims=True)
        grown = jnp.exp(scores - row_max)
        total = jnp.sum(grown, axis=1, keepdims=True)
        weights = (grown * (1.0 / total)).astype(bf16)
        weights_ref[head] = weights
        attended_ref[:, cols] = nn(weights, all_ref[keys, value_cols]).astype(bf16)


def weight_grad_kernel(
    at_ref, owner_ref, first_ref, second_ref, first_pair_ref, second_pair_ref, grad_ref, grad_pair_ref, grad_pair_c_ref,
    terms_hbm, turned_ref, pair_ref, terms_ref, sems,
):
    core, side = at_ref[0], at_ref[2]
    for half in range(2):
        cols = slice(half * QTR, (half + 1) * QTR)
        for n, ref in enumerate((first_ref, second_ref, first_pair_ref, second_pair_ref)):
            tokens = slice(n * TOK, (n + 1) * TOK)
            turned_ref[cols, tokens] = ref[:, cols].astype(f32).T.astype(bf16)
    pair_ref[:PAIR] = grad_ref[...]
    for ref, c in ((grad_pair_ref, core), (grad_pair_c_ref, 1 - core)):
        pair_ref[pl.ds(pl.multiple_of(PAIR + c * TOK, TOK), TOK), :] = ref[...]
    for block in range(NBLK):
        i, j = divmod(block, 4)
        slot = owner_ref[block]

        @pl.when(slot % 2 == side)
        def _():
            rows = turned_ref[i * QTR : (i + 1) * QTR, :]
            term = (nn(rows, pair_ref[:, j * BLK : (j + 1) * BLK]) * weight_scale).astype(bf16)
            place = slot // 2
            terms_ref[place] = term.reshape(N_PLANE, ROWS, BLK)
            pltpu.make_async_copy(
                terms_ref.at[place], terms_hbm.at[:, place], sems.at[place]
            ).start()

    for place in range(N_SIDE):
        pltpu.make_async_copy(terms_ref.at[place], terms_hbm.at[:, place], sems.at[place]).wait()


def backward_kernel(
    at_ref, first_ref, second_ref, query_ref, grad_ref,
    own_ref, other_ref, before_ref, crossed_ref, query_out_ref, sent_ref, kept_ref, all_ref, sum_ref,
):
    core = at_ref[0]
    place_blocks(core, own_ref, other_ref, before_ref, crossed_ref, all_ref)
    sum_ref[...] = jnp.zeros_like(sum_ref)
    for part in range(2):
        rows = slice(part * TOK, (part + 1) * TOK)
        keys = slice(part * TOK, (part + 3) * TOK)
        for head in range(4):
            cols = slice(head * HD, (head + 1) * HD)
            value_cols = slice(HALF + head * HD, HALF + (head + 1) * HD)
            low = (first_ref, second_ref)[part][head]
            weights = low.astype(f32)
            grad_head = grad_ref[rows, cols]
            query_head = query_ref[rows, cols]
            grad_weights = nt(grad_head, all_ref[keys, value_cols])
            grad_dot = jnp.sum(weights * grad_weights, axis=1, keepdims=True)
            grad_scores = (weights * (grad_weights - grad_dot)).astype(bf16)
            query_out_ref[rows, cols] = (nn(grad_scores, all_ref[keys, cols]) * head_scale).astype(bf16)
            sum_ref[keys, cols] += tn(grad_scores, query_head) * head_scale
            sum_ref[keys, value_cols] += tn(low, grad_head)
    sent_ref[...] = sum_ref[:PAIR].astype(bf16)
    kept_ref[...] = sum_ref[PAIR:]


def gather_grads_kernel(at_ref, query_ref, kept_ref, back_ref, mine_ref, other_ref):
    core = at_ref[0]
    for out_ref, rows in ((mine_ref, own_rows(core)), (other_ref, own_rows(1 - core))):
        out_ref[:, :HALF] = query_ref[rows, :]
        out_ref[:, HALF:] = (kept_ref[rows, :] + back_ref[rows, :].astype(f32)).astype(bf16)


def whole_width_kernel(at_ref, mine_ref, other_ref, query_ref, key_ref, value_ref):
    core = at_ref[0]
    for n, out_ref in enumerate((query_ref, key_ref, value_ref)):
        for half in range(2):
            cols = slice(n * HALF + half * QTR, n * HALF + (half + 1) * QTR)
            mine, other = mine_ref[:, cols], other_ref[:, cols]
            out_ref[0, :, half * HALF : half * HALF + QTR] = jnp.where(core == 0, mine, other)
            out_ref[0, :, half * HALF + QTR : (half + 1) * HALF] = jnp.where(core == 0, other, mine)


def sum_parts_kernel(parts_ref, stats_ref, total_ref):
    total = parts_ref[0].astype(f32)
    for n in range(1, N_OUTER):
        total = total + parts_ref[n].astype(f32)
    total_low = total.astype(bf16)
    for n in range(N_PLANE):
        total_ref[n, :ROWS] = total_low
        total_ref[n, ROWS : 2 * ROWS] = stats_ref[0]
        total_ref[n, 2 * ROWS :] = stats_ref[1]


def newton_kernel(
    at_ref, half_ref, half_c_ref, stat_rows_hbm,
    new_rows_ref, update_ref, slot_ref, stats_ref, left_ref, right_ref, stat_rows_ref, sem,
):
    core, row_first = at_ref[0], at_ref[3]
    arrival = pltpu.make_async_copy(stat_rows_hbm, stat_rows_ref, sem)
    arrival.start()
    for ref, c in ((half_ref, core), (half_c_ref, 1 - core)):
        for n in range(N_PLANE):
            rows = pl.ds(pl.multiple_of(c * QTR + n * ROWS, ROWS), ROWS)
            slot_ref[rows, :] = ref[n, :ROWS]
            rows = pl.ds(pl.multiple_of((2 * n + c) * ROWS, ROWS), ROWS)
            stats_ref[0, rows, :] = ref[n, ROWS : 2 * ROWS]
            stats_ref[1, rows, :] = ref[n, 2 * ROWS :]
    slot = slot_ref[...]
    own = pl.ds(pl.multiple_of(row_first, ROWS), ROWS)
    left_ref[...] = nt(slot, slot)
    right_ref[...] = tn(slot, slot)
    new_rows_ref[0, 0] = left_ref[own, :]
    new_rows_ref[0, 1] = right_ref[own, :]
    left = decay_rate * stats_ref[0].astype(f32) + left_ref[...]
    right = decay_rate * stats_ref[1].astype(f32) + right_ref[...]

    def scaled(stat):
        norm_square = jnp.sum(jnp.sum(stat * stat, axis=0, keepdims=True), axis=1, keepdims=True)
        matrix = stat * lax.rsqrt(norm_square)
        low_matrix = matrix.astype(bf16)
        step = (nn(low_matrix, low_matrix) - 10.0 * matrix).astype(bf16)
        return matrix, low_matrix, step, jnp.exp(-0.125 * jnp.log(norm_square))

    left_matrix, left_low, left_step, left_scale = scaled(left)
    right_matrix, right_low, right_step, right_scale = scaled(right)
    left_ref[...] = left_matrix
    identity_rows = jnp.where(
        lax.broadcasted_iota(jnp.int32, (ROWS, BLK), 0) + row_first
        == lax.broadcasted_iota(jnp.int32, (ROWS, BLK), 1),
        1.0,
        0.0,
    )

    def rooted(factor, low_matrix, step):
        square = (25.0 * factor + nn(factor.astype(bf16), step)) * 0.0625
        fourth = (25.0 * square + nn(square.astype(bf16), step)) * 0.0625
        return (5.0 * factor - nn(fourth.astype(bf16), low_matrix)) * 0.25

    left_factor = (5.0 * identity_rows - left_ref[own, :]) * 0.25
    left_rows = rooted(left_factor, left_low, left_step)
    moved = nn(left_rows.astype(bf16), slot)
    right_factor = (5.0 * moved - nn(moved.astype(bf16), right_low)) * 0.25
    update = rooted(right_factor, right_low, right_step) * (step_scale * left_scale * right_scale)
    update_low = update.astype(bf16)
    for n in range(NBLK):
        update_ref[n] = update_low
    arrival.wait()
    new_rows_ref[...] += decay_rate * stat_rows_ref[...]


def order_kernel(owner_ref, slots_ref, blocks_ref):
    for block in range(NBLK):
        blocks_ref[block] = slots_ref[owner_ref[block]]


def swapped(block, axis, mask=1):
    n = lax.axis_size(axis)
    return lax.ppermute(block, axis, [(i, i ^ mask) for i in range(n)])


def local(query_states, key_states, value_states, grad_out, doc_ids, out_weight, owners, statistics):
    core, side = lax.axis_index("c"), lax.axis_index("xl")
    chip = lax.axis_index(PLANE)
    at = jnp.stack([core, chip, side, (chip * 2 + core) * ROWS]).astype(jnp.int32)
    query, key, value, grad = query_states[0], key_states[0], value_states[0], grad_out[0]

    own, other = call(
        pack_kernel,
        (shaped((TOK, KVW), bf16), shaped((TOK, KVW), bf16)),
        (far(key), far(value), far(doc_ids)),
        scratch=(
            pltpu.VMEM((1, TOK), jnp.int32),
            pltpu.SemaphoreType.DMA((8,)),
            pltpu.SemaphoreType.DMA,
        ),
        at_hbm=(0, 1, 2),
        name="pack",
    )
    before = lax.ppermute(own, SEQ, [(i, i + 2) for i in range(N_SEQ - 2)])
    crossed = lax.ppermute(other, SEQ, [(i, (i ^ 1) + 2) for i in range(N_SEQ - 2)])
    query, grad, own, other = lax.optimization_barrier((query, grad, own, other))
    partner = swapped(other, "c")
    query_partner = swapped(query, "c")
    grad_partner = swapped(grad, "c")
    grad_pair = swapped(grad, "xl")
    attended_grad, query_all, grad_all = call(
        grad_attended_kernel,
        (shaped((PAIR, HALF), bf16), shaped((PAIR, HALF), bf16), shaped((PAIR, D), bf16)),
        (at, query, query_partner, grad, grad_partner, far(out_weight)),
        flops=2 * PAIR * HALF * D,
        nbytes=8 * MIB,
        scratch=(pltpu.VMEM((2, QTR, D), bf16), pltpu.SemaphoreType.DMA((2,))),
        name="grad_attended",
        at_hbm=(5,),
    )
    attended, attended_pair, weights = [], [], []
    for part in range(2):
        attended_part, weights_part = call(
            functools.partial(forward_kernel, part),
            (shaped((TOK, HALF), bf16), shaped((4, TOK, 3 * TOK), bf16)),
            (at, query_all, own, partner, before, crossed),
            scratch=(pltpu.VMEM((2 * PAIR, KVW), bf16),),
            flops=PAIR * HALF * 6 * TOK,
            nbytes=2 * MIB,
            name="forward",
        )
        attended.append(attended_part)
        attended_pair.append(swapped(attended_part, "xl"))
        weights.append(weights_part)
    grad_pair, _ = lax.optimization_barrier((grad_pair, attended[1]))
    grad_pair_c = swapped(grad_pair, "c")
    query_grad, sent, kept = call(
        backward_kernel,
        (shaped((PAIR, HALF), bf16), shaped((PAIR, HW), bf16), shaped((PAIR, HW), f32)),
        (at, *weights, query_all, attended_grad, own, partner, before, crossed),
        scratch=(pltpu.VMEM((2 * PAIR, KVW), bf16), pltpu.VMEM((2 * PAIR, HW), f32)),
        flops=2 * PAIR * HALF * 4 * 3 * TOK,
        nbytes=6 * MIB,
        name="backward",
    )
    terms = call(
        weight_grad_kernel,
        shaped((N_PLANE, N_SIDE, ROWS, BLK), bf16),
        (at, owners, *attended, *attended_pair, grad_all, grad_pair, grad_pair_c),
        scratch=(
            pltpu.VMEM((HALF, 2 * PAIR), bf16),
            pltpu.VMEM((2 * PAIR, D), bf16),
            pltpu.VMEM((N_SIDE, N_PLANE, ROWS, BLK), bf16),
            pltpu.SemaphoreType.DMA((N_SIDE,)),
        ),
        flops=2 * PAIR * HALF * D,
        nbytes=4 * MIB,
        name="weight_grad",
        out_specs=ANYWHERE,
    )
    parts = lax.all_to_all(terms.reshape(N_OUTER, ROWS, BLK), OUTER, 0, 0, tiled=True)
    back = lax.ppermute(sent, SEQ, [(i + 2, i) for i in range(N_SEQ - 2)])
    parts, kept = lax.optimization_barrier((parts, kept))
    stats_low, _ = lax.optimization_barrier((statistics[0], query_grad))
    stats_low = stats_low.astype(bf16)
    copies = call(
        sum_parts_kernel,
        shaped((N_PLANE, 3 * ROWS, BLK), bf16),
        (parts, stats_low),
        nbytes=2 * MIB,
        name="sum_outer",
    )
    half_slot = lax.all_to_all(copies, PLANE, 0, 0, tiled=True)
    kept, _ = lax.optimization_barrier((kept, copies))
    mine, theirs = call(
        gather_grads_kernel,
        (shaped((TOK, 3 * HALF), bf16), shaped((TOK, 3 * HALF), bf16)),
        (at, query_grad, kept, back),
        name="gather_grads",
    )
    received = swapped(theirs, "c")
    query_out, key_out, value_out = call(
        whole_width_kernel,
        tuple(shaped((1, TOK, HW), bf16) for _ in range(3)),
        (at, mine, received),
        name="whole_width",
    )
    half_slot, query_out, key_out, value_out = lax.optimization_barrier(
        (half_slot, query_out, key_out, value_out)
    )
    half_slot_c = swapped(half_slot, "c")

    new_statistics, update_rows = call(
        newton_kernel,
        (shaped((1, 2, ROWS, BLK), f32), shaped((NBLK, ROWS, BLK), bf16)),
        (at, half_slot, half_slot_c, far(statistics)),
        scratch=(
            pltpu.VMEM((BLK, BLK), bf16),
            pltpu.VMEM((2, BLK, BLK), bf16),
            pltpu.VMEM((BLK, BLK), f32),
            pltpu.VMEM((BLK, BLK), f32),
            pltpu.VMEM((1, 2, ROWS, BLK), f32),
            pltpu.SemaphoreType.DMA,
        ),
        flops=2 * BLK**3 * 5,
        nbytes=4 * MIB,
        name="newton",
        at_hbm=(3,),
    )
    slots = lax.all_to_all(update_rows, REP, 0, 0, tiled=True)
    update = call(order_kernel, shaped((NBLK, ROWS, BLK), bf16), (owners, slots), name="order")
    return query_out, key_out, value_out, new_statistics, update


def solution(mesh):
    split = Mesh(mesh.devices.reshape(2, 4, 2, 2, 2, 2), ("zl", "y", "c", "zh", "xh", "xl"))
    tokens = P(REP, SEQ, None)
    return jax.shard_map(
        local,
        mesh=split,
        in_specs=(
            tokens, tokens, tokens, tokens, P(REP, SEQ), P(), P(), P(REP, None, SEQ, None),
        ),
        out_specs=(tokens, tokens, tokens, P(REP, None, SEQ, None), P(None, SEQ, None)),
        check_vma=False,
    )
```

```python
import functools

import jax
import jax.numpy as jnp
from jax import lax
from jax.experimental import pallas as pl
from jax.experimental.pallas import tpu as pltpu
from jax.sharding import Mesh, PartitionSpec as P

D = 2048
HD = 128
HW = 1024
TOK = 128
BLK = 512
NBLK = 8
HALF = HW // 2
PAIR = 2 * TOK
QTR = 256
KVW = 2 * HALF + TOK

SEQ = ("zl", "y", "c")
REP = ("zh", "xh", "xl")
OUTER = ("zl", "y", "zh", "xh")
PLANE = ("zl", "y")
N_SEQ = 16
N_PLANE = 8
N_SIDE = NBLK // 2
N_OUTER = N_PLANE * N_SIDE
ROWS = BLK // N_SEQ

masked_score = -1e30
decay_rate = 0.9
step_scale = 16.0
head_scale = HD ** (-0.5)
weight_scale = 1.0 / 16384.0

f32 = jnp.float32
bf16 = jnp.bfloat16
MIB = 1024 * 1024
ANYWHERE = pl.BlockSpec(memory_space=pl.ANY)
SCALARS = pl.BlockSpec(memory_space=pltpu.SMEM)


def nt(left, right):
    return lax.dot_general(left, right, (((1,), (1,)), ((), ())), preferred_element_type=f32)


def tn(left, right):
    return lax.dot_general(left, right, (((0,), (0,)), ((), ())), preferred_element_type=f32)


def nn(left, right):
    return lax.dot_general(left, right, (((1,), (0,)), ((), ())), preferred_element_type=f32)


def whole(array):
    zeros = (0,) * len(array.shape)
    return pl.BlockSpec(tuple(array.shape), lambda i: zeros)


def call(body, outs, args, scratch=(), flops=0, nbytes=0, name=None, manual=False, limit=24, at_hbm=(), out_specs=None):
    place = (lambda array: ANYWHERE) if manual else whole
    specs = [
        SCALARS if a.dtype == jnp.int32 and a.ndim == 1 else ANYWHERE if n in at_hbm else place(a)
        for n, a in enumerate(args)
    ]
    return pl.pallas_call(
        body,
        grid=(1,),
        out_shape=outs,
        in_specs=specs,
        out_specs=out_specs or jax.tree.map(place, outs),
        scratch_shapes=list(scratch),
        compiler_params=pltpu.CompilerParams(vmem_limit_bytes=limit * MIB),
        cost_estimate=pl.CostEstimate(flops=flops, bytes_accessed=nbytes, transcendentals=0),
        name=name,
    )(*args)


def far(array):
    return pltpu.with_memory_space_constraint(array, pltpu.HBM)


def shaped(shape, dtype):
    return jax.ShapeDtypeStruct(shape, dtype)


def pick(core, ref, half):
    first = ref[:, half * HALF : half * HALF + QTR]
    second = ref[:, half * HALF + QTR : (half + 1) * HALF]
    return jnp.where(core == 0, first, second)


def pack_kernel(key_hbm, value_hbm, doc_hbm, own_ref, other_ref, doc_ref, sems, doc_sem):
    core = lax.axis_index("c")
    doc_copy = pltpu.make_async_copy(doc_hbm, doc_ref, doc_sem)
    doc_copy.start()
    copies = []
    for out_ref, which in ((own_ref, core), (other_ref, 1 - core)):
        for n, hbm in enumerate((key_hbm, value_hbm)):
            for half in range(2):
                start = pl.multiple_of(half * HALF + which * QTR, QTR)
                place = n * HALF + half * QTR
                copies.append(pltpu.make_async_copy(
                    hbm.at[:, pl.ds(start, QTR)],
                    out_ref.at[:, pl.ds(place, QTR)],
                    sems.at[len(copies)],
                ))
                copies[-1].start()
    doc_copy.wait()
    docs = jnp.broadcast_to(doc_ref[...].astype(f32), (TOK, TOK)).T.astype(bf16)
    own_ref[:, 2 * HALF :] = docs
    other_ref[:, 2 * HALF :] = docs
    for copy in copies:
        copy.wait()


def own_rows(core):
    return pl.ds(pl.multiple_of(core * TOK, TOK), TOK)


def grad_attended_kernel(
    at_ref, query_ref, query_other_ref, grad_ref, grad_other_ref, weight_hbm,
    attended_grad_ref, query_all_ref, grad_all_ref, weight_ref, sems,
):
    core = at_ref[0]
    copies = []
    for half in range(2):
        start = pl.multiple_of(half * HALF + core * QTR, QTR)
        copies.append(pltpu.make_async_copy(
            weight_hbm.at[pl.ds(start, QTR)], weight_ref.at[half], sems.at[half]
        ))
        copies[half].start()
    mine, other = own_rows(core), own_rows(1 - core)
    for half in range(2):
        cols = slice(half * QTR, (half + 1) * QTR)
        query_all_ref[mine, cols] = pick(core, query_ref, half)
        query_all_ref[other, cols] = pick(core, query_other_ref, half)
    grad_all_ref[mine, :] = grad_ref[...]
    grad_all_ref[other, :] = grad_other_ref[...]
    grad_rows = grad_all_ref[...]
    for half in range(2):
        copies[half].wait()
        product = nt(grad_rows, weight_ref[half])
        attended_grad_ref[:, half * QTR : (half + 1) * QTR] = product.astype(bf16)


def place_blocks(core, own_ref, other_ref, before_ref, crossed_ref, all_ref):
    for ref, place in (
        (before_ref, core), (crossed_ref, 1 - core), (own_ref, 2 + core), (other_ref, 3 - core)
    ):
        all_ref[pl.ds(pl.multiple_of(place * TOK, TOK), TOK), :] = ref[...]


def forward_kernel(
    part, at_ref, query_ref, own_ref, other_ref, before_ref, crossed_ref,
    attended_ref, weights_ref, all_ref,
):
    core, chip = at_ref[0], at_ref[1]
    place_blocks(core, own_ref, other_ref, before_ref, crossed_ref, all_ref)
    doc_cols = [all_ref[b * TOK : (b + 1) * TOK, 2 * HALF :].astype(f32) for b in range(4)]
    doc_row = jnp.concatenate([block.T for block in doc_cols], axis=1)
    query_at = lax.broadcasted_iota(jnp.int32, (TOK, 3 * TOK), 0)
    key_at = lax.broadcasted_iota(jnp.int32, (TOK, 3 * TOK), 1)
    window = (key_at <= query_at + PAIR) & (key_at > query_at)
    same = jnp.concatenate([doc_cols[2 + part]] * 3, axis=1) == doc_row[:, part * TOK : (part + 3) * TOK]
    present = key_at + part * TOK >= jnp.where(chip > 0, 0, PAIR)
    visible = window & same & present
    rows = slice(part * TOK, (part + 1) * TOK)
    keys = slice(part * TOK, (part + 3) * TOK)
    for head in range(4):
        cols = slice(head * HD, (head + 1) * HD)
        value_cols = slice(HALF + head * HD, HALF + (head + 1) * HD)
        scores = nt(query_ref[rows, cols], all_ref[keys, cols]) * head_scale
        scores = jnp.where(visible, scores, masked_score)
        row_max = jnp.max(scores, axis=1, keepdims=True)
        grown = jnp.exp(scores - row_max)
        total = jnp.sum(grown, axis=1, keepdims=True)
        weights = (grown * (1.0 / total)).astype(bf16)
        weights_ref[head] = weights
        attended_ref[:, cols] = nn(weights, all_ref[keys, value_cols]).astype(bf16)


def weight_grad_kernel(
    at_ref, owner_ref, first_ref, second_ref, first_pair_ref, second_pair_ref, grad_ref, grad_pair_ref, grad_pair_c_ref,
    terms_hbm, turned_ref, pair_ref, terms_ref, sems,
):
    core, side = at_ref[0], at_ref[2]
    for half in range(2):
        cols = slice(half * QTR, (half + 1) * QTR)
        for n, ref in enumerate((first_ref, second_ref, first_pair_ref, second_pair_ref)):
            tokens = slice(n * TOK, (n + 1) * TOK)
            turned_ref[cols, tokens] = ref[:, cols].astype(f32).T.astype(bf16)
    pair_ref[:PAIR] = grad_ref[...]
    for ref, c in ((grad_pair_ref, core), (grad_pair_c_ref, 1 - core)):
        pair_ref[pl.ds(pl.multiple_of(PAIR + c * TOK, TOK), TOK), :] = ref[...]
    for block in range(NBLK):
        i, j = divmod(block, 4)
        slot = owner_ref[block]

        @pl.when(slot % 2 == side)
        def _():
            rows = turned_ref[i * QTR : (i + 1) * QTR, :]
            term = (nn(rows, pair_ref[:, j * BLK : (j + 1) * BLK]) * weight_scale).astype(bf16)
            place = slot // 2
            terms_ref[place] = term.reshape(N_PLANE, ROWS, BLK)
            pltpu.make_async_copy(
                terms_ref.at[place], terms_hbm.at[:, place], sems.at[place]
            ).start()

    for place in range(N_SIDE):
        pltpu.make_async_copy(terms_ref.at[place], terms_hbm.at[:, place], sems.at[place]).wait()


def backward_kernel(
    at_ref, first_ref, second_ref, query_ref, grad_ref,
    own_ref, other_ref, before_ref, crossed_ref, query_out_ref, sent_ref, kept_ref, all_ref, sum_ref,
):
    core = at_ref[0]
    place_blocks(core, own_ref, other_ref, before_ref, crossed_ref, all_ref)
    sum_ref[...] = jnp.zeros_like(sum_ref)
    for part in range(2):
        rows = slice(part * TOK, (part + 1) * TOK)
        keys = slice(part * TOK, (part + 3) * TOK)
        for head in range(4):
            cols = slice(head * HD, (head + 1) * HD)
            value_cols = slice(HALF + head * HD, HALF + (head + 1) * HD)
            low = (first_ref, second_ref)[part][head]
            weights = low.astype(f32)
            grad_head = grad_ref[rows, cols]
            query_head = query_ref[rows, cols]
            grad_weights = nt(grad_head, all_ref[keys, value_cols])
            grad_dot = jnp.sum(weights * grad_weights, axis=1, keepdims=True)
            grad_scores = (weights * (grad_weights - grad_dot)).astype(bf16)
            query_out_ref[rows, cols] = (nn(grad_scores, all_ref[keys, cols]) * head_scale).astype(bf16)
            sum_ref[keys, cols] += tn(grad_scores, query_head) * head_scale
            sum_ref[keys, value_cols] += tn(low, grad_head)
    sent_ref[...] = sum_ref[:PAIR].astype(bf16)
    kept_ref[...] = sum_ref[PAIR:]


def gather_grads_kernel(at_ref, query_ref, kept_ref, back_ref, mine_ref, other_ref):
    core = at_ref[0]
    for out_ref, rows in ((mine_ref, own_rows(core)), (other_ref, own_rows(1 - core))):
        out_ref[:, :HALF] = query_ref[rows, :]
        out_ref[:, HALF:] = (kept_ref[rows, :] + back_ref[rows, :].astype(f32)).astype(bf16)


def whole_width_kernel(at_ref, mine_ref, other_ref, query_ref, key_ref, value_ref):
    core = at_ref[0]
    for n, out_ref in enumerate((query_ref, key_ref, value_ref)):
        for half in range(2):
            cols = slice(n * HALF + half * QTR, n * HALF + (half + 1) * QTR)
            mine, other = mine_ref[:, cols], other_ref[:, cols]
            out_ref[0, :, half * HALF : half * HALF + QTR] = jnp.where(core == 0, mine, other)
            out_ref[0, :, half * HALF + QTR : (half + 1) * HALF] = jnp.where(core == 0, other, mine)


def sum_parts_kernel(parts_ref, stats_ref, total_ref):
    total = parts_ref[0].astype(f32)
    for n in range(1, N_OUTER):
        total = total + parts_ref[n].astype(f32)
    total_low = total.astype(bf16)
    for n in range(N_PLANE):
        total_ref[n, :ROWS] = total_low
        total_ref[n, ROWS : 2 * ROWS] = stats_ref[0]
        total_ref[n, 2 * ROWS :] = stats_ref[1]


def newton_kernel(
    at_ref, half_ref, half_c_ref, stat_rows_hbm,
    new_rows_ref, update_ref, slot_ref, stats_ref, left_ref, right_ref, stat_rows_ref, sem,
):
    core, row_first = at_ref[0], at_ref[3]
    arrival = pltpu.make_async_copy(stat_rows_hbm, stat_rows_ref, sem)
    arrival.start()
    for ref, c in ((half_ref, core), (half_c_ref, 1 - core)):
        for n in range(N_PLANE):
            rows = pl.ds(pl.multiple_of(c * QTR + n * ROWS, ROWS), ROWS)
            slot_ref[rows, :] = ref[n, :ROWS]
            rows = pl.ds(pl.multiple_of((2 * n + c) * ROWS, ROWS), ROWS)
            stats_ref[0, rows, :] = ref[n, ROWS : 2 * ROWS]
            stats_ref[1, rows, :] = ref[n, 2 * ROWS :]
    slot = slot_ref[...]
    own = pl.ds(pl.multiple_of(row_first, ROWS), ROWS)
    left_ref[...] = nt(slot, slot)
    right_ref[...] = tn(slot, slot)
    new_rows_ref[0, 0] = left_ref[own, :]
    new_rows_ref[0, 1] = right_ref[own, :]
    left = decay_rate * stats_ref[0].astype(f32) + left_ref[...]
    right = decay_rate * stats_ref[1].astype(f32) + right_ref[...]

    def scaled(stat):
        norm_square = jnp.sum(jnp.sum(stat * stat, axis=0, keepdims=True), axis=1, keepdims=True)
        matrix = stat * lax.rsqrt(norm_square)
        low_matrix = matrix.astype(bf16)
        step = (nn(low_matrix, low_matrix) - 10.0 * matrix).astype(bf16)
        return matrix, low_matrix, step, jnp.exp(-0.125 * jnp.log(norm_square))

    left_matrix, left_low, left_step, left_scale = scaled(left)
    right_matrix, right_low, right_step, right_scale = scaled(right)
    left_ref[...] = left_matrix
    identity_rows = jnp.where(
        lax.broadcasted_iota(jnp.int32, (ROWS, BLK), 0) + row_first
        == lax.broadcasted_iota(jnp.int32, (ROWS, BLK), 1),
        1.0,
        0.0,
    )

    def rooted(factor, low_matrix, step):
        square = (25.0 * factor + nn(factor.astype(bf16), step)) * 0.0625
        fourth = (25.0 * square + nn(square.astype(bf16), step)) * 0.0625
        return (5.0 * factor - nn(fourth.astype(bf16), low_matrix)) * 0.25

    left_factor = (5.0 * identity_rows - left_ref[own, :]) * 0.25
    left_rows = rooted(left_factor, left_low, left_step)
    moved = nn(left_rows.astype(bf16), slot)
    right_factor = (5.0 * moved - nn(moved.astype(bf16), right_low)) * 0.25
    update = rooted(right_factor, right_low, right_step) * (step_scale * left_scale * right_scale)
    update_low = update.astype(bf16)
    for n in range(NBLK):
        update_ref[n] = update_low
    arrival.wait()
    new_rows_ref[...] += decay_rate * stat_rows_ref[...]


def order_kernel(owner_ref, slots_ref, blocks_ref):
    for block in range(NBLK):
        blocks_ref[block] = slots_ref[owner_ref[block]]


def swapped(block, axis, mask=1):
    n = lax.axis_size(axis)
    return lax.ppermute(block, axis, [(i, i ^ mask) for i in range(n)])


def local(query_states, key_states, value_states, grad_out, doc_ids, out_weight, owners, statistics):
    core, side = lax.axis_index("c"), lax.axis_index("xl")
    chip = lax.axis_index(PLANE)
    at = jnp.stack([core, chip, side, (chip * 2 + core) * ROWS]).astype(jnp.int32)
    query, key, value, grad = query_states[0], key_states[0], value_states[0], grad_out[0]

    own, other = call(
        pack_kernel,
        (shaped((TOK, KVW), bf16), shaped((TOK, KVW), bf16)),
        (far(key), far(value), far(doc_ids)),
        scratch=(
            pltpu.VMEM((1, TOK), jnp.int32),
            pltpu.SemaphoreType.DMA((8,)),
            pltpu.SemaphoreType.DMA,
        ),
        at_hbm=(0, 1, 2),
        name="pack",
    )
    before = lax.ppermute(own, SEQ, [(i, i + 2) for i in range(N_SEQ - 2)])
    crossed = lax.ppermute(other, SEQ, [(i, (i ^ 1) + 2) for i in range(N_SEQ - 2)])
    query, grad, own, other = lax.optimization_barrier((query, grad, own, other))
    partner = swapped(other, "c")
    query_partner = swapped(query, "c")
    grad_partner = swapped(grad, "c")
    grad_pair = swapped(grad, "xl")
    attended_grad, query_all, grad_all = call(
        grad_attended_kernel,
        (shaped((PAIR, HALF), bf16), shaped((PAIR, HALF), bf16), shaped((PAIR, D), bf16)),
        (at, query, query_partner, grad, grad_partner, far(out_weight)),
        flops=2 * PAIR * HALF * D,
        nbytes=8 * MIB,
        scratch=(pltpu.VMEM((2, QTR, D), bf16), pltpu.SemaphoreType.DMA((2,))),
        name="grad_attended",
        at_hbm=(5,),
    )
    attended, attended_pair, weights = [], [], []
    for part in range(2):
        attended_part, weights_part = call(
            functools.partial(forward_kernel, part),
            (shaped((TOK, HALF), bf16), shaped((4, TOK, 3 * TOK), bf16)),
            (at, query_all, own, partner, before, crossed),
            scratch=(pltpu.VMEM((2 * PAIR, KVW), bf16),),
            flops=PAIR * HALF * 6 * TOK,
            nbytes=2 * MIB,
            name="forward",
        )
        attended.append(attended_part)
        attended_pair.append(swapped(attended_part, "xl"))
        weights.append(weights_part)
    grad_pair, _ = lax.optimization_barrier((grad_pair, attended[1]))
    grad_pair_c = swapped(grad_pair, "c")
    query_grad, sent, kept = call(
        backward_kernel,
        (shaped((PAIR, HALF), bf16), shaped((PAIR, HW), bf16), shaped((PAIR, HW), f32)),
        (at, *weights, query_all, attended_grad, own, partner, before, crossed),
        scratch=(pltpu.VMEM((2 * PAIR, KVW), bf16), pltpu.VMEM((2 * PAIR, HW), f32)),
        flops=2 * PAIR * HALF * 4 * 3 * TOK,
        nbytes=6 * MIB,
        name="backward",
    )
    stats_low, _ = lax.optimization_barrier((statistics[0], attended[1]))
    stats_low = stats_low.astype(bf16)
    *attended_pair, kept, sent, stats_low = lax.optimization_barrier(
        (*attended_pair, kept, sent, stats_low)
    )
    terms = call(
        weight_grad_kernel,
        shaped((N_PLANE, N_SIDE, ROWS, BLK), bf16),
        (at, owners, *attended, *attended_pair, grad_all, grad_pair, grad_pair_c),
        scratch=(
            pltpu.VMEM((HALF, 2 * PAIR), bf16),
            pltpu.VMEM((2 * PAIR, D), bf16),
            pltpu.VMEM((N_SIDE, N_PLANE, ROWS, BLK), bf16),
            pltpu.SemaphoreType.DMA((N_SIDE,)),
        ),
        flops=2 * PAIR * HALF * D,
        nbytes=4 * MIB,
        name="weight_grad",
        out_specs=ANYWHERE,
    )
    parts = lax.all_to_all(terms.reshape(N_OUTER, ROWS, BLK), OUTER, 0, 0, tiled=True)
    copies = call(
        sum_parts_kernel,
        shaped((N_PLANE, 3 * ROWS, BLK), bf16),
        (parts, stats_low),
        nbytes=2 * MIB,
        name="sum_outer",
    )
    half_slot = lax.all_to_all(copies, PLANE, 0, 0, tiled=True)
    half_slot_c = swapped(half_slot, "c")
    sent, _ = lax.optimization_barrier((sent, half_slot))
    back = lax.ppermute(sent, SEQ, [(i + 2, i) for i in range(N_SEQ - 2)])

    new_statistics, update_rows = call(
        newton_kernel,
        (shaped((1, 2, ROWS, BLK), f32), shaped((NBLK, ROWS, BLK), bf16)),
        (at, half_slot, half_slot_c, far(statistics)),
        scratch=(
            pltpu.VMEM((BLK, BLK), bf16),
            pltpu.VMEM((2, BLK, BLK), bf16),
            pltpu.VMEM((BLK, BLK), f32),
            pltpu.VMEM((BLK, BLK), f32),
            pltpu.VMEM((1, 2, ROWS, BLK), f32),
            pltpu.SemaphoreType.DMA,
        ),
        flops=2 * BLK**3 * 5,
        nbytes=4 * MIB,
        name="newton",
        at_hbm=(3,),
    )
    slots = lax.all_to_all(update_rows, REP, 0, 0, tiled=True)
    kept, _ = lax.optimization_barrier((kept, slots))
    mine, theirs = call(
        gather_grads_kernel,
        (shaped((TOK, 3 * HALF), bf16), shaped((TOK, 3 * HALF), bf16)),
        (at, query_grad, kept, back),
        name="gather_grads",
    )
    received = swapped(theirs, "c")
    query_out, key_out, value_out = call(
        whole_width_kernel,
        tuple(shaped((1, TOK, HW), bf16) for _ in range(3)),
        (at, mine, received),
        name="whole_width",
    )
    update = call(order_kernel, shaped((NBLK, ROWS, BLK), bf16), (owners, slots), name="order")
    return query_out, key_out, value_out, new_statistics, update


def solution(mesh):
    split = Mesh(mesh.devices.reshape(2, 4, 2, 2, 2, 2), ("zl", "y", "c", "zh", "xh", "xl"))
    tokens = P(REP, SEQ, None)
    return jax.shard_map(
        local,
        mesh=split,
        in_specs=(
            tokens, tokens, tokens, tokens, P(REP, SEQ), P(), P(), P(REP, None, SEQ, None),
        ),
        out_specs=(tokens, tokens, tokens, P(REP, None, SEQ, None), P(None, SEQ, None)),
        check_vma=False,
    )
```

```python
import functools

import jax
import jax.numpy as jnp
from jax import lax
from jax.experimental import pallas as pl
from jax.experimental.pallas import tpu as pltpu
from jax.sharding import Mesh, PartitionSpec as P

D = 2048
HD = 128
HW = 1024
TOK = 128
BLK = 512
NBLK = 8
HALF = HW // 2
PAIR = 2 * TOK
QTR = 256
KVW = 2 * HALF + TOK

SEQ = ("zl", "y", "c")
REP = ("zh", "xh", "xl")
OUTER = ("zl", "y", "zh", "xh")
PLANE = ("zl", "y")
N_SEQ = 16
N_PLANE = 8
N_SIDE = NBLK // 2
N_OUTER = N_PLANE * N_SIDE
ROWS = BLK // N_SEQ

masked_score = -1e30
decay_rate = 0.9
step_scale = 16.0
head_scale = HD ** (-0.5)
weight_scale = 1.0 / 16384.0

f32 = jnp.float32
bf16 = jnp.bfloat16
MIB = 1024 * 1024
ANYWHERE = pl.BlockSpec(memory_space=pl.ANY)
SCALARS = pl.BlockSpec(memory_space=pltpu.SMEM)


def nt(left, right):
    return lax.dot_general(left, right, (((1,), (1,)), ((), ())), preferred_element_type=f32)


def tn(left, right):
    return lax.dot_general(left, right, (((0,), (0,)), ((), ())), preferred_element_type=f32)


def nn(left, right):
    return lax.dot_general(left, right, (((1,), (0,)), ((), ())), preferred_element_type=f32)


def whole(array):
    zeros = (0,) * len(array.shape)
    return pl.BlockSpec(tuple(array.shape), lambda i: zeros)


def call(body, outs, args, scratch=(), flops=0, nbytes=0, name=None, manual=False, limit=24, at_hbm=(), out_specs=None):
    place = (lambda array: ANYWHERE) if manual else whole
    specs = [
        SCALARS if a.dtype == jnp.int32 and a.ndim == 1 else ANYWHERE if n in at_hbm else place(a)
        for n, a in enumerate(args)
    ]
    return pl.pallas_call(
        body,
        grid=(1,),
        out_shape=outs,
        in_specs=specs,
        out_specs=out_specs or jax.tree.map(place, outs),
        scratch_shapes=list(scratch),
        compiler_params=pltpu.CompilerParams(vmem_limit_bytes=limit * MIB),
        cost_estimate=pl.CostEstimate(flops=flops, bytes_accessed=nbytes, transcendentals=0),
        name=name,
    )(*args)


def far(array):
    return pltpu.with_memory_space_constraint(array, pltpu.HBM)


def shaped(shape, dtype):
    return jax.ShapeDtypeStruct(shape, dtype)


def pick(core, ref, half):
    first = ref[:, half * HALF : half * HALF + QTR]
    second = ref[:, half * HALF + QTR : (half + 1) * HALF]
    return jnp.where(core == 0, first, second)


def pack_kernel(key_hbm, value_hbm, doc_hbm, own_ref, other_ref, doc_ref, sems, doc_sem):
    core = lax.axis_index("c")
    doc_copy = pltpu.make_async_copy(doc_hbm, doc_ref, doc_sem)
    doc_copy.start()
    copies = []
    for out_ref, which in ((own_ref, core), (other_ref, 1 - core)):
        for n, hbm in enumerate((key_hbm, value_hbm)):
            for half in range(2):
                start = pl.multiple_of(half * HALF + which * QTR, QTR)
                place = n * HALF + half * QTR
                copies.append(pltpu.make_async_copy(
                    hbm.at[:, pl.ds(start, QTR)],
                    out_ref.at[:, pl.ds(place, QTR)],
                    sems.at[len(copies)],
                ))
                copies[-1].start()
    doc_copy.wait()
    docs = jnp.broadcast_to(doc_ref[...].astype(f32), (TOK, TOK)).T.astype(bf16)
    own_ref[:, 2 * HALF :] = docs
    other_ref[:, 2 * HALF :] = docs
    for copy in copies:
        copy.wait()


def own_rows(core):
    return pl.ds(pl.multiple_of(core * TOK, TOK), TOK)


def grad_attended_kernel(
    at_ref, query_ref, query_other_ref, grad_ref, grad_other_ref, weight_hbm,
    attended_grad_ref, query_all_ref, grad_all_ref, weight_ref, sems,
):
    core = at_ref[0]
    copies = []
    for half in range(2):
        start = pl.multiple_of(half * HALF + core * QTR, QTR)
        copies.append(pltpu.make_async_copy(
            weight_hbm.at[pl.ds(start, QTR)], weight_ref.at[half], sems.at[half]
        ))
        copies[half].start()
    mine, other = own_rows(core), own_rows(1 - core)
    for half in range(2):
        cols = slice(half * QTR, (half + 1) * QTR)
        query_all_ref[mine, cols] = pick(core, query_ref, half)
        query_all_ref[other, cols] = pick(core, query_other_ref, half)
    grad_all_ref[mine, :] = grad_ref[...]
    grad_all_ref[other, :] = grad_other_ref[...]
    grad_rows = grad_all_ref[...]
    for half in range(2):
        copies[half].wait()
        product = nt(grad_rows, weight_ref[half])
        attended_grad_ref[:, half * QTR : (half + 1) * QTR] = product.astype(bf16)


def place_blocks(core, own_ref, other_ref, before_ref, crossed_ref, all_ref):
    for ref, place in (
        (before_ref, core), (crossed_ref, 1 - core), (own_ref, 2 + core), (other_ref, 3 - core)
    ):
        all_ref[pl.ds(pl.multiple_of(place * TOK, TOK), TOK), :] = ref[...]


def forward_kernel(
    part, at_ref, query_ref, own_ref, other_ref, before_ref, crossed_ref,
    attended_ref, weights_ref, all_ref,
):
    core, chip = at_ref[0], at_ref[1]
    unseen = 3 - 3 * part
    for ref, place in (
        (before_ref, core), (crossed_ref, 1 - core), (own_ref, 2 + core), (other_ref, 3 - core)
    ):

        @pl.when(place != unseen)
        def _():
            all_ref[pl.ds(pl.multiple_of(place * TOK, TOK), TOK), :] = ref[...]

    doc_cols = [
        all_ref[b * TOK : (b + 1) * TOK, 2 * HALF :].astype(f32) for b in range(part, part + 3)
    ]
    doc_row = jnp.concatenate([block.T for block in doc_cols], axis=1)
    query_at = lax.broadcasted_iota(jnp.int32, (TOK, 3 * TOK), 0)
    key_at = lax.broadcasted_iota(jnp.int32, (TOK, 3 * TOK), 1)
    window = (key_at <= query_at + PAIR) & (key_at > query_at)
    same = jnp.concatenate([doc_cols[2]] * 3, axis=1) == doc_row
    present = key_at + part * TOK >= jnp.where(chip > 0, 0, PAIR)
    visible = window & same & present
    rows = slice(part * TOK, (part + 1) * TOK)
    keys = slice(part * TOK, (part + 3) * TOK)
    for head in range(4):
        cols = slice(head * HD, (head + 1) * HD)
        value_cols = slice(HALF + head * HD, HALF + (head + 1) * HD)
        scores = nt(query_ref[rows, cols], all_ref[keys, cols]) * head_scale
        scores = jnp.where(visible, scores, masked_score)
        row_max = jnp.max(scores, axis=1, keepdims=True)
        grown = jnp.exp(scores - row_max)
        total = jnp.sum(grown, axis=1, keepdims=True)
        weights = (grown * (1.0 / total)).astype(bf16)
        weights_ref[head] = weights
        attended_ref[:, cols] = nn(weights, all_ref[keys, value_cols]).astype(bf16)


def weight_grad_kernel(
    at_ref, owner_ref, first_ref, second_ref, first_pair_ref, second_pair_ref, grad_ref, grad_pair_ref, grad_pair_c_ref,
    terms_hbm, turned_ref, pair_ref, terms_ref, sems,
):
    core, side = at_ref[0], at_ref[2]
    for half in range(2):
        cols = slice(half * QTR, (half + 1) * QTR)
        for n, ref in enumerate((first_ref, second_ref, first_pair_ref, second_pair_ref)):
            tokens = slice(n * TOK, (n + 1) * TOK)
            turned_ref[cols, tokens] = ref[:, cols].astype(f32).T.astype(bf16)
    pair_ref[:PAIR] = grad_ref[...]
    for ref, c in ((grad_pair_ref, core), (grad_pair_c_ref, 1 - core)):
        pair_ref[pl.ds(pl.multiple_of(PAIR + c * TOK, TOK), TOK), :] = ref[...]
    for block in range(NBLK):
        i, j = divmod(block, 4)
        slot = owner_ref[block]

        @pl.when(slot % 2 == side)
        def _():
            rows = turned_ref[i * QTR : (i + 1) * QTR, :]
            term = (nn(rows, pair_ref[:, j * BLK : (j + 1) * BLK]) * weight_scale).astype(bf16)
            place = slot // 2
            terms_ref[place] = term.reshape(N_PLANE, ROWS, BLK)
            pltpu.make_async_copy(
                terms_ref.at[place], terms_hbm.at[:, place], sems.at[place]
            ).start()

    for place in range(N_SIDE):
        pltpu.make_async_copy(terms_ref.at[place], terms_hbm.at[:, place], sems.at[place]).wait()


def backward_kernel(
    at_ref, first_ref, second_ref, query_ref, grad_ref,
    own_ref, other_ref, before_ref, crossed_ref, query_out_ref, sent_ref, kept_ref, all_ref, sum_ref,
):
    core = at_ref[0]
    place_blocks(core, own_ref, other_ref, before_ref, crossed_ref, all_ref)
    sum_ref[...] = jnp.zeros_like(sum_ref)
    for part in range(2):
        rows = slice(part * TOK, (part + 1) * TOK)
        keys = slice(part * TOK, (part + 3) * TOK)
        for head in range(4):
            cols = slice(head * HD, (head + 1) * HD)
            value_cols = slice(HALF + head * HD, HALF + (head + 1) * HD)
            low = (first_ref, second_ref)[part][head]
            weights = low.astype(f32)
            grad_head = grad_ref[rows, cols]
            query_head = query_ref[rows, cols]
            grad_weights = nt(grad_head, all_ref[keys, value_cols])
            grad_dot = jnp.sum(weights * grad_weights, axis=1, keepdims=True)
            grad_scores = (weights * (grad_weights - grad_dot)).astype(bf16)
            query_out_ref[rows, cols] = (nn(grad_scores, all_ref[keys, cols]) * head_scale).astype(bf16)
            sum_ref[keys, cols] += tn(grad_scores, query_head) * head_scale
            sum_ref[keys, value_cols] += tn(low, grad_head)
    sent_ref[...] = sum_ref[:PAIR].astype(bf16)
    kept_ref[...] = sum_ref[PAIR:]


def gather_grads_kernel(at_ref, query_ref, kept_ref, back_ref, mine_ref, other_ref):
    core = at_ref[0]
    for out_ref, rows in ((mine_ref, own_rows(core)), (other_ref, own_rows(1 - core))):
        out_ref[:, :HALF] = query_ref[rows, :]
        out_ref[:, HALF:] = (kept_ref[rows, :] + back_ref[rows, :].astype(f32)).astype(bf16)


def whole_width_kernel(at_ref, mine_ref, other_ref, query_ref, key_ref, value_ref):
    core = at_ref[0]
    for n, out_ref in enumerate((query_ref, key_ref, value_ref)):
        for half in range(2):
            cols = slice(n * HALF + half * QTR, n * HALF + (half + 1) * QTR)
            mine, other = mine_ref[:, cols], other_ref[:, cols]
            out_ref[0, :, half * HALF : half * HALF + QTR] = jnp.where(core == 0, mine, other)
            out_ref[0, :, half * HALF + QTR : (half + 1) * HALF] = jnp.where(core == 0, other, mine)


def sum_parts_kernel(parts_ref, stats_ref, total_ref):
    total = parts_ref[0].astype(f32)
    for n in range(1, N_OUTER):
        total = total + parts_ref[n].astype(f32)
    total_low = total.astype(bf16)
    for n in range(N_PLANE):
        total_ref[n, :ROWS] = total_low
        total_ref[n, ROWS : 2 * ROWS] = stats_ref[0]
        total_ref[n, 2 * ROWS :] = stats_ref[1]


def newton_kernel(
    at_ref, half_ref, half_c_ref, stat_rows_hbm,
    new_rows_ref, update_ref, slot_ref, stats_ref, left_ref, right_ref, stat_rows_ref, sem,
):
    core, row_first = at_ref[0], at_ref[3]
    arrival = pltpu.make_async_copy(stat_rows_hbm, stat_rows_ref, sem)
    arrival.start()
    for ref, c in ((half_ref, core), (half_c_ref, 1 - core)):
        for n in range(N_PLANE):
            rows = pl.ds(pl.multiple_of(c * QTR + n * ROWS, ROWS), ROWS)
            slot_ref[rows, :] = ref[n, :ROWS]
            rows = pl.ds(pl.multiple_of((2 * n + c) * ROWS, ROWS), ROWS)
            stats_ref[0, rows, :] = ref[n, ROWS : 2 * ROWS]
            stats_ref[1, rows, :] = ref[n, 2 * ROWS :]
    slot = slot_ref[...]
    own = pl.ds(pl.multiple_of(row_first, ROWS), ROWS)
    left_ref[...] = nt(slot, slot)
    right_ref[...] = tn(slot, slot)
    new_rows_ref[0, 0] = left_ref[own, :]
    new_rows_ref[0, 1] = right_ref[own, :]
    left = decay_rate * stats_ref[0].astype(f32) + left_ref[...]
    right = decay_rate * stats_ref[1].astype(f32) + right_ref[...]

    def scaled(stat):
        norm_square = jnp.sum(jnp.sum(stat * stat, axis=0, keepdims=True), axis=1, keepdims=True)
        matrix = stat * lax.rsqrt(norm_square)
        low_matrix = matrix.astype(bf16)
        step = (nn(low_matrix, low_matrix) - 10.0 * matrix).astype(bf16)
        return matrix, low_matrix, step, jnp.exp(-0.125 * jnp.log(norm_square))

    left_matrix, left_low, left_step, left_scale = scaled(left)
    right_matrix, right_low, right_step, right_scale = scaled(right)
    left_ref[...] = left_matrix
    identity_rows = jnp.where(
        lax.broadcasted_iota(jnp.int32, (ROWS, BLK), 0) + row_first
        == lax.broadcasted_iota(jnp.int32, (ROWS, BLK), 1),
        1.0,
        0.0,
    )

    def rooted(factor, low_matrix, step):
        square = (25.0 * factor + nn(factor.astype(bf16), step)) * 0.0625
        fourth = (25.0 * square + nn(square.astype(bf16), step)) * 0.0625
        return (5.0 * factor - nn(fourth.astype(bf16), low_matrix)) * 0.25

    left_factor = (5.0 * identity_rows - left_ref[own, :]) * 0.25
    left_rows = rooted(left_factor, left_low, left_step)
    moved = nn(left_rows.astype(bf16), slot)
    right_factor = (5.0 * moved - nn(moved.astype(bf16), right_low)) * 0.25
    update = rooted(right_factor, right_low, right_step) * (step_scale * left_scale * right_scale)
    update_low = update.astype(bf16)
    for n in range(NBLK):
        update_ref[n] = update_low
    arrival.wait()
    new_rows_ref[...] += decay_rate * stat_rows_ref[...]


def order_kernel(owner_ref, slots_ref, blocks_ref):
    for block in range(NBLK):
        blocks_ref[block] = slots_ref[owner_ref[block]]


def swapped(block, axis, mask=1):
    n = lax.axis_size(axis)
    return lax.ppermute(block, axis, [(i, i ^ mask) for i in range(n)])


def local(query_states, key_states, value_states, grad_out, doc_ids, out_weight, owners, statistics):
    core, side = lax.axis_index("c"), lax.axis_index("xl")
    chip = lax.axis_index(PLANE)
    at = jnp.stack([core, chip, side, (chip * 2 + core) * ROWS]).astype(jnp.int32)
    query, key, value, grad = query_states[0], key_states[0], value_states[0], grad_out[0]

    own, other = call(
        pack_kernel,
        (shaped((TOK, KVW), bf16), shaped((TOK, KVW), bf16)),
        (far(key), far(value), far(doc_ids)),
        scratch=(
            pltpu.VMEM((1, TOK), jnp.int32),
            pltpu.SemaphoreType.DMA((8,)),
            pltpu.SemaphoreType.DMA,
        ),
        at_hbm=(0, 1, 2),
        name="pack",
    )
    before = lax.ppermute(own, SEQ, [(i, i + 2) for i in range(N_SEQ - 2)])
    crossed = lax.ppermute(other, SEQ, [(i, (i ^ 1) + 2) for i in range(N_SEQ - 2)])
    query, grad, own, other = lax.optimization_barrier((query, grad, own, other))
    partner = swapped(other, "c")
    query_partner = swapped(query, "c")
    grad_partner = swapped(grad, "c")
    grad_pair = swapped(grad, "xl")
    attended_grad, query_all, grad_all = call(
        grad_attended_kernel,
        (shaped((PAIR, HALF), bf16), shaped((PAIR, HALF), bf16), shaped((PAIR, D), bf16)),
        (at, query, query_partner, grad, grad_partner, far(out_weight)),
        flops=2 * PAIR * HALF * D,
        nbytes=8 * MIB,
        scratch=(pltpu.VMEM((2, QTR, D), bf16), pltpu.SemaphoreType.DMA((2,))),
        name="grad_attended",
        at_hbm=(5,),
    )
    attended, attended_pair, weights = [], [], []
    for part in range(2):
        attended_part, weights_part = call(
            functools.partial(forward_kernel, part),
            (shaped((TOK, HALF), bf16), shaped((4, TOK, 3 * TOK), bf16)),
            (at, query_all, own, partner, before, crossed),
            scratch=(pltpu.VMEM((2 * PAIR, KVW), bf16),),
            flops=PAIR * HALF * 6 * TOK,
            nbytes=2 * MIB,
            name="forward",
        )
        attended.append(attended_part)
        attended_pair.append(swapped(attended_part, "xl"))
        weights.append(weights_part)
    grad_pair, _ = lax.optimization_barrier((grad_pair, attended[1]))
    grad_pair_c = swapped(grad_pair, "c")
    query_grad, sent, kept = call(
        backward_kernel,
        (shaped((PAIR, HALF), bf16), shaped((PAIR, HW), bf16), shaped((PAIR, HW), f32)),
        (at, *weights, query_all, attended_grad, own, partner, before, crossed),
        scratch=(pltpu.VMEM((2 * PAIR, KVW), bf16), pltpu.VMEM((2 * PAIR, HW), f32)),
        flops=2 * PAIR * HALF * 4 * 3 * TOK,
        nbytes=6 * MIB,
        name="backward",
    )
    stats_low, _ = lax.optimization_barrier((statistics[0], attended[1]))
    stats_low = stats_low.astype(bf16)
    *attended_pair, kept, sent, stats_low = lax.optimization_barrier(
        (*attended_pair, kept, sent, stats_low)
    )
    terms = call(
        weight_grad_kernel,
        shaped((N_PLANE, N_SIDE, ROWS, BLK), bf16),
        (at, owners, *attended, *attended_pair, grad_all, grad_pair, grad_pair_c),
        scratch=(
            pltpu.VMEM((HALF, 2 * PAIR), bf16),
            pltpu.VMEM((2 * PAIR, D), bf16),
            pltpu.VMEM((N_SIDE, N_PLANE, ROWS, BLK), bf16),
            pltpu.SemaphoreType.DMA((N_SIDE,)),
        ),
        flops=2 * PAIR * HALF * D,
        nbytes=4 * MIB,
        name="weight_grad",
        out_specs=ANYWHERE,
    )
    parts = lax.all_to_all(terms.reshape(N_OUTER, ROWS, BLK), OUTER, 0, 0, tiled=True)
    copies = call(
        sum_parts_kernel,
        shaped((N_PLANE, 3 * ROWS, BLK), bf16),
        (parts, stats_low),
        nbytes=2 * MIB,
        name="sum_outer",
    )
    half_slot = lax.all_to_all(copies, PLANE, 0, 0, tiled=True)
    half_slot_c = swapped(half_slot, "c")
    sent, _ = lax.optimization_barrier((sent, half_slot))
    back = lax.ppermute(sent, SEQ, [(i + 2, i) for i in range(N_SEQ - 2)])

    new_statistics, update_rows = call(
        newton_kernel,
        (shaped((1, 2, ROWS, BLK), f32), shaped((NBLK, ROWS, BLK), bf16)),
        (at, half_slot, half_slot_c, far(statistics)),
        scratch=(
            pltpu.VMEM((BLK, BLK), bf16),
            pltpu.VMEM((2, BLK, BLK), bf16),
            pltpu.VMEM((BLK, BLK), f32),
            pltpu.VMEM((BLK, BLK), f32),
            pltpu.VMEM((1, 2, ROWS, BLK), f32),
            pltpu.SemaphoreType.DMA,
        ),
        flops=2 * BLK**3 * 5,
        nbytes=4 * MIB,
        name="newton",
        at_hbm=(3,),
    )
    slots = lax.all_to_all(update_rows, REP, 0, 0, tiled=True)
    kept, _ = lax.optimization_barrier((kept, slots))
    mine, theirs = call(
        gather_grads_kernel,
        (shaped((TOK, 3 * HALF), bf16), shaped((TOK, 3 * HALF), bf16)),
        (at, query_grad, kept, back),
        name="gather_grads",
    )
    received = swapped(theirs, "c")
    query_out, key_out, value_out = call(
        whole_width_kernel,
        tuple(shaped((1, TOK, HW), bf16) for _ in range(3)),
        (at, mine, received),
        name="whole_width",
    )
    update = call(order_kernel, shaped((NBLK, ROWS, BLK), bf16), (owners, slots), name="order")
    return query_out, key_out, value_out, new_statistics, update


def solution(mesh):
    split = Mesh(mesh.devices.reshape(2, 4, 2, 2, 2, 2), ("zl", "y", "c", "zh", "xh", "xl"))
    tokens = P(REP, SEQ, None)
    return jax.shard_map(
        local,
        mesh=split,
        in_specs=(
            tokens, tokens, tokens, tokens, P(REP, SEQ), P(), P(), P(REP, None, SEQ, None),
        ),
        out_specs=(tokens, tokens, tokens, P(REP, None, SEQ, None), P(None, SEQ, None)),
        check_vma=False,
    )
```

```python
import functools

import jax
import jax.numpy as jnp
from jax import lax
from jax.experimental import pallas as pl
from jax.experimental.pallas import tpu as pltpu
from jax.sharding import Mesh, PartitionSpec as P

D = 2048
HD = 128
HW = 1024
TOK = 128
BLK = 512
NBLK = 8
HALF = HW // 2
PAIR = 2 * TOK
QTR = 256
KVW = 2 * HALF + TOK

SEQ = ("zl", "y", "c")
REP = ("zh", "xh", "xl")
OUTER = ("zl", "y", "zh", "xh")
PLANE = ("zl", "y")
N_SEQ = 16
N_PLANE = 8
N_SIDE = NBLK // 2
N_OUTER = N_PLANE * N_SIDE
ROWS = BLK // N_SEQ

masked_score = -1e30
decay_rate = 0.9
step_scale = 16.0
head_scale = HD ** (-0.5)
weight_scale = 1.0 / 16384.0

f32 = jnp.float32
bf16 = jnp.bfloat16
MIB = 1024 * 1024
ANYWHERE = pl.BlockSpec(memory_space=pl.ANY)
SCALARS = pl.BlockSpec(memory_space=pltpu.SMEM)


def nt(left, right):
    return lax.dot_general(left, right, (((1,), (1,)), ((), ())), preferred_element_type=f32)


def tn(left, right):
    return lax.dot_general(left, right, (((0,), (0,)), ((), ())), preferred_element_type=f32)


def nn(left, right):
    return lax.dot_general(left, right, (((1,), (0,)), ((), ())), preferred_element_type=f32)


def whole(array):
    zeros = (0,) * len(array.shape)
    return pl.BlockSpec(tuple(array.shape), lambda i: zeros)


def call(body, outs, args, scratch=(), flops=0, nbytes=0, name=None, manual=False, limit=24, at_hbm=(), out_specs=None):
    place = (lambda array: ANYWHERE) if manual else whole
    specs = [
        SCALARS if a.dtype == jnp.int32 and a.ndim == 1 else ANYWHERE if n in at_hbm else place(a)
        for n, a in enumerate(args)
    ]
    return pl.pallas_call(
        body,
        grid=(1,),
        out_shape=outs,
        in_specs=specs,
        out_specs=out_specs or jax.tree.map(place, outs),
        scratch_shapes=list(scratch),
        compiler_params=pltpu.CompilerParams(vmem_limit_bytes=limit * MIB),
        cost_estimate=pl.CostEstimate(flops=flops, bytes_accessed=nbytes, transcendentals=0),
        name=name,
    )(*args)


def far(array):
    return pltpu.with_memory_space_constraint(array, pltpu.HBM)


def shaped(shape, dtype):
    return jax.ShapeDtypeStruct(shape, dtype)


def pick(core, ref, half):
    first = ref[:, half * HALF : half * HALF + QTR]
    second = ref[:, half * HALF + QTR : (half + 1) * HALF]
    return jnp.where(core == 0, first, second)


def pack_kernel(key_hbm, value_hbm, doc_hbm, own_ref, other_ref, doc_ref, sems, doc_sem):
    core = lax.axis_index("c")
    doc_copy = pltpu.make_async_copy(doc_hbm, doc_ref, doc_sem)
    doc_copy.start()
    copies = []
    for out_ref, which in ((own_ref, core), (other_ref, 1 - core)):
        for n, hbm in enumerate((key_hbm, value_hbm)):
            for half in range(2):
                start = pl.multiple_of(half * HALF + which * QTR, QTR)
                place = n * HALF + half * QTR
                copies.append(pltpu.make_async_copy(
                    hbm.at[:, pl.ds(start, QTR)],
                    out_ref.at[:, pl.ds(place, QTR)],
                    sems.at[len(copies)],
                ))
                copies[-1].start()
    doc_copy.wait()
    docs = jnp.broadcast_to(doc_ref[...].astype(f32), (TOK, TOK)).T.astype(bf16)
    own_ref[:, 2 * HALF :] = docs
    other_ref[:, 2 * HALF :] = docs
    for copy in copies:
        copy.wait()


def own_rows(core):
    return pl.ds(pl.multiple_of(core * TOK, TOK), TOK)


def grad_attended_kernel(
    at_ref, query_ref, query_other_ref, grad_ref, grad_other_ref, weight_hbm,
    attended_grad_ref, query_all_ref, grad_all_ref, weight_ref, sems,
):
    core = at_ref[0]
    copies = []
    for half in range(2):
        start = pl.multiple_of(half * HALF + core * QTR, QTR)
        copies.append(pltpu.make_async_copy(
            weight_hbm.at[pl.ds(start, QTR)], weight_ref.at[half], sems.at[half]
        ))
        copies[half].start()
    mine, other = own_rows(core), own_rows(1 - core)
    for half in range(2):
        cols = slice(half * QTR, (half + 1) * QTR)
        query_all_ref[mine, cols] = pick(core, query_ref, half)
        query_all_ref[other, cols] = pick(core, query_other_ref, half)
    grad_all_ref[mine, :] = grad_ref[...]
    grad_all_ref[other, :] = grad_other_ref[...]
    grad_rows = grad_all_ref[...]
    for half in range(2):
        copies[half].wait()
        product = nt(grad_rows, weight_ref[half])
        attended_grad_ref[:, half * QTR : (half + 1) * QTR] = product.astype(bf16)


def place_blocks(core, own_ref, other_ref, before_ref, crossed_ref, all_ref):
    for ref, place in (
        (before_ref, core), (crossed_ref, 1 - core), (own_ref, 2 + core), (other_ref, 3 - core)
    ):
        all_ref[pl.ds(pl.multiple_of(place * TOK, TOK), TOK), :] = ref[...]


def forward_kernel(
    part, at_ref, query_ref, own_ref, other_ref, before_ref, crossed_ref,
    attended_ref, weights_ref, all_ref,
):
    core, chip = at_ref[0], at_ref[1]
    unseen = 3 - 3 * part
    for ref, place in (
        (before_ref, core), (crossed_ref, 1 - core), (own_ref, 2 + core), (other_ref, 3 - core)
    ):

        @pl.when(place != unseen)
        def _():
            all_ref[pl.ds(pl.multiple_of(place * TOK, TOK), TOK), :] = ref[...]

    doc_cols = [
        all_ref[b * TOK : (b + 1) * TOK, 2 * HALF :].astype(f32) for b in range(part, part + 3)
    ]
    doc_row = jnp.concatenate([block.T for block in doc_cols], axis=1)
    query_at = lax.broadcasted_iota(jnp.int32, (TOK, 3 * TOK), 0)
    key_at = lax.broadcasted_iota(jnp.int32, (TOK, 3 * TOK), 1)
    window = (key_at <= query_at + PAIR) & (key_at > query_at)
    same = jnp.concatenate([doc_cols[2]] * 3, axis=1) == doc_row
    present = key_at + part * TOK >= jnp.where(chip > 0, 0, PAIR)
    visible = window & same & present
    rows = slice(part * TOK, (part + 1) * TOK)
    keys = slice(part * TOK, (part + 3) * TOK)
    for head in range(4):
        cols = slice(head * HD, (head + 1) * HD)
        value_cols = slice(HALF + head * HD, HALF + (head + 1) * HD)
        scores = nt(query_ref[rows, cols], all_ref[keys, cols]) * head_scale
        scores = jnp.where(visible, scores, masked_score)
        row_max = jnp.max(scores, axis=1, keepdims=True)
        grown = jnp.exp(scores - row_max)
        total = jnp.sum(grown, axis=1, keepdims=True)
        weights = (grown * (1.0 / total)).astype(bf16)
        weights_ref[head] = weights
        attended_ref[:, cols] = nn(weights, all_ref[keys, value_cols]).astype(bf16)


def weight_grad_kernel(
    at_ref, owner_ref, first_ref, second_ref, first_pair_ref, second_pair_ref, grad_ref, grad_pair_ref, grad_pair_c_ref,
    terms_hbm, turned_ref, pair_ref, terms_ref, sems,
):
    core, side = at_ref[0], at_ref[2]
    for half in range(2):
        cols = slice(half * QTR, (half + 1) * QTR)
        for n, ref in enumerate((first_ref, second_ref, first_pair_ref, second_pair_ref)):
            tokens = slice(n * TOK, (n + 1) * TOK)
            turned_ref[cols, tokens] = ref[:, cols].T
    pair_ref[:PAIR] = grad_ref[...]
    for ref, c in ((grad_pair_ref, core), (grad_pair_c_ref, 1 - core)):
        pair_ref[pl.ds(pl.multiple_of(PAIR + c * TOK, TOK), TOK), :] = ref[...]
    for block in range(NBLK):
        i, j = divmod(block, 4)
        slot = owner_ref[block]

        @pl.when(slot % 2 == side)
        def _():
            rows = turned_ref[i * QTR : (i + 1) * QTR, :]
            term = (nn(rows, pair_ref[:, j * BLK : (j + 1) * BLK]) * weight_scale).astype(bf16)
            place = slot // 2
            terms_ref[place] = term.reshape(N_PLANE, ROWS, BLK)
            pltpu.make_async_copy(
                terms_ref.at[place], terms_hbm.at[:, place], sems.at[place]
            ).start()

    for place in range(N_SIDE):
        pltpu.make_async_copy(terms_ref.at[place], terms_hbm.at[:, place], sems.at[place]).wait()


def backward_kernel(
    at_ref, first_ref, second_ref, query_ref, grad_ref,
    own_ref, other_ref, before_ref, crossed_ref, query_out_ref, sent_ref, kept_ref, all_ref, sum_ref,
):
    core = at_ref[0]
    place_blocks(core, own_ref, other_ref, before_ref, crossed_ref, all_ref)
    sum_ref[...] = jnp.zeros_like(sum_ref)
    for part in range(2):
        rows = slice(part * TOK, (part + 1) * TOK)
        keys = slice(part * TOK, (part + 3) * TOK)
        for head in range(4):
            cols = slice(head * HD, (head + 1) * HD)
            value_cols = slice(HALF + head * HD, HALF + (head + 1) * HD)
            low = (first_ref, second_ref)[part][head]
            weights = low.astype(f32)
            grad_head = grad_ref[rows, cols]
            query_head = query_ref[rows, cols]
            grad_weights = nt(grad_head, all_ref[keys, value_cols])
            grad_dot = jnp.sum(weights * grad_weights, axis=1, keepdims=True)
            grad_scores = (weights * (grad_weights - grad_dot)).astype(bf16)
            query_out_ref[rows, cols] = (nn(grad_scores, all_ref[keys, cols]) * head_scale).astype(bf16)
            sum_ref[keys, cols] += tn(grad_scores, query_head) * head_scale
            sum_ref[keys, value_cols] += tn(low, grad_head)
    sent_ref[...] = sum_ref[:PAIR].astype(bf16)
    kept_ref[...] = sum_ref[PAIR:]


def gather_grads_kernel(at_ref, query_ref, kept_ref, back_ref, mine_ref, other_ref):
    core = at_ref[0]
    for out_ref, rows in ((mine_ref, own_rows(core)), (other_ref, own_rows(1 - core))):
        out_ref[:, :HALF] = query_ref[rows, :]
        out_ref[:, HALF:] = (kept_ref[rows, :] + back_ref[rows, :].astype(f32)).astype(bf16)


def whole_width_kernel(at_ref, mine_ref, other_ref, query_ref, key_ref, value_ref):
    core = at_ref[0]
    for n, out_ref in enumerate((query_ref, key_ref, value_ref)):
        for half in range(2):
            cols = slice(n * HALF + half * QTR, n * HALF + (half + 1) * QTR)
            mine, other = mine_ref[:, cols], other_ref[:, cols]
            out_ref[0, :, half * HALF : half * HALF + QTR] = jnp.where(core == 0, mine, other)
            out_ref[0, :, half * HALF + QTR : (half + 1) * HALF] = jnp.where(core == 0, other, mine)


def sum_parts_kernel(parts_ref, stats_ref, total_ref):
    total = parts_ref[0].astype(f32)
    for n in range(1, N_OUTER):
        total = total + parts_ref[n].astype(f32)
    total_low = total.astype(bf16)
    for n in range(N_PLANE):
        total_ref[n, :ROWS] = total_low
        total_ref[n, ROWS : 2 * ROWS] = stats_ref[0]
        total_ref[n, 2 * ROWS :] = stats_ref[1]


def newton_kernel(
    at_ref, half_ref, half_c_ref, stat_rows_hbm,
    new_rows_ref, update_ref, slot_ref, stats_ref, left_ref, right_ref, stat_rows_ref, sem,
):
    core, row_first = at_ref[0], at_ref[3]
    arrival = pltpu.make_async_copy(stat_rows_hbm, stat_rows_ref, sem)
    arrival.start()
    for ref, c in ((half_ref, core), (half_c_ref, 1 - core)):
        for n in range(N_PLANE):
            rows = pl.ds(pl.multiple_of(c * QTR + n * ROWS, ROWS), ROWS)
            slot_ref[rows, :] = ref[n, :ROWS]
            rows = pl.ds(pl.multiple_of((2 * n + c) * ROWS, ROWS), ROWS)
            stats_ref[0, rows, :] = ref[n, ROWS : 2 * ROWS]
            stats_ref[1, rows, :] = ref[n, 2 * ROWS :]
    slot = slot_ref[...]
    own = pl.ds(pl.multiple_of(row_first, ROWS), ROWS)
    left_ref[...] = nt(slot, slot)
    right_ref[...] = tn(slot, slot)
    new_rows_ref[0, 0] = left_ref[own, :]
    new_rows_ref[0, 1] = right_ref[own, :]
    left = decay_rate * stats_ref[0].astype(f32) + left_ref[...]
    right = decay_rate * stats_ref[1].astype(f32) + right_ref[...]

    def scaled(stat):
        norm_square = jnp.sum(jnp.sum(stat * stat, axis=0, keepdims=True), axis=1, keepdims=True)
        matrix = stat * lax.rsqrt(norm_square)
        low_matrix = matrix.astype(bf16)
        step = (nn(low_matrix, low_matrix) - 10.0 * matrix).astype(bf16)
        return matrix, low_matrix, step, jnp.exp(-0.125 * jnp.log(norm_square))

    left_matrix, left_low, left_step, left_scale = scaled(left)
    right_matrix, right_low, right_step, right_scale = scaled(right)
    left_ref[...] = left_matrix
    identity_rows = jnp.where(
        lax.broadcasted_iota(jnp.int32, (ROWS, BLK), 0) + row_first
        == lax.broadcasted_iota(jnp.int32, (ROWS, BLK), 1),
        1.0,
        0.0,
    )

    def rooted(factor, low_matrix, step):
        square = (25.0 * factor + nn(factor.astype(bf16), step)) * 0.0625
        fourth = (25.0 * square + nn(square.astype(bf16), step)) * 0.0625
        return (5.0 * factor - nn(fourth.astype(bf16), low_matrix)) * 0.25

    left_factor = (5.0 * identity_rows - left_ref[own, :]) * 0.25
    left_rows = rooted(left_factor, left_low, left_step)
    moved = nn(left_rows.astype(bf16), slot)
    right_factor = (5.0 * moved - nn(moved.astype(bf16), right_low)) * 0.25
    update = rooted(right_factor, right_low, right_step) * (step_scale * left_scale * right_scale)
    update_low = update.astype(bf16)
    for n in range(NBLK):
        update_ref[n] = update_low
    arrival.wait()
    new_rows_ref[...] += decay_rate * stat_rows_ref[...]


def order_kernel(owner_ref, slots_ref, blocks_ref):
    for block in range(NBLK):
        blocks_ref[block] = slots_ref[owner_ref[block]]


def swapped(block, axis, mask=1):
    n = lax.axis_size(axis)
    return lax.ppermute(block, axis, [(i, i ^ mask) for i in range(n)])


def local(query_states, key_states, value_states, grad_out, doc_ids, out_weight, owners, statistics):
    core, side = lax.axis_index("c"), lax.axis_index("xl")
    chip = lax.axis_index(PLANE)
    at = jnp.stack([core, chip, side, (chip * 2 + core) * ROWS]).astype(jnp.int32)
    query, key, value, grad = query_states[0], key_states[0], value_states[0], grad_out[0]

    own, other = call(
        pack_kernel,
        (shaped((TOK, KVW), bf16), shaped((TOK, KVW), bf16)),
        (far(key), far(value), far(doc_ids)),
        scratch=(
            pltpu.VMEM((1, TOK), jnp.int32),
            pltpu.SemaphoreType.DMA((8,)),
            pltpu.SemaphoreType.DMA,
        ),
        at_hbm=(0, 1, 2),
        name="pack",
    )
    before = lax.ppermute(own, SEQ, [(i, i + 2) for i in range(N_SEQ - 2)])
    crossed = lax.ppermute(other, SEQ, [(i, (i ^ 1) + 2) for i in range(N_SEQ - 2)])
    query, grad, own, other = lax.optimization_barrier((query, grad, own, other))
    partner = swapped(other, "c")
    query_partner = swapped(query, "c")
    grad_partner = swapped(grad, "c")
    grad_pair = swapped(grad, "xl")
    attended_grad, query_all, grad_all = call(
        grad_attended_kernel,
        (shaped((PAIR, HALF), bf16), shaped((PAIR, HALF), bf16), shaped((PAIR, D), bf16)),
        (at, query, query_partner, grad, grad_partner, far(out_weight)),
        flops=2 * PAIR * HALF * D,
        nbytes=8 * MIB,
        scratch=(pltpu.VMEM((2, QTR, D), bf16), pltpu.SemaphoreType.DMA((2,))),
        name="grad_attended",
        at_hbm=(5,),
    )
    attended, attended_pair, weights = [], [], []
    for part in range(2):
        attended_part, weights_part = call(
            functools.partial(forward_kernel, part),
            (shaped((TOK, HALF), bf16), shaped((4, TOK, 3 * TOK), bf16)),
            (at, query_all, own, partner, before, crossed),
            scratch=(pltpu.VMEM((2 * PAIR, KVW), bf16),),
            flops=PAIR * HALF * 6 * TOK,
            nbytes=2 * MIB,
            name="forward",
        )
        attended.append(attended_part)
        attended_pair.append(swapped(attended_part, "xl"))
        weights.append(weights_part)
    grad_pair, _ = lax.optimization_barrier((grad_pair, attended[1]))
    grad_pair_c = swapped(grad_pair, "c")
    query_grad, sent, kept = call(
        backward_kernel,
        (shaped((PAIR, HALF), bf16), shaped((PAIR, HW), bf16), shaped((PAIR, HW), f32)),
        (at, *weights, query_all, attended_grad, own, partner, before, crossed),
        scratch=(pltpu.VMEM((2 * PAIR, KVW), bf16), pltpu.VMEM((2 * PAIR, HW), f32)),
        flops=2 * PAIR * HALF * 4 * 3 * TOK,
        nbytes=6 * MIB,
        name="backward",
    )
    stats_low, _ = lax.optimization_barrier((statistics[0], attended[1]))
    stats_low = stats_low.astype(bf16)
    *attended_pair, kept, sent, stats_low = lax.optimization_barrier(
        (*attended_pair, kept, sent, stats_low)
    )
    terms = call(
        weight_grad_kernel,
        shaped((N_PLANE, N_SIDE, ROWS, BLK), bf16),
        (at, owners, *attended, *attended_pair, grad_all, grad_pair, grad_pair_c),
        scratch=(
            pltpu.VMEM((HALF, 2 * PAIR), bf16),
            pltpu.VMEM((2 * PAIR, D), bf16),
            pltpu.VMEM((N_SIDE, N_PLANE, ROWS, BLK), bf16),
            pltpu.SemaphoreType.DMA((N_SIDE,)),
        ),
        flops=2 * PAIR * HALF * D,
        nbytes=4 * MIB,
        name="weight_grad",
        out_specs=ANYWHERE,
    )
    parts = lax.all_to_all(terms.reshape(N_OUTER, ROWS, BLK), OUTER, 0, 0, tiled=True)
    copies = call(
        sum_parts_kernel,
        shaped((N_PLANE, 3 * ROWS, BLK), bf16),
        (parts, stats_low),
        nbytes=2 * MIB,
        name="sum_outer",
    )
    half_slot = lax.all_to_all(copies, PLANE, 0, 0, tiled=True)
    half_slot_c = swapped(half_slot, "c")
    sent, _ = lax.optimization_barrier((sent, half_slot))
    back = lax.ppermute(sent, SEQ, [(i + 2, i) for i in range(N_SEQ - 2)])

    new_statistics, update_rows = call(
        newton_kernel,
        (shaped((1, 2, ROWS, BLK), f32), shaped((NBLK, ROWS, BLK), bf16)),
        (at, half_slot, half_slot_c, far(statistics)),
        scratch=(
            pltpu.VMEM((BLK, BLK), bf16),
            pltpu.VMEM((2, BLK, BLK), bf16),
            pltpu.VMEM((BLK, BLK), f32),
            pltpu.VMEM((BLK, BLK), f32),
            pltpu.VMEM((1, 2, ROWS, BLK), f32),
            pltpu.SemaphoreType.DMA,
        ),
        flops=2 * BLK**3 * 5,
        nbytes=4 * MIB,
        name="newton",
        at_hbm=(3,),
    )
    slots = lax.all_to_all(update_rows, REP, 0, 0, tiled=True)
    kept, _ = lax.optimization_barrier((kept, slots))
    mine, theirs = call(
        gather_grads_kernel,
        (shaped((TOK, 3 * HALF), bf16), shaped((TOK, 3 * HALF), bf16)),
        (at, query_grad, kept, back),
        name="gather_grads",
    )
    received = swapped(theirs, "c")
    query_out, key_out, value_out = call(
        whole_width_kernel,
        tuple(shaped((1, TOK, HW), bf16) for _ in range(3)),
        (at, mine, received),
        name="whole_width",
    )
    update = call(order_kernel, shaped((NBLK, ROWS, BLK), bf16), (owners, slots), name="order")
    return query_out, key_out, value_out, new_statistics, update


def solution(mesh):
    split = Mesh(mesh.devices.reshape(2, 4, 2, 2, 2, 2), ("zl", "y", "c", "zh", "xh", "xl"))
    tokens = P(REP, SEQ, None)
    return jax.shard_map(
        local,
        mesh=split,
        in_specs=(
            tokens, tokens, tokens, tokens, P(REP, SEQ), P(), P(), P(REP, None, SEQ, None),
        ),
        out_specs=(tokens, tokens, tokens, P(REP, None, SEQ, None), P(None, SEQ, None)),
        check_vma=False,
    )
```
